128 devices in a mesh: dp: 64 (over z, x, y), seq: 2 (over core).
Axes of the slice: x: 4, y: 4, z: 4, core: 2. Of those that a mesh axis runs over, the one named last changes fastest.
Arguments:
- hidden_in: bfloat16 [64, 512, 768], P('dp', 'seq'), may hold values from -6 to 6
- segments: int32 [64, 512], P('dp'), may hold values from 0 to 2, as said below
- projection_in: bfloat16 [2, 768, 3352], P(None, ('dp', 'seq')), may hold values from -0.21875 to 0.21875
- projection_out: bfloat16 [2, 1536, 768], P(None, ('dp', 'seq')), may hold values from -0.15625 to 0.15625
- kernel_weight: bfloat16 [2, 4, 1792], P(None, None, ('dp', 'seq')), may hold values from -3 to 3
- kernel_bias: bfloat16 [2, 1792], P(None, ('dp', 'seq')), may hold values from -3 to 3
- norm_gain: bfloat16 [2, 768], P(None, ('dp', 'seq')), may hold values from 0.099609375 to 1.8984375
- gate_gain: bfloat16 [2, 1536], P(None, ('dp', 'seq')), may hold values from 0.099609375 to 1.8984375
- head_values: float32 [2, 3, 24], replicated, may hold values from -9.3 to 1.5, as said below
- cotangent: bfloat16 [64, 512, 768], P('dp', 'seq'), may hold values from -6 to 6
Outputs:
- hidden_out: bfloat16 [64, 512, 768], P('dp', 'seq')
- input_gradient: bfloat16 [64, 512, 768], P('dp', 'seq')
- projection_in_gradient: float32 [2, 768, 3352], P(None, ('dp', 'seq'))
- projection_out_gradient: float32 [2, 1536, 768], P(None, ('dp', 'seq'))
- kernel_weight_gradient: float32 [2, 4, 1792], P(None, None, ('dp', 'seq'))
- kernel_bias_gradient: float32 [2, 1792], P(None, ('dp', 'seq'))
- norm_gain_gradient: float32 [2, 768], P(None, ('dp', 'seq'))
- gate_gain_gradient: float32 [2, 1536], P(None, ('dp', 'seq'))
- head_values_gradient: float32 [2, 3, 24], replicated
The draws below stay inside these ranges and needn't reach their ends.
Inputs may be any that keep to these rules, and one draw needn't show every extreme that they name: Segment numbers never fall along a row and each row holds segments 0, 1 and 2; segment 1 reaches from the row's first block of 256 positions into its last. `head_values`: row 0 of a layer holds inverse softplus values of positive steps, row 1 logarithms of decay rates, row 2 skip gains.
All inputs are finite; a program needn't handle non-finite values.
Results may differ from the reference program's by a relative error of at most 0.012.
Values may be sent and summed in bfloat16 or wider, within the bound.
No kernel may reach another device: no remote copies, remote signals or barrier semaphores. Data moves between devices by JAX's collectives and lax.ppermute only.
A program may use at most 256 MiB of HBM per device.

```python
import math
import jax
import jax.numpy as jnp
from jax import lax

D = 768
HEADS = 24
HEAD_DIM = 64
STATE = 128
KERNEL = 4
BLOCK = 256
LAYERS = 2
INNER = 1536
CONV_CH = 1792
PROJ = 3352
ROWS = 64
ROW_LEN = 512


def draw_segments(key, part):
    starts = jax.random.randint(jax.random.fold_in(key, 101), (ROWS, 1), 8, BLOCK - 8)
    finish = jax.random.randint(jax.random.fold_in(key, 102), (ROWS, 1), ROW_LEN - BLOCK + 8, ROW_LEN - 8)
    position = jnp.arange(ROW_LEN)[None, :]
    return (position >= starts).astype(jnp.int32) + (position >= finish).astype(jnp.int32)


def draw_head_values(key, part):
    shape_one = (LAYERS, 1, HEADS)
    log_step = jax.random.uniform(jax.random.fold_in(key, 201), shape_one, jnp.float32, math.log(0.0003), math.log(0.05))
    step_size = jnp.exp(log_step)
    step_offset = step_size + jnp.log(-jnp.expm1(-step_size))
    rate_log = jax.random.uniform(jax.random.fold_in(key, 202), shape_one, jnp.float32, 0.0, math.log(4.0))
    skip_gain = jax.random.uniform(jax.random.fold_in(key, 203), shape_one, jnp.float32, 0.5, 1.5)
    return jnp.concatenate([step_offset, rate_log, skip_gain], axis=1)


def steps_of(stream_key, extent, cuts, low, top_value):
    def one(dim, shards_of):
        heights = jax.random.uniform(jax.random.fold_in(jax.random.fold_in(stream_key, 6), dim), (shards_of,), jnp.float32, low / len(cuts), top_value / len(cuts))
        return jnp.repeat(jnp.exp(heights), extent[dim] // shards_of).reshape((-1,) + (1,) * (len(extent) - dim - 1))

    factor_of = one(*cuts[0])
    for cut in cuts[1:]:
        factor_of = factor_of * one(*cut)
    return factor_of


def normal_values(own_key, extent, scale, limit, shards=(), kind=jnp.bfloat16):
    array = jax.random.normal(own_key, extent, jnp.float32) * scale
    if len(shards) > 0:
        array = steps_of(own_key, extent, shards, -0.22, 0.18) * array
    return jnp.clip(array, min=-limit, max=limit).astype(kind)


def setup_inputs(seed: int = 0) -> dict:
    splits = jax.random.split(jax.random.key(seed), 11)
    hidden_in = normal_values(splits[0], (ROWS, ROW_LEN, D), 1.0, 6.0, ((0, 64), (1, 2)))
    segments = draw_segments(jax.random.fold_in(splits[10], 71), 0)
    projection_in = normal_values(splits[2], (LAYERS, D, PROJ), D ** -0.5, 0.21875, ((1, 128),))
    projection_out = normal_values(splits[3], (LAYERS, INNER, D), INNER ** -0.5, 0.15625, ((1, 128),))
    kernel_weight = normal_values(splits[4], (LAYERS, KERNEL, CONV_CH), KERNEL ** -0.5, 3.0, ((2, 128),))
    kernel_bias = normal_values(splits[5], (LAYERS, CONV_CH), 0.5, 3.0, ((1, 128),))
    norm_gain = jnp.clip(1.0 + 0.18 * jax.random.normal(splits[6], (LAYERS, D), jnp.float32), 0.099609375, 1.8984375).astype(jnp.bfloat16)
    gate_gain = jnp.clip(1.0 + 0.18 * jax.random.normal(splits[7], (LAYERS, INNER), jnp.float32), 0.099609375, 1.8984375).astype(jnp.bfloat16)
    head_values = draw_head_values(jax.random.fold_in(splits[10], 71), 0)
    cotangent = normal_values(splits[9], (ROWS, ROW_LEN, D), 1.0, 6.0, ((0, 64), (1, 2)))
    return dict(hidden_in=hidden_in, segments=segments, projection_in=projection_in, projection_out=projection_out, kernel_weight=kernel_weight, kernel_bias=kernel_bias, norm_gain=norm_gain, gate_gain=gate_gain, head_values=head_values, cotangent=cotangent)


@jax.custom_vjp
def low(v):
    return lax.optimization_barrier(v.astype(jnp.bfloat16)).astype(jnp.float32)

@jax.custom_vjp
def low_back(v):
    return v

def low_keep(v):
    return (low(v), None)

def low_pass(kept, grad):
    return (grad,)

def back_keep(v):
    return (v, None)

def back_low(kept, grad):
    return (low(grad),)
low.defvjp(low_keep, low_pass)
low_back.defvjp(back_keep, back_low)
norm_eps = 1e-05
highest = lax.Precision.HIGHEST

def rms_scale(values, gain):
    return values * lax.rsqrt(lax.optimization_barrier(jnp.mean(values * values, axis=-1, keepdims=True)) + norm_eps) * gain

def row_mixing(pieces):
    scaled, writers, readers, cumul_rate, segment_row = pieces
    length = segment_row.shape[0]
    position = jnp.arange(length)
    allowed = (position[:, None] >= position[None, :]) & (segment_row[:, None] == segment_row[None, :])
    cumul_heads = cumul_rate.T
    spread = cumul_heads[:, :, None] - cumul_heads[:, None, :]
    decay_matrix = jnp.where(allowed[None], jnp.exp(jnp.where(allowed[None], spread, 0.0)), 0.0)
    affinity = jnp.dot(readers, writers.T, precision=highest, preferred_element_type=jnp.float32)
    return jnp.einsum('hts,shp->thp', decay_matrix * affinity[None], scaled, precision=highest)

def mixer_layer(values, segment_rows, weight_set):
    weight_in, weight_out, kernel_weights, kernel_offset, norm_scale, gate_scale, head_layer = weight_set
    group_rows, length = (values.shape[0], values.shape[1])
    normed = low(rms_scale(values, norm_scale))
    projected = low_back(jnp.einsum('gtd,dp->gtp', normed, weight_in, precision=highest))
    gate_in = projected[..., :INNER]
    signal = projected[..., INNER:INNER + CONV_CH]
    extended = jnp.pad(signal, ((0, 0), (KERNEL - 1, 0), (0, 0)))
    segment_pad = jnp.pad(segment_rows, ((0, 0), (KERNEL - 1, 0)), constant_values=-1)
    summed = jnp.zeros_like(signal)
    for offset in range(KERNEL):
        same_segment = (segment_pad[:, offset:offset + length] == segment_rows).astype(signal.dtype)
        summed = summed + kernel_weights[offset] * extended[:, offset:offset + length] * same_segment[..., None]
    active = jax.nn.silu(summed + kernel_offset)
    inputs = active[..., :INNER].reshape(group_rows, length, HEADS, HEAD_DIM)
    writers = active[..., INNER:INNER + STATE]
    readers = active[..., INNER + STATE:]
    step_size = jax.nn.softplus(projected[..., INNER + CONV_CH:] + head_layer[0])
    cumul_rate = jnp.cumsum(-step_size * jnp.exp(head_layer[1]), axis=1)
    scaled = inputs * step_size[..., None]
    mixed_out = lax.map(jax.checkpoint(row_mixing), (scaled, writers, readers, cumul_rate, segment_rows))
    total_out = mixed_out + head_layer[2][:, None] * inputs
    gated_out = total_out.reshape(group_rows, length, INNER) * jax.nn.silu(gate_in)
    outgoing = low(rms_scale(gated_out, gate_scale))
    branch = low_back(jnp.einsum('gte,ed->gtd', outgoing, weight_out, precision=highest))
    return values + branch

def forward(values, segment_rows, weight_set):
    for layer_index in range(LAYERS):
        values = mixer_layer(values, segment_rows, tuple((member[layer_index] for member in weight_set)))
    return values

def reference(hidden_in, segments, projection_in, projection_out, kernel_weight, kernel_bias, norm_gain, gate_gain, head_values, cotangent):
    weights = tuple((member.astype(jnp.float32) for member in (projection_in, projection_out, kernel_weight, kernel_bias, norm_gain, gate_gain, head_values)))
    group_rows = 8 if ROWS % 8 == 0 else 1
    blocks = ROWS // group_rows
    values_all = hidden_in.astype(jnp.float32).reshape(blocks, group_rows, ROW_LEN, D)
    segment_all = segments.reshape(blocks, group_rows, ROW_LEN)
    upstream_all = cotangent.astype(jnp.float32).reshape(blocks, group_rows, ROW_LEN, D)

    def visit_block(totals, pieces):
        values, segment_rows, upstream = pieces
        result, pullback = jax.vjp(lambda probe_values, probe_weights: forward(probe_values, segment_rows, probe_weights), values, weights)
        input_back, weight_back = pullback(upstream)
        totals = jax.tree.map(jnp.add, totals, weight_back)
        return (totals, (result.astype(jnp.bfloat16), input_back.astype(jnp.bfloat16)))
    zero_grads = jax.tree.map(jnp.zeros_like, weights)
    totals, (out_blocks, back_blocks) = lax.scan(visit_block, zero_grads, (values_all, segment_all, upstream_all))
    return (out_blocks.reshape(ROWS, ROW_LEN, D), back_blocks.reshape(ROWS, ROW_LEN, D), totals[0], totals[1], totals[2], totals[3], totals[4], totals[5], totals[6])
```

```python
import jax
import jax.numpy as jnp
from jax import lax
from jax.experimental import pallas as pl
from jax.experimental.pallas import tpu as pltpu
from jax.sharding import Mesh
from jax.sharding import PartitionSpec as P

HEADS = 24
HEAD_DIM = 64
STATE = 128
INNER = 1536
CONV_CH = 1792
WIDTH = 768
TOKENS = 512
HALF = 256
OWN_HEADS = 12
OWN = OWN_HEADS * HEAD_DIM
OWN_CONV = OWN + 2 * STATE
OWN_COLS = OWN + OWN_CONV + 128
NORM_EPS = 1e-05
NEGATIVE = -1e30
F32 = jnp.float32
BF16 = jnp.bfloat16
HIGHEST = lax.Precision.HIGHEST


def dot(a, b, dims=((1,), (0,)), precision=None):
    return lax.dot_general(a, b, (dims, ((), ())), precision=precision, preferred_element_type=F32)


def dot_nt(a, b, precision=None):
    return dot(a, b, ((1,), (1,)), precision)


def dot_tn(a, b, precision=None):
    return dot(a, b, ((0,), (0,)), precision)


def iota(shape, dim):
    return lax.broadcasted_iota(jnp.int32, shape, dim)


def padded_order():
    column = iota((WIDTH, 1024), 1)
    core = column >> 9
    chip = (column & 511) >> 3
    place = column & 7
    feature = jnp.where(place < 6, 12 * chip + 6 * core + place, -1)
    return jnp.where(feature == iota((WIDTH, 1024), 0), 1.0, 0.0).astype(BF16)


def head_spread():
    return jnp.where(iota((128, OWN), 0) == (iota((128, OWN), 1) >> 6), 1.0, 0.0).astype(F32)


def softplus(v):
    return jnp.maximum(v, 0.0) + jnp.log1p(jnp.exp(-jnp.abs(v)))


def tap_masks(segment_column):
    position = iota((TOKENS, 1), 0)
    wide = jnp.broadcast_to(segment_column, (TOKENS, 128))
    masks = [None]
    for back in range(1, 4):
        before = pltpu.roll(wide, back, 0)[:, :1]
        same = (before == segment_column) & (position >= back)
        masks.append(jnp.where(same, 1.0, 0.0).astype(F32))
    return masks


def convolved(signal, taps, masks):
    total = taps[3:4] * signal
    for back in range(1, 4):
        total = total + taps[3 - back : 4 - back] * (pltpu.roll(signal, back, 0) * masks[back])
    return total + taps[4:5]


def steps_of(raw, heads):
    shifted = raw + heads[0:1]
    step = softplus(shifted)
    log_decay = -step * jnp.exp(heads[1:2])
    lower = jnp.where(iota((TOKENS, TOKENS), 0) >= iota((TOKENS, TOKENS), 1), 1.0, 0.0).astype(F32)
    return shifted, step, dot(lower, log_decay, precision=HIGHEST)


def lane_masks():
    low = iota((1, 128), 1) < HEAD_DIM
    return (jnp.where(low, 1.0, 0.0).astype(BF16), jnp.where(low, 0.0, 1.0).astype(BF16))


def forward_kernel(
    u_ref, win_ref, wout_ref, segc_ref, segr_ref, taps_ref, heads_ref, gain_ref,
    zx_ref, y_ref, out_ref, square_ref, dtx_ref, affinity_ref, bias_ref,
):
    order = padded_order()
    u_padded = dot(u_ref[...], order).astype(BF16)
    zx_ref[...] = dot(u_padded[:, :512], win_ref[:, :OWN_COLS]) + dot(
        u_padded[:, 512:], win_ref[:, OWN_COLS : 2 * OWN_COLS]
    )
    taps = taps_ref[...]
    heads = heads_ref[...]
    segc = segc_ref[...]
    masks = tap_masks(segc)
    before = convolved(zx_ref[:, OWN : OWN + OWN_CONV], taps, masks)
    active = before * jax.nn.sigmoid(before)
    inputs = active[:, :OWN]
    writers = active[:, OWN : OWN + STATE].astype(BF16)
    readers = active[:, OWN + STATE :].astype(BF16)
    _, step, cumul = steps_of(zx_ref[:, OWN + OWN_CONV :], heads)
    cumul_rows = cumul.T
    spread = head_spread()
    dtx_ref[...] = (dot(step, spread, precision=HIGHEST) * inputs).astype(BF16)
    y_ref[...] = dot(heads, spread, precision=HIGHEST)[2:3] * inputs
    allowed = (iota((TOKENS, TOKENS), 0) >= iota((TOKENS, TOKENS), 1)) & (segc == segr_ref[...])
    bias_ref[...] = jnp.where(allowed, 0.0, NEGATIVE).astype(F32)
    affinity_ref[...] = dot_nt(readers, writers)
    halves = lane_masks()
    for pair in range(OWN_HEADS // 2):
        lanes = slice(128 * pair, 128 * pair + 128)
        pair_inputs = dtx_ref[:, lanes]
        for block in range(2):
            rows = slice(HALF * block, HALF * block + HALF)
            reach = HALF * (block + 1)
            total = y_ref[rows, lanes]
            for member in range(2):
                head = 2 * pair + member
                decay = jnp.exp(
                    cumul[rows, head : head + 1]
                    - cumul_rows[head : head + 1, :reach]
                    + bias_ref[rows, :reach]
                )
                mixing = (decay * affinity_ref[rows, :reach]).astype(BF16)
                total = total + dot(mixing, pair_inputs[:reach] * halves[member])
            y_ref[rows, lanes] = total
    gate = zx_ref[:, :OWN]
    gated = y_ref[...] * (gate * jax.nn.sigmoid(gate))
    out_ref[...] = dot((gated * gain_ref[0:1]).astype(BF16), wout_ref[...]).astype(out_ref.dtype)
    square_ref[...] = jnp.broadcast_to(
        jnp.sum(gated * gated, axis=1, keepdims=True), square_ref.shape
    )


def forward_mix(u, win, wout, segc, segr, taps, heads, gain, interpret=False):
    return pl.pallas_call(
        forward_kernel,
        out_shape=(
            jax.ShapeDtypeStruct((TOKENS, OWN_COLS), F32),
            jax.ShapeDtypeStruct((TOKENS, OWN), F32),
            jax.ShapeDtypeStruct((TOKENS, WIDTH), BF16),
            jax.ShapeDtypeStruct((TOKENS, 128), F32),
        ),
        scratch_shapes=[
            pltpu.VMEM((TOKENS, OWN), BF16),
            pltpu.VMEM((TOKENS, TOKENS), F32),
            pltpu.VMEM((TOKENS, TOKENS), F32),
        ],
        compiler_params=pltpu.CompilerParams(vmem_limit_bytes=58 * 2**20),
        interpret=interpret,
    )(u, win, wout, segc, segr, taps, heads, gain)


def backward_kernel(
    seed_ref, mean_ref, rho_ref, u_ref, win_ref, wout_ref, zx_ref, y_ref,
    segc_ref, segr_ref, taps_ref, heads_ref, gain_ref,
    du_ref, dwin_ref, dwout_ref, dtaps_ref, dheads_ref, dgain_ref,
    dtx_ref, affinity_ref, bias_ref, daffinity_ref, dy_ref, dzx_ref, dact_ref, rise_ref, direct_ref,
):
    seed = seed_ref[...]
    gain = gain_ref[0:1]
    rho = rho_ref[...]
    gate = zx_ref[:, :OWN]
    y = y_ref[...]
    open_gate = jax.nn.sigmoid(gate)
    passed = gate * open_gate
    scaled = y * passed * rho
    dyn = dot_nt(seed, wout_ref[...])
    dgain_ref[...] = jnp.broadcast_to(jnp.sum(dyn * scaled, axis=0, keepdims=True), dgain_ref.shape)
    dgated = rho * (dyn * gain - scaled * mean_ref[...])
    dy_ref[...] = dgated * passed
    dzx_ref[:, :OWN] = (dgated * y * (open_gate * (1.0 + gate * (1.0 - open_gate)))).astype(BF16)
    dwout_ref[...] = dot_tn((scaled * gain).astype(BF16), seed).astype(BF16)

    taps = taps_ref[...]
    heads = heads_ref[...]
    segc = segc_ref[...]
    masks = tap_masks(segc)
    signal = zx_ref[:, OWN : OWN + OWN_CONV]
    before = convolved(signal, taps, masks)
    open_act = jax.nn.sigmoid(before)
    active = before * open_act
    inputs = active[:, :OWN]
    writers = active[:, OWN : OWN + STATE].astype(BF16)
    readers = active[:, OWN + STATE :].astype(BF16)
    shifted, step, cumul = steps_of(zx_ref[:, OWN + OWN_CONV :], heads)
    cumul_rows = cumul.T
    spread = head_spread()
    step_wide = dot(step, spread, precision=HIGHEST)
    skip_wide = dot(heads, spread, precision=HIGHEST)[2:3]
    dtx_ref[...] = (step_wide * inputs).astype(BF16)
    allowed = (iota((TOKENS, TOKENS), 0) <= iota((TOKENS, TOKENS), 1)) & (segc == segr_ref[...])
    bias_ref[...] = jnp.where(allowed, 0.0, NEGATIVE).astype(F32)
    affinity_ref[...] = dot_nt(writers, readers)
    daffinity_ref[...] = jnp.zeros_like(daffinity_ref)
    rise_ref[...] = jnp.zeros_like(rise_ref)
    halves = lane_masks()
    head_lane = iota((1, 128), 1)
    fall_blocks = [jnp.zeros((HALF, 128), F32), jnp.zeros((HALF, 128), F32)]
    for pair in range(OWN_HEADS // 2):
        lanes = slice(128 * pair, 128 * pair + 128)
        pair_inputs = dtx_ref[:, lanes]
        pair_dy = dy_ref[:, lanes].astype(BF16)
        member_dy = [pair_dy * half for half in halves]
        for block in range(2):
            rows = slice(HALF * block, HALF * block + HALF)
            start = HALF * block
            dinput = jnp.zeros((HALF, 128), F32)
            for member in range(2):
                head = 2 * pair + member
                decay = jnp.exp(
                    cumul_rows[head : head + 1, start:]
                    - cumul[rows, head : head + 1]
                    + bias_ref[rows, start:]
                )
                dmixing = dot_nt(pair_inputs[rows], member_dy[member][start:]) * decay
                daffinity_ref[rows, start:] += dmixing
                affinity = affinity_ref[rows, start:]
                dinput = dinput + dot((decay * affinity).astype(BF16), member_dy[member][start:])
                dspread = dmixing * affinity
                fall = jnp.sum(dspread, axis=1, keepdims=True)
                fall_blocks[block] = fall_blocks[block] + jnp.where(head_lane == head, fall, 0.0)
                rise_ref[head : head + 1, start:] += jnp.sum(dspread, axis=0, keepdims=True)
            direct_ref[rows, lanes] = dinput
    dinputs = direct_ref[...]
    dy = dy_ref[...]
    dact_ref[:, :OWN] = step_wide * dinputs + skip_wide * dy
    daffinity = daffinity_ref[...].astype(BF16)
    dact_ref[:, OWN : OWN + STATE] = dot(daffinity, readers)
    dact_ref[:, OWN + STATE :] = dot_tn(daffinity, writers)
    dstep = dot_nt(dinputs * inputs, spread, precision=HIGHEST)
    skip_sum = jnp.broadcast_to(jnp.sum(dy * inputs, axis=0, keepdims=True), (8, OWN))
    dskip = dot_nt(skip_sum, spread, precision=HIGHEST)[0:1]
    dcumul = rise_ref[...].T - jnp.concatenate(fall_blocks, axis=0)
    upper = jnp.where(iota((TOKENS, TOKENS), 0) <= iota((TOKENS, TOKENS), 1), 1.0, 0.0).astype(F32)
    dlog = dot(upper, dcumul, precision=HIGHEST)
    rate = jnp.exp(heads[1:2])
    draw = (dstep - dlog * rate) * jax.nn.sigmoid(shifted)
    dheads_ref[...] = jnp.zeros_like(dheads_ref)
    dheads_ref[0:1] = jnp.sum(draw, axis=0, keepdims=True)
    dheads_ref[1:2] = jnp.sum(-dlog * step * rate, axis=0, keepdims=True)
    dheads_ref[2:3] = dskip
    dzx_ref[:, OWN + OWN_CONV :] = draw.astype(BF16)

    dconv = dact_ref[...] * (open_act * (1.0 + before * (1.0 - open_act)))
    dtaps_ref[...] = jnp.zeros_like(dtaps_ref)
    dtaps_ref[4:5] = jnp.sum(dconv, axis=0, keepdims=True)
    dtaps_ref[3:4] = jnp.sum(dconv * signal, axis=0, keepdims=True)
    dsignal = taps[3:4] * dconv
    for back in range(1, 4):
        masked = dconv * masks[back]
        dtaps_ref[3 - back : 4 - back] = jnp.sum(
            masked * pltpu.roll(signal, back, 0), axis=0, keepdims=True
        )
        dsignal = dsignal + taps[3 - back : 4 - back] * pltpu.roll(masked, TOKENS - back, 0)
    dzx_ref[:, OWN : OWN + OWN_CONV] = dsignal.astype(BF16)

    order = padded_order()
    dzx = dzx_ref[...]
    u_padded = dot(u_ref[...], order).astype(BF16)
    du_parts = []
    for core in range(2):
        columns = slice(OWN_COLS * core, OWN_COLS * core + OWN_COLS)
        dwin_ref[:, columns] = dot_tn(u_padded[:, 512 * core : 512 * core + 512], dzx).astype(BF16)
        du_parts.append(dot_nt(dzx, win_ref[:, columns]).astype(BF16))
    du_ref[...] = dot_nt(jnp.concatenate(du_parts, axis=1), order).astype(BF16)


def backward_mix(seed, mean, rho, u, win, wout, zx, y, segc, segr, taps, heads, gain, interpret=False):
    square = (TOKENS, TOKENS)
    return pl.pallas_call(
        backward_kernel,
        out_shape=(
            jax.ShapeDtypeStruct((TOKENS, WIDTH), BF16),
            jax.ShapeDtypeStruct((512, 2 * OWN_COLS), BF16),
            jax.ShapeDtypeStruct((OWN, WIDTH), BF16),
            jax.ShapeDtypeStruct((8, OWN_CONV), F32),
            jax.ShapeDtypeStruct((8, 128), F32),
            jax.ShapeDtypeStruct((8, OWN), F32),
        ),
        scratch_shapes=[
            pltpu.VMEM((TOKENS, OWN), BF16),
            pltpu.VMEM(square, F32),
            pltpu.VMEM(square, F32),
            pltpu.VMEM(square, F32),
            pltpu.VMEM((TOKENS, OWN), F32),
            pltpu.VMEM((TOKENS, OWN_COLS), BF16),
            pltpu.VMEM((TOKENS, OWN_CONV), F32),
            pltpu.VMEM((128, TOKENS), F32),
            pltpu.VMEM((TOKENS, OWN), F32),
        ],
        compiler_params=pltpu.CompilerParams(vmem_limit_bytes=58 * 2**20),
        interpret=interpret,
    )(seed, mean, rho, u, win, wout, zx, y, segc, segr, taps, heads, gain)


DP = ("dp_0", "dp_1", "dp_2")
DP_SEQ = DP + ("seq",)
CHIPS = 64
LAYERS = 2
GATHER_COLS = 2 * OWN_COLS + 3 * 384 + 128


def swapped(v):
    return lax.ppermute(v, "seq", [(0, 1), (1, 0)])


def part(v, index, size, axis):
    return lax.dynamic_slice_in_dim(v, index * size, size, axis)


def in_order(core, own, other, axis):
    first = jnp.where(core == 0, own, other)
    second = jnp.where(core == 0, other, own)
    return jnp.concatenate([first, second], axis=axis)


def padded(v, sizes):
    return jnp.pad(v, [(0, size - now) for now, size in zip(v.shape, sizes)])


def columns_of(win, core):
    gate = part(win, core, OWN, 2)
    inputs = part(win[:, :, INNER : 2 * INNER], core, OWN, 2)
    shared = win[:, :, 2 * INNER : INNER + CONV_CH]
    steps = part(win[:, :, INNER + CONV_CH :], core, OWN_HEADS, 2)
    steps = padded(steps, steps.shape[:2] + (128,))
    return jnp.concatenate([gate, inputs, shared, steps], axis=2)


def packed_weights(win, wout, kernel_weight, kernel_bias, norm_gain, gate_gain, core):
    win = padded(win, (LAYERS, 8, win.shape[2]))
    win_part = in_order(core, columns_of(win, core), swapped(columns_of(win, 1 - core)), 2)
    wout_part = in_order(core, part(wout, core, 384, 2), swapped(part(wout, 1 - core, 384, 2)), 1)
    wout_part = wout_part.reshape(LAYERS, 3, 8, 384).transpose(0, 2, 1, 3).reshape(LAYERS, 8, 1152)
    rows = [padded(kernel_weight, (LAYERS, 4, 16))]
    for vector in (kernel_bias, norm_gain, gate_gain):
        rows.append(padded(vector[:, None], (LAYERS, 1, 16)))
    vectors = padded(jnp.concatenate(rows, axis=1), (LAYERS, 8, 16))
    vectors = padded(in_order(core, vectors, swapped(vectors), 2), (LAYERS, 8, 128))
    return jnp.concatenate([win_part, wout_part, vectors], axis=2)


def gathered_weights(block):
    spread = jnp.broadcast_to(block[None], (CHIPS,) + block.shape)
    return lax.all_to_all(spread, DP, 0, 0, tiled=True)


def unpacked_weights(gathered, core):
    wout = gathered[:, :, 2 * OWN_COLS : 2 * OWN_COLS + 1152].reshape(CHIPS, 8, 3, 384)
    wout = wout.transpose(0, 2, 1, 3).reshape(INNER, 384)
    wout = in_order(core, part(wout, core, OWN, 0), swapped(part(wout, 1 - core, OWN, 0)), 1)
    vectors = gathered[:, :, GATHER_COLS - 128 : GATHER_COLS - 96].astype(F32)
    vectors = vectors.reshape(CHIPS, 8, 2, 16).transpose(1, 0, 2, 3)
    taps = vectors[:5, :, :, :14].reshape(5, CONV_CH)
    taps = jnp.concatenate([part(taps[:, :INNER], core, OWN, 1), taps[:, INNER:]], axis=1)
    norm = vectors[5, :, :, :6].reshape(1, WIDTH)
    gain = part(vectors[6, :, :, :12].reshape(1, INNER), core, OWN, 1)
    return (
        gathered.reshape(CHIPS * 8, GATHER_COLS),
        wout,
        padded(taps, (8, OWN_CONV)),
        norm,
        jnp.broadcast_to(gain, (8, OWN)),
    )


def over_positions(partial_sum, core):
    own = part(partial_sum, core, HALF, 0).astype(F32)
    return own + swapped(part(partial_sum, 1 - core, HALF, 0)).astype(F32)


def packed_gradients(dwin, dwout, dtaps, dheads, dnorm, dgain, core):
    dwout = in_order(core, part(dwout, core, 384, 1), swapped(part(dwout, 1 - core, 384, 1)), 0)
    dwout = dwout.reshape(CHIPS, 3, 8, 384).transpose(0, 2, 1, 3).reshape(CHIPS, 8, 1152)
    taps = jnp.zeros((5, INNER), F32)
    taps = lax.dynamic_update_slice_in_dim(taps, dtaps[:5, :OWN], core * OWN, 1)
    taps = jnp.concatenate([taps, dtaps[:5, OWN:]], axis=1)
    gain = lax.dynamic_update_slice_in_dim(jnp.zeros((1, INNER), F32), dgain[:1], core * OWN, 1)
    heads = jnp.zeros((3, HEADS), F32)
    heads = lax.dynamic_update_slice_in_dim(
        heads, dheads[:3, :OWN_HEADS], core * OWN_HEADS, 1
    ).reshape(1, 72)
    rows = [padded(taps.reshape(5, CHIPS, 2, 14), (5, CHIPS, 2, 16))]
    rows.append(padded(dnorm.reshape(1, CHIPS, 2, 6), (1, CHIPS, 2, 16)))
    rows.append(padded(gain.reshape(1, CHIPS, 2, 12), (1, CHIPS, 2, 16)))
    vectors = jnp.concatenate(rows, axis=0).reshape(7, CHIPS, 32)
    vectors = padded(vectors, (7, CHIPS, 128)).transpose(1, 0, 2)
    heads = jnp.broadcast_to(jnp.pad(heads, ((0, 0), (32, 24)))[None], (CHIPS, 1, 128))
    vectors = jnp.concatenate([vectors, heads], axis=1)
    vectors = vectors + swapped(vectors)
    high = lax.reduce_precision(vectors, 8, 7)
    return jnp.concatenate(
        [
            dwin.reshape(CHIPS, 8, 2 * OWN_COLS),
            dwout,
            high.astype(BF16),
            (vectors - high).astype(BF16),
        ],
        axis=2,
    )


def reduced_gradients(packed):
    arrived = lax.all_to_all(packed, DP, 0, 0, tiled=True)
    return jnp.sum(arrived.astype(F32), axis=0)


def unpacked_gradients(total, core):
    win = [total[:6, :OWN_COLS], total[:6, OWN_COLS : 2 * OWN_COLS]]
    own = jnp.where(core == 0, win[0], win[1])
    got = swapped(jnp.where(core == 0, win[1], win[0]))
    left = jnp.where(core == 0, own, got)
    right = jnp.where(core == 0, got, own)
    shared = slice(2 * OWN, 2 * OWN + 2 * STATE)
    steps = slice(2 * OWN + 2 * STATE, 2 * OWN + 2 * STATE + OWN_HEADS)
    dwin = jnp.concatenate(
        [
            left[:, :OWN],
            right[:, :OWN],
            left[:, OWN : 2 * OWN],
            right[:, OWN : 2 * OWN],
            left[:, shared] + right[:, shared],
            left[:, steps],
            right[:, steps],
        ],
        axis=1,
    )
    start = 2 * OWN_COLS
    wout = total[:, start : start + 1152].reshape(8, 3, 384).transpose(1, 0, 2).reshape(24, 384)
    dwout = in_order(core, part(wout, core, 12, 0), swapped(part(wout, 1 - core, 12, 0)), 1)
    vectors = total[:, start + 1152 : start + 1280] + total[:, start + 1280 : start + 1408]
    own_vectors = part(vectors[:, :32], core, 16, 1)
    return (
        dwin,
        dwout,
        own_vectors[:4, :14],
        own_vectors[4, :14],
        own_vectors[5, :6],
        own_vectors[6, :12],
        vectors[7, 32:104].reshape(3, HEADS),
    )


def mean_square_scale(values):
    return lax.rsqrt(jnp.mean(values * values, axis=1, keepdims=True) + NORM_EPS)


def layers_of(hidden, cotangent, segments, head_values, weights_of, core, send, interpret=False):
    segr = segments
    segc = segments.reshape(TOKENS, 1)
    heads_all = padded(part(head_values, core, OWN_HEADS, 2), (LAYERS, 8, 128))
    current = hidden.astype(F32)
    saved = []
    for layer in range(LAYERS):
        win, wout, taps, norm, gain = weights_of(layer)
        heads = heads_all[layer]
        sigma = mean_square_scale(current)
        u = lax.all_gather((current * sigma * norm).astype(BF16), "seq", axis=0, tiled=True)
        zx, y, out, square = forward_mix(
            u, win, wout, segc, segr, taps, heads, gain, interpret=interpret
        )
        square = square + swapped(square)
        rho = lax.rsqrt(square[:, :1] / INNER + NORM_EPS)
        branch = over_positions(out, core)
        own_rho = part(rho, core, HALF, 0)
        saved.append((current, sigma, u, zx, y, rho, own_rho, branch))
        current = current + own_rho * branch
    upstream = cotangent.astype(F32)
    sent = [None] * LAYERS
    for layer in reversed(range(LAYERS)):
        win, wout, taps, norm, gain = weights_of(layer)
        heads = heads_all[layer]
        before, sigma, u, zx, y, rho, own_rho, branch = saved[layer]
        seed = upstream.astype(BF16)
        mean = own_rho * jnp.sum(seed.astype(F32) * branch, axis=1, keepdims=True) / INNER
        seed = lax.all_gather(seed, "seq", axis=0, tiled=True)
        mean = lax.all_gather(jnp.broadcast_to(mean, (HALF, 128)), "seq", axis=0, tiled=True)
        du, dwin, dwout, dtaps, dheads, dgain = backward_mix(
            seed, mean[:, :1], rho, u, win, wout, zx, y, segc, segr, taps, heads, gain,
            interpret=interpret,
        )
        du = over_positions(du, core)
        dnorm = jnp.sum(du * (before * sigma), axis=0, keepdims=True)
        scaled = du * norm
        upstream = upstream + sigma * (
            scaled
            - before * (sigma * sigma) * jnp.mean(scaled * before, axis=1, keepdims=True)
        )
        sent[layer] = send(dwin, dwout, dtaps, dheads, dnorm, dgain)
    return current.astype(BF16), upstream.astype(BF16), sent


def per_device(
    hidden_in,
    segments,
    projection_in,
    projection_out,
    kernel_weight,
    kernel_bias,
    norm_gain,
    gate_gain,
    head_values,
    cotangent,
):
    core = lax.axis_index("seq")
    blocks = packed_weights(
        projection_in, projection_out, kernel_weight, kernel_bias, norm_gain, gate_gain, core
    )
    weights = [unpacked_weights(gathered_weights(blocks[layer]), core) for layer in range(LAYERS)]

    def send(*gradients):
        return reduced_gradients(packed_gradients(*gradients, core))

    hidden_out, input_gradient, totals = layers_of(
        hidden_in[0], cotangent[0], segments, head_values, lambda layer: weights[layer], core, send
    )
    pieces = [unpacked_gradients(total, core) for total in totals]
    stacked = tuple(jnp.stack([piece[slot] for piece in pieces]) for slot in range(7))
    return (hidden_out[None], input_gradient[None]) + stacked


def solution(mesh):
    torus = Mesh(mesh.devices.reshape(4, 4, 4, mesh.shape["seq"]), DP_SEQ)
    tokens = P(DP, "seq", None)
    weights = (
        P(None, DP_SEQ, None),
        P(None, DP_SEQ, None),
        P(None, None, DP_SEQ),
        P(None, DP_SEQ),
        P(None, DP_SEQ),
        P(None, DP_SEQ),
    )
    return jax.shard_map(
        per_device,
        mesh=torus,
        in_specs=(tokens, P(DP, None)) + weights + (P(), tokens),
        out_specs=(tokens, tokens) + weights + (P(),),
        check_vma=False,
    )
```

```python
import jax
import jax.numpy as jnp
from jax import lax
from jax.experimental import pallas as pl
from jax.experimental.pallas import tpu as pltpu
from jax.sharding import Mesh
from jax.sharding import PartitionSpec as P

HEADS = 24
HEAD_DIM = 64
STATE = 128
INNER = 1536
CONV_CH = 1792
WIDTH = 768
TOKENS = 512
HALF = 256
OWN_HEADS = 12
OWN = OWN_HEADS * HEAD_DIM
OWN_CONV = OWN + 2 * STATE
OWN_COLS = OWN + OWN_CONV + 128
FOLD = 1024
WIN_COLS = OWN_COLS + FOLD
STEP_TILE = OWN + OWN_CONV
NORM_EPS = 1e-05
NEGATIVE = -1e30
F32 = jnp.float32
BF16 = jnp.bfloat16
HIGHEST = lax.Precision.HIGHEST


def dot(a, b, dims=((1,), (0,)), precision=None):
    return lax.dot_general(a, b, (dims, ((), ())), precision=precision, preferred_element_type=F32)


def dot_nt(a, b, precision=None):
    return dot(a, b, ((1,), (1,)), precision)


def dot_tn(a, b, precision=None):
    return dot(a, b, ((0,), (0,)), precision)


def iota(shape, dim):
    return lax.broadcasted_iota(jnp.int32, shape, dim)


def padded_orders():
    column = iota((WIDTH, 512), 1)
    row = iota((WIDTH, 512), 0)
    start = 12 * (column >> 3)
    place = column & 7
    features = (
        start + place,
        jnp.where(place < 4, start + place + 8, -1),
        jnp.where(place < 4, -1, start + place + 4),
    )
    return [jnp.where(feature == row, 1.0, 0.0).astype(BF16) for feature in features]


def head_spread():
    return jnp.where(iota((128, OWN), 0) == (iota((128, OWN), 1) >> 6), 1.0, 0.0).astype(F32)


def softplus(v):
    return jnp.maximum(v, 0.0) + jnp.log1p(jnp.exp(-jnp.abs(v)))


def tap_masks(segment_column):
    position = iota((TOKENS, 1), 0)
    wide = jnp.broadcast_to(segment_column, (TOKENS, 128))
    masks = [None]
    for back in range(1, 4):
        before = pltpu.roll(wide, back, 0)[:, :1]
        same = (before == segment_column) & (position >= back)
        masks.append(jnp.where(same, 1.0, 0.0).astype(F32))
    return masks


def convolved(signal, taps, masks):
    total = taps[3:4] * signal
    for back in range(1, 4):
        total = total + taps[3 - back : 4 - back] * (pltpu.roll(signal, back, 0) * masks[back])
    return total + taps[4:5]


def steps_of(raw, heads):
    shifted = raw + heads[0:1]
    step = softplus(shifted)
    log_decay = -step * jnp.exp(heads[1:2])
    lower = jnp.where(iota((TOKENS, TOKENS), 0) >= iota((TOKENS, TOKENS), 1), 1.0, 0.0).astype(F32)
    return shifted, step, dot(lower, log_decay, precision=HIGHEST)


def lane_masks():
    low = iota((1, 128), 1) < HEAD_DIM
    return (jnp.where(low, 1.0, 0.0).astype(BF16), jnp.where(low, 0.0, 1.0).astype(BF16))


def forward_kernel(
    u_ref, win_ref, wout_ref, segc_ref, segr_ref, taps_ref, heads_ref, gain_ref,
    zx_ref, y_ref, out_ref, square_ref, dtx_ref, affinity_ref, bias_ref,
):
    u = u_ref[...]
    u_full, u_low, u_high = [dot(u, order).astype(BF16) for order in padded_orders()]
    zx_ref[:, :FOLD] = dot(u_full, win_ref[:, :FOLD]) + dot(
        u_low, win_ref[:, OWN_COLS : OWN_COLS + FOLD]
    )
    zx_ref[:, FOLD:] = dot(u_full, win_ref[:, FOLD:OWN_COLS]) + dot(
        u_high, win_ref[:, OWN_COLS : 2 * OWN_COLS - FOLD]
    )
    taps = taps_ref[...]
    heads = heads_ref[...]
    segc = segc_ref[...]
    masks = tap_masks(segc)
    before = convolved(zx_ref[:, OWN : OWN + OWN_CONV], taps, masks)
    active = before * jax.nn.sigmoid(before)
    inputs = active[:, :OWN]
    writers = active[:, OWN : OWN + STATE].astype(BF16)
    readers = active[:, OWN + STATE :].astype(BF16)
    _, step, cumul = steps_of(zx_ref[:, OWN + OWN_CONV :], heads)
    cumul_rows = cumul.T
    spread = head_spread()
    dtx_ref[...] = (dot(step, spread, precision=HIGHEST) * inputs).astype(BF16)
    y_ref[...] = dot(heads, spread, precision=HIGHEST)[2:3] * inputs
    allowed = (iota((TOKENS, TOKENS), 0) >= iota((TOKENS, TOKENS), 1)) & (segc == segr_ref[...])
    bias_ref[...] = jnp.where(allowed, 0.0, NEGATIVE).astype(F32)
    affinity_ref[...] = dot_nt(readers, writers)
    halves = lane_masks()
    for pair in range(OWN_HEADS // 2):
        lanes = slice(128 * pair, 128 * pair + 128)
        pair_inputs = dtx_ref[:, lanes]
        for block in range(2):
            rows = slice(HALF * block, HALF * block + HALF)
            reach = HALF * (block + 1)
            total = y_ref[rows, lanes]
            for member in range(2):
                head = 2 * pair + member
                decay = jnp.exp(
                    cumul[rows, head : head + 1]
                    - cumul_rows[head : head + 1, :reach]
                    + bias_ref[rows, :reach]
                )
                mixing = (decay * affinity_ref[rows, :reach]).astype(BF16)
                total = total + dot(mixing, pair_inputs[:reach] * halves[member])
            y_ref[rows, lanes] = total
    gate = zx_ref[:, :OWN]
    gated = y_ref[...] * (gate * jax.nn.sigmoid(gate))
    out_ref[...] = dot((gated * gain_ref[0:1]).astype(BF16), wout_ref[...]).astype(out_ref.dtype)
    square_ref[...] = jnp.broadcast_to(
        jnp.sum(gated * gated, axis=1, keepdims=True), square_ref.shape
    )


def forward_mix(u, win, wout, segc, segr, taps, heads, gain, interpret=False):
    return pl.pallas_call(
        forward_kernel,
        out_shape=(
            jax.ShapeDtypeStruct((TOKENS, OWN_COLS), F32),
            jax.ShapeDtypeStruct((TOKENS, OWN), F32),
            jax.ShapeDtypeStruct((TOKENS, WIDTH), BF16),
            jax.ShapeDtypeStruct((TOKENS, 128), F32),
        ),
        scratch_shapes=[
            pltpu.VMEM((TOKENS, OWN), BF16),
            pltpu.VMEM((TOKENS, TOKENS), F32),
            pltpu.VMEM((TOKENS, TOKENS), F32),
        ],
        compiler_params=pltpu.CompilerParams(vmem_limit_bytes=58 * 2**20),
        interpret=interpret,
    )(u, win, wout, segc, segr, taps, heads, gain)


def backward_kernel(
    seed_ref, mean_ref, rho_ref, u_ref, win_ref, wout_ref, zx_ref, y_ref,
    segc_ref, segr_ref, taps_ref, heads_ref, gain_ref,
    du_ref, dwin_ref, dwout_ref, dtaps_ref, dheads_ref, dgain_ref,
    dtx_ref, affinity_ref, bias_ref, daffinity_ref, dy_ref, dzx_ref, dact_ref, rise_ref, direct_ref,
):
    seed = seed_ref[...]
    gain = gain_ref[0:1]
    rho = rho_ref[...]
    gate = zx_ref[:, :OWN]
    y = y_ref[...]
    open_gate = jax.nn.sigmoid(gate)
    passed = gate * open_gate
    scaled = y * passed * rho
    dyn = dot_nt(seed, wout_ref[...])
    dgain_ref[...] = jnp.broadcast_to(jnp.sum(dyn * scaled, axis=0, keepdims=True), dgain_ref.shape)
    dgated = rho * (dyn * gain - scaled * mean_ref[...])
    dy_ref[...] = dgated * passed
    dzx_ref[:, :OWN] = (dgated * y * (open_gate * (1.0 + gate * (1.0 - open_gate)))).astype(BF16)
    dwout_ref[...] = dot_tn((scaled * gain).astype(BF16), seed).astype(BF16)

    taps = taps_ref[...]
    heads = heads_ref[...]
    segc = segc_ref[...]
    masks = tap_masks(segc)
    signal = zx_ref[:, OWN : OWN + OWN_CONV]
    before = convolved(signal, taps, masks)
    open_act = jax.nn.sigmoid(before)
    active = before * open_act
    inputs = active[:, :OWN]
    writers = active[:, OWN : OWN + STATE].astype(BF16)
    readers = active[:, OWN + STATE :].astype(BF16)
    shifted, step, cumul = steps_of(zx_ref[:, OWN + OWN_CONV :], heads)
    cumul_rows = cumul.T
    spread = head_spread()
    step_wide = dot(step, spread, precision=HIGHEST)
    skip_wide = dot(heads, spread, precision=HIGHEST)[2:3]
    dtx_ref[...] = (step_wide * inputs).astype(BF16)
    allowed = (iota((TOKENS, TOKENS), 0) <= iota((TOKENS, TOKENS), 1)) & (segc == segr_ref[...])
    bias_ref[...] = jnp.where(allowed, 0.0, NEGATIVE).astype(F32)
    affinity_ref[...] = dot_nt(writers, readers)
    daffinity_ref[...] = jnp.zeros_like(daffinity_ref)
    rise_ref[...] = jnp.zeros_like(rise_ref)
    halves = lane_masks()
    head_lane = iota((1, 128), 1)
    fall_blocks = [jnp.zeros((HALF, 128), F32), jnp.zeros((HALF, 128), F32)]
    for pair in range(OWN_HEADS // 2):
        lanes = slice(128 * pair, 128 * pair + 128)
        pair_inputs = dtx_ref[:, lanes]
        pair_dy = dy_ref[:, lanes].astype(BF16)
        member_dy = [pair_dy * half for half in halves]
        for block in range(2):
            rows = slice(HALF * block, HALF * block + HALF)
            start = HALF * block
            dinput = jnp.zeros((HALF, 128), F32)
            for member in range(2):
                head = 2 * pair + member
                decay = jnp.exp(
                    cumul_rows[head : head + 1, start:]
                    - cumul[rows, head : head + 1]
                    + bias_ref[rows, start:]
                )
                dmixing = dot_nt(pair_inputs[rows], member_dy[member][start:]) * decay
                daffinity_ref[rows, start:] += dmixing
                affinity = affinity_ref[rows, start:]
                dinput = dinput + dot((decay * affinity).astype(BF16), member_dy[member][start:])
                dspread = dmixing * affinity
                fall = jnp.sum(dspread, axis=1, keepdims=True)
                fall_blocks[block] = fall_blocks[block] + jnp.where(head_lane == head, fall, 0.0)
                rise_ref[head : head + 1, start:] += jnp.sum(dspread, axis=0, keepdims=True)
            direct_ref[rows, lanes] = dinput
    dinputs = direct_ref[...]
    dy = dy_ref[...]
    dact_ref[:, :OWN] = step_wide * dinputs + skip_wide * dy
    daffinity = daffinity_ref[...].astype(BF16)
    dact_ref[:, OWN : OWN + STATE] = dot(daffinity, readers)
    dact_ref[:, OWN + STATE :] = dot_tn(daffinity, writers)
    dstep = dot_nt(dinputs * inputs, spread, precision=HIGHEST)
    skip_sum = jnp.broadcast_to(jnp.sum(dy * inputs, axis=0, keepdims=True), (8, OWN))
    dskip = dot_nt(skip_sum, spread, precision=HIGHEST)[0:1]
    dcumul = rise_ref[...].T - jnp.concatenate(fall_blocks, axis=0)
    upper = jnp.where(iota((TOKENS, TOKENS), 0) <= iota((TOKENS, TOKENS), 1), 1.0, 0.0).astype(F32)
    dlog = dot(upper, dcumul, precision=HIGHEST)
    rate = jnp.exp(heads[1:2])
    draw = (dstep - dlog * rate) * jax.nn.sigmoid(shifted)
    dheads_ref[...] = jnp.zeros_like(dheads_ref)
    dheads_ref[0:1] = jnp.sum(draw, axis=0, keepdims=True)
    dheads_ref[1:2] = jnp.sum(-dlog * step * rate, axis=0, keepdims=True)
    dheads_ref[2:3] = dskip
    dzx_ref[:, OWN + OWN_CONV :] = draw.astype(BF16)

    dconv = dact_ref[...] * (open_act * (1.0 + before * (1.0 - open_act)))
    dtaps_ref[...] = jnp.zeros_like(dtaps_ref)
    dtaps_ref[4:5] = jnp.sum(dconv, axis=0, keepdims=True)
    dtaps_ref[3:4] = jnp.sum(dconv * signal, axis=0, keepdims=True)
    dsignal = taps[3:4] * dconv
    for back in range(1, 4):
        masked = dconv * masks[back]
        dtaps_ref[3 - back : 4 - back] = jnp.sum(
            masked * pltpu.roll(signal, back, 0), axis=0, keepdims=True
        )
        dsignal = dsignal + taps[3 - back : 4 - back] * pltpu.roll(masked, TOKENS - back, 0)
    dzx_ref[:, OWN : OWN + OWN_CONV] = dsignal.astype(BF16)

    orders = padded_orders()
    dzx = dzx_ref[...]
    u = u_ref[...]
    u_full, u_low, u_high = [dot(u, order).astype(BF16) for order in orders]
    rest = OWN_COLS - FOLD
    dwin_ref[:, :OWN_COLS] = dot_tn(u_full, dzx).astype(BF16)
    folded = dot_tn(u_low, dzx[:, :FOLD])
    dwin_ref[:, OWN_COLS : OWN_COLS + rest] = (
        folded[:, :rest] + dot_tn(u_high, dzx[:, FOLD:])
    ).astype(BF16)
    dwin_ref[:, OWN_COLS + rest :] = folded[:, rest:].astype(BF16)
    du_parts = (
        dot_nt(dzx, win_ref[:, :OWN_COLS]),
        dot_nt(dzx[:, :FOLD], win_ref[:, OWN_COLS:WIN_COLS]),
        dot_nt(dzx[:, FOLD:], win_ref[:, OWN_COLS : OWN_COLS + rest]),
    )
    du = [dot_nt(piece.astype(BF16), order) for piece, order in zip(du_parts, orders)]
    du_ref[...] = (du[0] + du[1] + du[2]).astype(BF16)


def backward_mix(seed, mean, rho, u, win, wout, zx, y, segc, segr, taps, heads, gain, interpret=False):
    square = (TOKENS, TOKENS)
    return pl.pallas_call(
        backward_kernel,
        out_shape=(
            jax.ShapeDtypeStruct((TOKENS, WIDTH), BF16),
            jax.ShapeDtypeStruct((512, WIN_COLS), BF16),
            jax.ShapeDtypeStruct((OWN, WIDTH), BF16),
            jax.ShapeDtypeStruct((8, OWN_CONV), F32),
            jax.ShapeDtypeStruct((8, 128), F32),
            jax.ShapeDtypeStruct((8, OWN), F32),
        ),
        scratch_shapes=[
            pltpu.VMEM((TOKENS, OWN), BF16),
            pltpu.VMEM(square, F32),
            pltpu.VMEM(square, F32),
            pltpu.VMEM(square, F32),
            pltpu.VMEM((TOKENS, OWN), F32),
            pltpu.VMEM((TOKENS, OWN_COLS), BF16),
            pltpu.VMEM((TOKENS, OWN_CONV), F32),
            pltpu.VMEM((128, TOKENS), F32),
            pltpu.VMEM((TOKENS, OWN), F32),
        ],
        compiler_params=pltpu.CompilerParams(vmem_limit_bytes=58 * 2**20),
        interpret=interpret,
    )(seed, mean, rho, u, win, wout, zx, y, segc, segr, taps, heads, gain)


DP = ("dp_0", "dp_1", "dp_2")
DP_SEQ = DP + ("seq",)
CHIPS = 64
LAYERS = 2
GATHER_COLS = WIN_COLS + 3 * 384
VECTORS = STEP_TILE + OWN_HEADS


def swapped(v):
    return lax.ppermute(v, "seq", [(0, 1), (1, 0)])


def part(v, index, size, axis):
    return lax.dynamic_slice_in_dim(v, index * size, size, axis)


def in_order(core, own, other, axis):
    first = jnp.where(core == 0, own, other)
    second = jnp.where(core == 0, other, own)
    return jnp.concatenate([first, second], axis=axis)


def padded(v, sizes):
    return jnp.pad(v, [(0, size - now) for now, size in zip(v.shape, sizes)])


def columns_of(win, core):
    gate = part(win, core, OWN, 2)
    inputs = part(win[:, :, INNER : 2 * INNER], core, OWN, 2)
    shared = win[:, :, 2 * INNER : INNER + CONV_CH]
    steps = part(win[:, :, INNER + CONV_CH :], core, OWN_HEADS, 2)
    steps = padded(steps, steps.shape[:2] + (128,))
    return jnp.concatenate([gate, inputs, shared, steps], axis=2)


def packed_weights(win, wout, kernel_weight, kernel_bias, norm_gain, gate_gain, core):
    win_rows = in_order(core, columns_of(win, core), swapped(columns_of(win, 1 - core)), 1)
    folded = padded(win_rows[:, 8:], (LAYERS, 4, 2 * FOLD)).reshape(LAYERS, 4, 2, FOLD)
    folded = folded.transpose(0, 2, 1, 3).reshape(LAYERS, 8, FOLD)
    wout_part = in_order(core, part(wout, core, 384, 2), swapped(part(wout, 1 - core, 384, 2)), 1)
    wout_part = wout_part.reshape(LAYERS, 3, 8, 384).transpose(0, 2, 1, 3).reshape(LAYERS, 8, 1152)
    rows = [padded(kernel_weight, (LAYERS, 4, 16))]
    for vector in (kernel_bias, norm_gain, gate_gain):
        rows.append(padded(vector[:, None], (LAYERS, 1, 16)))
    vectors = padded(jnp.concatenate(rows, axis=1), (LAYERS, 8, 16))
    vectors = in_order(core, vectors, swapped(vectors), 2)
    steps = win_rows[:, :8, STEP_TILE:VECTORS]
    tile = padded(jnp.concatenate([steps, vectors], axis=2), (LAYERS, 8, 128))
    return jnp.concatenate([win_rows[:, :8, :STEP_TILE], tile, folded, wout_part], axis=2)


def gathered_weights(block):
    spread = jnp.broadcast_to(block[None], (CHIPS,) + block.shape)
    return lax.all_to_all(spread, DP, 0, 0, tiled=True)


def unpacked_weights(gathered, core):
    wout = gathered[:, :, WIN_COLS:].reshape(CHIPS, 8, 3, 384)
    wout = wout.transpose(0, 2, 1, 3).reshape(INNER, 384)
    wout = in_order(core, part(wout, core, OWN, 0), swapped(part(wout, 1 - core, OWN, 0)), 1)
    vectors = gathered[:, :, VECTORS : VECTORS + 32].astype(F32)
    vectors = vectors.reshape(CHIPS, 8, 2, 16).transpose(1, 0, 2, 3)
    taps = vectors[:5, :, :, :14].reshape(5, CONV_CH)
    taps = jnp.concatenate([part(taps[:, :INNER], core, OWN, 1), taps[:, INNER:]], axis=1)
    norm = vectors[5, :, :, :6].reshape(1, WIDTH)
    gain = part(vectors[6, :, :, :12].reshape(1, INNER), core, OWN, 1)
    return (
        gathered.reshape(CHIPS * 8, GATHER_COLS),
        wout,
        padded(taps, (8, OWN_CONV)),
        norm,
        jnp.broadcast_to(gain, (8, OWN)),
    )


def over_positions(partial_sum, core):
    own = part(partial_sum, core, HALF, 0).astype(F32)
    return own + swapped(part(partial_sum, 1 - core, HALF, 0)).astype(F32)


def packed_gradients(dwin, dwout, dtaps, dheads, dnorm, dgain, core):
    dwout = in_order(core, part(dwout, core, 384, 1), swapped(part(dwout, 1 - core, 384, 1)), 0)
    dwout = dwout.reshape(CHIPS, 3, 8, 384).transpose(0, 2, 1, 3).reshape(CHIPS, 8, 1152)
    taps = jnp.zeros((5, INNER), F32)
    taps = lax.dynamic_update_slice_in_dim(taps, dtaps[:5, :OWN], core * OWN, 1)
    taps = jnp.concatenate([taps, dtaps[:5, OWN:]], axis=1)
    gain = lax.dynamic_update_slice_in_dim(jnp.zeros((1, INNER), F32), dgain[:1], core * OWN, 1)
    heads = jnp.zeros((3, HEADS), F32)
    heads = lax.dynamic_update_slice_in_dim(
        heads, dheads[:3, :OWN_HEADS], core * OWN_HEADS, 1
    ).reshape(1, 72)
    rows = [padded(taps.reshape(5, CHIPS, 2, 14), (5, CHIPS, 2, 16))]
    rows.append(padded(dnorm.reshape(1, CHIPS, 2, 6), (1, CHIPS, 2, 16)))
    rows.append(padded(gain.reshape(1, CHIPS, 2, 12), (1, CHIPS, 2, 16)))
    vectors = jnp.concatenate(rows, axis=0).reshape(7, CHIPS, 32)
    vectors = padded(vectors, (8, CHIPS, 32)).transpose(1, 0, 2)
    heads = jnp.broadcast_to(heads.reshape(1, 8, 9), (CHIPS, 8, 9))
    vectors = jnp.concatenate([vectors, heads], axis=2)
    high = lax.reduce_precision(vectors, 8, 7)
    dwin = dwin.reshape(CHIPS, 8, WIN_COLS)
    tile = jnp.concatenate(
        [dwin[:, :, STEP_TILE:VECTORS], high.astype(BF16), (vectors - high).astype(BF16)], axis=2
    )
    return jnp.concatenate(
        [dwin[:, :, :STEP_TILE], padded(tile, (CHIPS, 8, 128)), dwin[:, :, OWN_COLS:], dwout],
        axis=2,
    )


def reduced_gradients(packed):
    arrived = lax.all_to_all(packed, DP, 0, 0, tiled=True)
    return jnp.sum(arrived.astype(F32), axis=0)


def unpacked_gradients(total, core):
    folded = total[:, OWN_COLS:WIN_COLS].reshape(2, 4, FOLD).transpose(1, 0, 2)
    folded = folded.reshape(4, 2 * FOLD)[:, :OWN_COLS]
    win = jnp.concatenate([total[:, :OWN_COLS], folded], axis=0)
    own = part(win, core, 6, 0)
    got = swapped(part(win, 1 - core, 6, 0))
    left = jnp.where(core == 0, own, got)
    right = jnp.where(core == 0, got, own)
    shared = slice(2 * OWN, 2 * OWN + 2 * STATE)
    steps = slice(2 * OWN + 2 * STATE, 2 * OWN + 2 * STATE + OWN_HEADS)
    dwin = jnp.concatenate(
        [
            left[:, :OWN],
            right[:, :OWN],
            left[:, OWN : 2 * OWN],
            right[:, OWN : 2 * OWN],
            left[:, shared] + right[:, shared],
            left[:, steps],
            right[:, steps],
        ],
        axis=1,
    )
    wout = total[:, WIN_COLS:].reshape(8, 3, 384).transpose(1, 0, 2).reshape(24, 384)
    dwout = in_order(core, part(wout, core, 12, 0), swapped(part(wout, 1 - core, 12, 0)), 1)
    vectors = total[:, VECTORS : VECTORS + 41] + total[:, VECTORS + 41 : VECTORS + 82]
    vectors = vectors + swapped(vectors)
    own_vectors = part(vectors[:, :32], core, 16, 1)
    return (
        dwin,
        dwout,
        own_vectors[:4, :14],
        own_vectors[4, :14],
        own_vectors[5, :6],
        own_vectors[6, :12],
        vectors[:, 32:].reshape(3, HEADS),
    )


def mean_square_scale(values):
    return lax.rsqrt(jnp.mean(values * values, axis=1, keepdims=True) + NORM_EPS)


def layers_of(hidden, cotangent, segments, head_values, weights_of, core, send, interpret=False):
    segr = segments
    segc = segments.reshape(TOKENS, 1)
    heads_all = padded(part(head_values, core, OWN_HEADS, 2), (LAYERS, 8, 128))
    current = hidden.astype(F32)
    saved = []
    for layer in range(LAYERS):
        win, wout, taps, norm, gain = weights_of(layer)
        heads = heads_all[layer]
        sigma = mean_square_scale(current)
        u = lax.all_gather((current * sigma * norm).astype(BF16), "seq", axis=0, tiled=True)
        zx, y, out, square = forward_mix(
            u, win, wout, segc, segr, taps, heads, gain, interpret=interpret
        )
        square = square + swapped(square)
        rho = lax.rsqrt(square[:, :1] / INNER + NORM_EPS)
        branch = over_positions(out, core)
        own_rho = part(rho, core, HALF, 0)
        saved.append((current, sigma, u, zx, y, rho, own_rho, branch))
        current = current + own_rho * branch
    upstream = cotangent.astype(F32)
    sent = [None] * LAYERS
    for layer in reversed(range(LAYERS)):
        win, wout, taps, norm, gain = weights_of(layer)
        heads = heads_all[layer]
        before, sigma, u, zx, y, rho, own_rho, branch = saved[layer]
        seed = upstream.astype(BF16)
        mean = own_rho * jnp.sum(seed.astype(F32) * branch, axis=1, keepdims=True) / INNER
        seed = lax.all_gather(seed, "seq", axis=0, tiled=True)
        mean = lax.all_gather(jnp.broadcast_to(mean, (HALF, 128)), "seq", axis=0, tiled=True)
        du, dwin, dwout, dtaps, dheads, dgain = backward_mix(
            seed, mean[:, :1], rho, u, win, wout, zx, y, segc, segr, taps, heads, gain,
            interpret=interpret,
        )
        du = over_positions(du, core)
        dnorm = jnp.sum(du * (before * sigma), axis=0, keepdims=True)
        scaled = du * norm
        upstream = upstream + sigma * (
            scaled
            - before * (sigma * sigma) * jnp.mean(scaled * before, axis=1, keepdims=True)
        )
        sent[layer] = send(dwin, dwout, dtaps, dheads, dnorm, dgain)
    return current.astype(BF16), upstream.astype(BF16), sent


def per_device(
    hidden_in,
    segments,
    projection_in,
    projection_out,
    kernel_weight,
    kernel_bias,
    norm_gain,
    gate_gain,
    head_values,
    cotangent,
):
    core = lax.axis_index("seq")
    blocks = packed_weights(
        projection_in, projection_out, kernel_weight, kernel_bias, norm_gain, gate_gain, core
    )
    first = gathered_weights(blocks[0])
    first, later = lax.optimization_barrier((first, blocks[1]))
    gathered = (first, gathered_weights(later))
    weights = [unpacked_weights(block, core) for block in gathered]

    def send(*gradients):
        return reduced_gradients(packed_gradients(*gradients, core))

    hidden_out, input_gradient, totals = layers_of(
        hidden_in[0], cotangent[0], segments, head_values, lambda layer: weights[layer], core, send
    )
    pieces = [unpacked_gradients(total, core) for total in totals]
    stacked = tuple(jnp.stack([piece[slot] for piece in pieces]) for slot in range(7))
    return (hidden_out[None], input_gradient[None]) + stacked


def solution(mesh):
    torus = Mesh(mesh.devices.reshape(4, 4, 4, mesh.shape["seq"]), DP_SEQ)
    tokens = P(DP, "seq", None)
    weights = (
        P(None, DP_SEQ, None),
        P(None, DP_SEQ, None),
        P(None, None, DP_SEQ),
        P(None, DP_SEQ),
        P(None, DP_SEQ),
        P(None, DP_SEQ),
    )
    return jax.shard_map(
        per_device,
        mesh=torus,
        in_specs=(tokens, P(DP, None)) + weights + (P(), tokens),
        out_specs=(tokens, tokens) + weights + (P(),),
        check_vma=False,
    )
```

```python
import functools

import jax
import jax.numpy as jnp
from jax import lax
from jax.experimental import pallas as pl
from jax.experimental.pallas import tpu as pltpu
from jax.sharding import Mesh
from jax.sharding import PartitionSpec as P

HEADS = 24
HEAD_DIM = 64
STATE = 128
INNER = 1536
CONV_CH = 1792
WIDTH = 768
TOKENS = 512
CHIPS = 64
HALF = 256
OWN_HEADS = 12
OWN = OWN_HEADS * HEAD_DIM
OWN_CONV = OWN + 2 * STATE
REST = OWN_CONV + 128
GATE_FOLD = OWN // 2
REST_FOLD = 640
GATE_COLS = OWN + GATE_FOLD
REST_COLS = REST + REST_FOLD
WIN_COLS = GATE_COLS + REST_COLS
OUT_COLS = 3 * (WIDTH // 2)
LAYER_COLS = WIN_COLS + OUT_COLS
VECTORS = OWN_HEADS
REMAINDERS = 64
VECTOR_COLS = 40
NORM_EPS = 1e-05
NEGATIVE = -1e30
F32 = jnp.float32
BF16 = jnp.bfloat16
HIGHEST = lax.Precision.HIGHEST


def dot(a, b, dims=((1,), (0,)), precision=None):
    return lax.dot_general(a, b, (dims, ((), ())), precision=precision, preferred_element_type=F32)


def dot_nt(a, b, precision=None):
    return dot(a, b, ((1,), (1,)), precision)


def dot_tn(a, b, precision=None):
    return dot(a, b, ((0,), (0,)), precision)


def iota(shape, dim):
    return lax.broadcasted_iota(jnp.int32, shape, dim)


def padded_orders():
    column = iota((WIDTH, 512), 1)
    row = iota((WIDTH, 512), 0)
    start = 12 * (column >> 3)
    place = column & 7
    features = (
        start + place,
        jnp.where(place < 4, start + place + 8, -1),
        jnp.where(place < 4, -1, start + place + 4),
    )
    return [jnp.where(feature == row, 1.0, 0.0).astype(BF16) for feature in features]


def head_spread():
    return jnp.where(iota((128, OWN), 0) == (iota((128, OWN), 1) >> 6), 1.0, 0.0).astype(F32)


def softplus(v):
    return jnp.maximum(v, 0.0) + jnp.log1p(jnp.exp(-jnp.abs(v)))


def tap_masks(segment_column):
    position = iota((TOKENS, 1), 0)
    wide = jnp.broadcast_to(segment_column, (TOKENS, 128))
    masks = [None]
    for back in range(1, 4):
        before = pltpu.roll(wide, back, 0)[:, :1]
        same = (before == segment_column) & (position >= back)
        masks.append(jnp.where(same, 1.0, 0.0).astype(F32))
    return masks


def convolved(signal, taps, masks):
    total = taps[3:4] * signal
    for back in range(1, 4):
        total = total + taps[3 - back : 4 - back] * (pltpu.roll(signal, back, 0) * masks[back])
    return total + taps[4:5]


def steps_of(raw, heads):
    shifted = raw + heads[0:1]
    step = softplus(shifted)
    log_decay = -step * jnp.exp(heads[1:2])
    lower = jnp.where(iota((TOKENS, TOKENS), 0) >= iota((TOKENS, TOKENS), 1), 1.0, 0.0).astype(F32)
    return shifted, step, dot(lower, log_decay, precision=HIGHEST)


def lane_masks():
    low = iota((1, 128), 1) < HEAD_DIM
    return (jnp.where(low, 1.0, 0.0).astype(BF16), jnp.where(low, 0.0, 1.0).astype(BF16))


def reordered(scaled):
    return [dot(scaled, order).astype(BF16) for order in padded_orders()]


def projected(parts, full, folded, fold):
    u_full, u_low, u_high = parts
    rest = full.shape[1] - fold
    left = dot(u_full, full[:, :fold]) + dot(u_low, folded)
    right = dot(u_full, full[:, fold:]) + dot(u_high, folded[:, :rest])
    return left, right


def weight_gradient(parts, grad, fold):
    u_full, u_low, u_high = parts
    rest = grad.shape[1] - fold
    folded = dot_tn(u_low, grad[:, :fold])
    high = dot_tn(u_high, grad[:, fold:])
    if rest < fold:
        high = jnp.concatenate([high, jnp.zeros((high.shape[0], fold - rest), F32)], axis=1)
    return dot_tn(u_full, grad), folded + high


def input_gradients(grad, full, folded, fold):
    rest = grad.shape[1] - fold
    return (
        dot_nt(grad, full),
        dot_nt(grad[:, :fold], folded),
        dot_nt(grad[:, fold:], folded[:, :rest]),
    )


def column_picks(maps, kind, columns):
    chips = maps[2 * kind : 2 * kind + 1, :columns]
    places = maps[2 * kind + 1 : 2 * kind + 2, :columns]
    rows = iota((512, 1), 0) >> 3
    keep = jnp.where(rows == chips, 1.0, 0.0).astype(F32)
    pick = jnp.where(iota((128, columns), 0) == places + VECTORS, 1.0, 0.0).astype(F32)
    return keep, pick


def vectors_from(tile, maps, kind, columns):
    keep, pick = column_picks(maps, kind, columns)
    spread = dot(tile, pick.astype(BF16)) * keep
    return jnp.sum(spread.reshape(CHIPS, 8, columns), axis=0)


def vectors_into(values, maps, kind):
    columns = values.shape[1]
    keep, pick = column_picks(maps, kind, columns)
    tiled = jnp.broadcast_to(values[None], (CHIPS, 8, columns)).reshape(512, columns)
    return dot_nt(tiled * keep, pick, precision=HIGHEST)


def only_row(values, row):
    return jnp.where(iota((8, 1), 0) == row, values, 0.0)


def fetched(source, target, semaphore, layer, columns):
    start = layer * LAYER_COLS
    return pltpu.make_async_copy(source.at[:, start : start + columns], target, semaphore)


def forward_kernel(
    layer, xhat_ref, weights_ref, wout_ref, segc_ref, segr_ref, heads_ref, maps_ref,
    gate_ref, rest_ref, y_ref, out_ref, square_ref, taps_ref, norm_ref, gain_ref,
    win_ref, dtx_ref, affinity_ref, bias_ref, semaphore,
):
    copy = fetched(weights_ref, win_ref, semaphore, layer, WIN_COLS)
    copy.start()
    segc = segc_ref[...]
    masks = tap_masks(segc)
    allowed = (iota((TOKENS, TOKENS), 0) >= iota((TOKENS, TOKENS), 1)) & (segc == segr_ref[...])
    bias_ref[...] = jnp.where(allowed, 0.0, NEGATIVE).astype(F32)
    copy.wait()
    maps = maps_ref[...]
    tile = win_ref[:, GATE_COLS + OWN_CONV : GATE_COLS + REST]
    taps = vectors_from(tile, maps, 0, OWN_CONV)
    norm = vectors_from(tile, maps, 1, WIDTH)[5:6]
    gain = vectors_from(tile, maps, 2, OWN)[6:7]
    taps_ref[...] = taps
    norm_ref[...] = jnp.broadcast_to(norm, norm_ref.shape)
    gain_ref[...] = jnp.broadcast_to(gain, gain_ref.shape)
    parts = reordered((xhat_ref[...].astype(F32) * norm).astype(BF16))
    rest_ref[:, :REST_FOLD], rest_ref[:, REST_FOLD:] = projected(
        parts, win_ref[:, GATE_COLS : GATE_COLS + REST], win_ref[:, GATE_COLS + REST :], REST_FOLD
    )
    gate_ref[:, :GATE_FOLD], gate_ref[:, GATE_FOLD:] = projected(
        parts, win_ref[:, :OWN], win_ref[:, OWN:GATE_COLS], GATE_FOLD
    )
    heads = heads_ref[...]
    before = convolved(rest_ref[:, :OWN_CONV], taps, masks)
    active = before * jax.nn.sigmoid(before)
    inputs = active[:, :OWN]
    writers = active[:, OWN : OWN + STATE].astype(BF16)
    readers = active[:, OWN + STATE :].astype(BF16)
    _, step, cumul = steps_of(rest_ref[:, OWN_CONV:], heads)
    cumul_rows = cumul.T
    spread = head_spread()
    dtx_ref[...] = (dot(step, spread, precision=HIGHEST) * inputs).astype(BF16)
    y_ref[...] = dot(heads, spread, precision=HIGHEST)[2:3] * inputs
    affinity_ref[...] = dot_nt(readers, writers)
    halves = lane_masks()
    for pair in range(OWN_HEADS // 2):
        lanes = slice(128 * pair, 128 * pair + 128)
        pair_inputs = dtx_ref[:, lanes]
        for block in range(2):
            rows = slice(HALF * block, HALF * block + HALF)
            reach = HALF * (block + 1)
            total = y_ref[rows, lanes]
            for member in range(2):
                head = 2 * pair + member
                decay = jnp.exp(
                    cumul[rows, head : head + 1]
                    - cumul_rows[head : head + 1, :reach]
                    + bias_ref[rows, :reach]
                )
                mixing = (decay * affinity_ref[rows, :reach]).astype(BF16)
                total = total + dot(mixing, pair_inputs[:reach] * halves[member])
            y_ref[rows, lanes] = total
    gate = gate_ref[...]
    gated = y_ref[...] * (gate * jax.nn.sigmoid(gate))
    out_ref[...] = dot((gated * gain).astype(BF16), wout_ref[...]).astype(out_ref.dtype)
    square_ref[...] = jnp.broadcast_to(
        jnp.sum(gated * gated, axis=1, keepdims=True), square_ref.shape
    )


def vmem(count):
    return [pl.BlockSpec(memory_space=pltpu.VMEM)] * count


def forward_mix(layer, xhat, weights, wout, segc, segr, heads, maps, interpret=False):
    return pl.pallas_call(
        functools.partial(forward_kernel, layer),
        in_specs=vmem(1) + [pl.BlockSpec(memory_space=pl.ANY)] + vmem(5),
        out_shape=(
            jax.ShapeDtypeStruct((TOKENS, OWN), F32),
            jax.ShapeDtypeStruct((TOKENS, REST), F32),
            jax.ShapeDtypeStruct((TOKENS, OWN), F32),
            jax.ShapeDtypeStruct((TOKENS, WIDTH), BF16),
            jax.ShapeDtypeStruct((TOKENS, 128), F32),
            jax.ShapeDtypeStruct((8, OWN_CONV), F32),
            jax.ShapeDtypeStruct((8, WIDTH), F32),
            jax.ShapeDtypeStruct((8, OWN), F32),
        ),
        scratch_shapes=[
            pltpu.VMEM((512, WIN_COLS), BF16),
            pltpu.VMEM((TOKENS, OWN), BF16),
            pltpu.VMEM((TOKENS, TOKENS), F32),
            pltpu.VMEM((TOKENS, TOKENS), F32),
            pltpu.SemaphoreType.DMA,
        ],
        compiler_params=pltpu.CompilerParams(vmem_limit_bytes=58 * 2**20),
        interpret=interpret,
    )(xhat, weights, wout, segc, segr, heads, maps)


def gate_kernel(
    seed_ref, rho_ref, xhat_ref, norm_ref, wout_ref, gate_ref, y_ref, gain_ref,
    dgate_ref, dy_ref, dwin_ref, dwout_ref, dgain_ref,
):
    seed = seed_ref[:, :WIDTH]
    mean = seed_ref[:, WIDTH : WIDTH + 128].astype(F32)
    mean = mean[:, 0:1] + mean[:, 1:2]
    gain = gain_ref[0:1]
    rho = rho_ref[...]
    gate = gate_ref[...]
    y = y_ref[...]
    open_gate = jax.nn.sigmoid(gate)
    passed = gate * open_gate
    scaled = y * passed * rho
    dyn = dot_nt(seed, wout_ref[...])
    dwout_ref[...] = dot_tn((scaled * gain).astype(BF16), seed).astype(BF16)
    dgain_ref[...] = jnp.broadcast_to(jnp.sum(dyn * scaled, axis=0, keepdims=True), dgain_ref.shape)
    dgated = rho * (dyn * gain - scaled * mean)
    dy_ref[...] = dgated * passed
    dgate = (dgated * y * (open_gate * (1.0 + gate * (1.0 - open_gate)))).astype(BF16)
    dgate_ref[...] = dgate
    parts = reordered((xhat_ref[...].astype(F32) * norm_ref[0:1]).astype(BF16))
    full, folded = weight_gradient(parts, dgate, GATE_FOLD)
    dwin_ref[:, :OWN] = full.astype(BF16)
    dwin_ref[:, OWN:] = folded.astype(BF16)


def gate_back(seed, rho, xhat, norm, wout, gate, y, gain, interpret=False):
    return pl.pallas_call(
        gate_kernel,
        out_shape=(
            jax.ShapeDtypeStruct((TOKENS, OWN), BF16),
            jax.ShapeDtypeStruct((TOKENS, OWN), F32),
            jax.ShapeDtypeStruct((512, GATE_COLS), BF16),
            jax.ShapeDtypeStruct((OWN, WIDTH), BF16),
            jax.ShapeDtypeStruct((8, OWN), F32),
        ),
        compiler_params=pltpu.CompilerParams(vmem_limit_bytes=58 * 2**20),
        interpret=interpret,
    )(seed, rho, xhat, norm, wout, gate, y, gain)


def backward_kernel(
    layer, dgate_ref, dy_ref, xhat_ref, norm_ref, weights_ref, rest_ref,
    segc_ref, segr_ref, taps_ref, heads_ref, dgain_ref, maps_ref,
    dscaled_ref, dwin_ref,
    win_ref, dtx_ref, affinity_ref, bias_ref, daffinity_ref, drest_ref, dact_ref, rise_ref,
    direct_ref, dtaps_ref, semaphore,
):
    copy = fetched(weights_ref, win_ref, semaphore, layer, WIN_COLS)
    copy.start()
    taps = taps_ref[...]
    heads = heads_ref[...]
    segc = segc_ref[...]
    masks = tap_masks(segc)
    signal = rest_ref[:, :OWN_CONV]
    before = convolved(signal, taps, masks)
    open_act = jax.nn.sigmoid(before)
    active = before * open_act
    inputs = active[:, :OWN]
    writers = active[:, OWN : OWN + STATE].astype(BF16)
    readers = active[:, OWN + STATE :].astype(BF16)
    shifted, step, cumul = steps_of(rest_ref[:, OWN_CONV:], heads)
    cumul_rows = cumul.T
    spread = head_spread()
    step_wide = dot(step, spread, precision=HIGHEST)
    skip_wide = dot(heads, spread, precision=HIGHEST)[2:3]
    dtx_ref[...] = (step_wide * inputs).astype(BF16)
    allowed = (iota((TOKENS, TOKENS), 0) <= iota((TOKENS, TOKENS), 1)) & (segc == segr_ref[...])
    bias_ref[...] = jnp.where(allowed, 0.0, NEGATIVE).astype(F32)
    affinity_ref[...] = dot_nt(writers, readers)
    daffinity_ref[...] = jnp.zeros_like(daffinity_ref)
    rise_ref[...] = jnp.zeros_like(rise_ref)
    halves = lane_masks()
    head_lane = iota((1, 128), 1)
    fall_blocks = [jnp.zeros((HALF, 128), F32), jnp.zeros((HALF, 128), F32)]
    for pair in range(OWN_HEADS // 2):
        lanes = slice(128 * pair, 128 * pair + 128)
        pair_inputs = dtx_ref[:, lanes]
        pair_dy = dy_ref[:, lanes].astype(BF16)
        member_dy = [pair_dy * half for half in halves]
        for block in range(2):
            rows = slice(HALF * block, HALF * block + HALF)
            start = HALF * block
            dinput = jnp.zeros((HALF, 128), F32)
            for member in range(2):
                head = 2 * pair + member
                decay = jnp.exp(
                    cumul_rows[head : head + 1, start:]
                    - cumul[rows, head : head + 1]
                    + bias_ref[rows, start:]
                )
                dmixing = dot_nt(pair_inputs[rows], member_dy[member][start:]) * decay
                daffinity_ref[rows, start:] += dmixing
                affinity = affinity_ref[rows, start:]
                dinput = dinput + dot((decay * affinity).astype(BF16), member_dy[member][start:])
                dspread = dmixing * affinity
                fall = jnp.sum(dspread, axis=1, keepdims=True)
                fall_blocks[block] = fall_blocks[block] + jnp.where(head_lane == head, fall, 0.0)
                rise_ref[head : head + 1, start:] += jnp.sum(dspread, axis=0, keepdims=True)
            direct_ref[rows, lanes] = dinput
    dinputs = direct_ref[...]
    dy = dy_ref[...]
    dact_ref[:, :OWN] = step_wide * dinputs + skip_wide * dy
    daffinity = daffinity_ref[...].astype(BF16)
    dact_ref[:, OWN : OWN + STATE] = dot(daffinity, readers)
    dact_ref[:, OWN + STATE :] = dot_tn(daffinity, writers)
    dstep = dot_nt(dinputs * inputs, spread, precision=HIGHEST)
    skip_sum = jnp.broadcast_to(jnp.sum(dy * inputs, axis=0, keepdims=True), (8, OWN))
    dskip = dot_nt(skip_sum, spread, precision=HIGHEST)[0:1]
    dcumul = rise_ref[...].T - jnp.concatenate(fall_blocks, axis=0)
    upper = jnp.where(iota((TOKENS, TOKENS), 0) <= iota((TOKENS, TOKENS), 1), 1.0, 0.0).astype(F32)
    dlog = dot(upper, dcumul, precision=HIGHEST)
    rate = jnp.exp(heads[1:2])
    draw = (dstep - dlog * rate) * jax.nn.sigmoid(shifted)
    head_rows = (
        jnp.sum(draw, axis=0, keepdims=True),
        jnp.sum(-dlog * step * rate, axis=0, keepdims=True),
        dskip,
    )
    drest_ref[:, OWN_CONV:] = draw.astype(BF16)

    dconv = dact_ref[...] * (open_act * (1.0 + before * (1.0 - open_act)))
    dtaps_ref[...] = jnp.zeros_like(dtaps_ref)
    dtaps_ref[4:5] = jnp.sum(dconv, axis=0, keepdims=True)
    dtaps_ref[3:4] = jnp.sum(dconv * signal, axis=0, keepdims=True)
    dsignal = taps[3:4] * dconv
    for back in range(1, 4):
        masked = dconv * masks[back]
        dtaps_ref[3 - back : 4 - back] = jnp.sum(
            masked * pltpu.roll(signal, back, 0), axis=0, keepdims=True
        )
        dsignal = dsignal + taps[3 - back : 4 - back] * pltpu.roll(masked, TOKENS - back, 0)
    drest_ref[:, :OWN_CONV] = dsignal.astype(BF16)

    norm = norm_ref[0:1]
    xhat = xhat_ref[...].astype(F32)
    orders = padded_orders()
    u = (xhat * norm).astype(BF16)
    parts = [dot(u, order).astype(BF16) for order in orders]
    drest = drest_ref[...]
    copy.wait()
    from_rest = input_gradients(
        drest, win_ref[:, GATE_COLS : GATE_COLS + REST], win_ref[:, GATE_COLS + REST :], REST_FOLD
    )
    from_gate = input_gradients(
        dgate_ref[...], win_ref[:, :OWN], win_ref[:, OWN:GATE_COLS], GATE_FOLD
    )
    du = jnp.zeros((TOKENS, WIDTH), F32)
    for one, other, order in zip(from_rest, from_gate, orders):
        du = du + dot_nt((one + other).astype(BF16), order)
    dscaled_ref[...] = (du * norm).astype(BF16)

    full, folded = weight_gradient(parts, drest, REST_FOLD)
    dwin_ref[:, :OWN_CONV] = full[:, :OWN_CONV].astype(BF16)
    dwin_ref[:, REST:] = folded.astype(BF16)
    maps = maps_ref[...]
    dnorm = jnp.sum(du * xhat, axis=0, keepdims=True)
    vectors = (
        vectors_into(dtaps_ref[...], maps, 0)
        + vectors_into(only_row(dnorm, 5), maps, 1)
        + vectors_into(only_row(dgain_ref[...], 6), maps, 2)
    )
    last_row = jnp.zeros((8, 128), F32)
    for place, row in enumerate(head_rows):
        shift = VECTORS + OWN_HEADS * place
        last_row = last_row + pltpu.roll(jnp.broadcast_to(row, (8, 128)), shift, 1)
    vectors = vectors + jnp.where((iota((512, 1), 0) & 7) == 7, last_row[0:1], 0.0)
    high = vectors.astype(BF16).astype(F32)
    low = pltpu.roll(vectors - high, REMAINDERS - VECTORS, 1)
    dwin_ref[:, OWN_CONV:REST] = (full[:, OWN_CONV:] + high + low).astype(BF16)


def backward_mix(
    layer, dgate, dy, xhat, norm, weights, rest, segc, segr, taps, heads, dgain, maps,
    interpret=False,
):
    square = (TOKENS, TOKENS)
    return pl.pallas_call(
        functools.partial(backward_kernel, layer),
        in_specs=vmem(4) + [pl.BlockSpec(memory_space=pl.ANY)] + vmem(7),
        out_shape=(
            jax.ShapeDtypeStruct((TOKENS, WIDTH), BF16),
            jax.ShapeDtypeStruct((512, REST_COLS), BF16),
        ),
        scratch_shapes=[
            pltpu.VMEM((512, WIN_COLS), BF16),
            pltpu.VMEM((TOKENS, OWN), BF16),
            pltpu.VMEM(square, F32),
            pltpu.VMEM(square, F32),
            pltpu.VMEM(square, F32),
            pltpu.VMEM((TOKENS, REST), BF16),
            pltpu.VMEM((TOKENS, OWN_CONV), F32),
            pltpu.VMEM((128, TOKENS), F32),
            pltpu.VMEM((TOKENS, OWN), F32),
            pltpu.VMEM((8, OWN_CONV), F32),
            pltpu.SemaphoreType.DMA,
        ],
        compiler_params=pltpu.CompilerParams(vmem_limit_bytes=58 * 2**20),
        interpret=interpret,
    )(dgate, dy, xhat, norm, weights, rest, segc, segr, taps, heads, dgain, maps)


DP = ("dp_0", "dp_1", "dp_2")
DP_SEQ = DP + ("seq",)
LAYERS = 2


def swapped(v):
    return lax.ppermute(v, "seq", [(0, 1), (1, 0)])


def part(v, index, size, axis):
    return lax.dynamic_slice_in_dim(v, index * size, size, axis)


def in_order(core, own, other, axis):
    first = jnp.where(core == 0, own, other)
    second = jnp.where(core == 0, other, own)
    return jnp.concatenate([first, second], axis=axis)


def padded(v, sizes):
    return jnp.pad(v, [(0, size - now) for now, size in zip(v.shape, sizes)])


def folded_rows(rows, fold):
    tail = padded(rows[:, 8:], (LAYERS, 4, 2 * fold)).reshape(LAYERS, 4, 2, fold)
    return tail.transpose(0, 2, 1, 3).reshape(LAYERS, 8, fold)


def packed_weights(win, wout, kernel_weight, kernel_bias, norm_gain, gate_gain, core):
    win = in_order(core, win, swapped(win), 1)
    wout = in_order(core, wout, swapped(wout), 1)
    rows = [kernel_weight, kernel_bias[:, None]]
    rows += [padded(vector[:, None], (LAYERS, 1, 14)) for vector in (norm_gain, gate_gain)]
    vectors = padded(jnp.concatenate(rows, axis=1), (LAYERS, 8, 14))
    others = swapped(vectors)
    first = jnp.where(core == 0, vectors, others)
    second = jnp.where(core == 0, others, vectors)
    joined = []
    for start, stop, size in ((0, 5, 14), (5, 6, 6), (6, 8, 12)):
        both = [first[:, start:stop, :size], second[:, start:stop, :size]]
        both = jnp.concatenate(both, axis=2)
        joined.append(padded(both, both.shape[:2] + (128 - OWN_HEADS,)))
    vectors = jnp.concatenate(joined, axis=1)
    gate = part(win[:, :, :INNER], core, OWN, 2)
    steps = part(win[:, :, INNER + CONV_CH :], core, OWN_HEADS, 2)
    tail = padded(steps[:, 8:], (LAYERS, 4, 128))
    tile = jnp.concatenate([steps[:, :8], vectors], axis=2)
    rest = jnp.concatenate(
        [
            part(win[:, :, INNER : 2 * INNER], core, OWN, 2),
            win[:, :, 2 * INNER : INNER + CONV_CH],
            jnp.concatenate([tile, tail], axis=1),
        ],
        axis=2,
    )
    wout = part(wout, core, WIDTH // 2, 2)
    wout = wout.reshape(LAYERS, 3, 8, WIDTH // 2).transpose(0, 2, 1, 3)
    block = jnp.concatenate(
        [
            gate[:, :8],
            folded_rows(gate, GATE_FOLD),
            rest[:, :8],
            folded_rows(rest, REST_FOLD),
            wout.reshape(LAYERS, 8, OUT_COLS),
        ],
        axis=2,
    )
    return block.transpose(1, 0, 2).reshape(8, LAYERS * LAYER_COLS)


def output_weights(gathered, core):
    wout = gathered.reshape(CHIPS, 8, LAYERS, LAYER_COLS)[:, :, :, WIN_COLS:]
    wout = wout.reshape(CHIPS, 8, LAYERS, 3, WIDTH // 2).transpose(2, 0, 3, 1, 4)
    wout = wout.reshape(LAYERS, INNER, WIDTH // 2)
    return in_order(core, part(wout, core, OWN, 1), swapped(part(wout, 1 - core, OWN, 1)), 2)


def vector_maps(core):
    column = jnp.arange(OWN_CONV)
    channel = jnp.where(column < OWN, column + core * OWN, column - OWN + INNER)
    feature = column + core * OWN
    rows = [channel // 28, channel % 28, column // 12, column % 12, feature // 24, feature % 24]
    return padded(jnp.stack(rows).astype(jnp.int32), (8, OWN_CONV))


def over_positions(partial_sum, core):
    own = part(partial_sum, core, HALF, 0).astype(F32)
    return own + swapped(part(partial_sum, 1 - core, HALF, 0)).astype(F32)


def reduced(packed):
    arrived = lax.all_to_all(packed, DP, 0, 0, tiled=True)
    return jnp.sum(arrived.astype(F32), axis=0)


def reduced_output(dwout, core):
    half = WIDTH // 2
    dwout = in_order(core, part(dwout, core, half, 1), swapped(part(dwout, 1 - core, half, 1)), 0)
    dwout = dwout.reshape(CHIPS, 3, 8, half).transpose(0, 2, 1, 3)
    return reduced(dwout.reshape(CHIPS, 8, OUT_COLS))


def reduced_input(dwin):
    return reduced(dwin.reshape(CHIPS, 8, dwin.shape[1]))


def unfolded(total, columns, fold):
    tail = total[:, columns:].reshape(2, 4, fold).transpose(1, 0, 2).reshape(4, 2 * fold)
    return jnp.concatenate([total[:, :columns], tail[:, :columns]], axis=0)


def unpacked_gradients(gate_total, out_total, rest_total, core):
    win = jnp.concatenate(
        [unfolded(gate_total, OWN, GATE_FOLD), unfolded(rest_total, REST, REST_FOLD)], axis=1
    )
    own = part(win, core, 6, 0)
    got = swapped(part(win, 1 - core, 6, 0))
    left = jnp.where(core == 0, own, got)
    right = jnp.where(core == 0, got, own)
    shared = slice(2 * OWN, 2 * OWN + 2 * STATE)
    steps = slice(2 * OWN + 2 * STATE, 2 * OWN + 2 * STATE + OWN_HEADS)
    dwin = jnp.concatenate(
        [
            left[:, :OWN],
            right[:, :OWN],
            left[:, OWN : 2 * OWN],
            right[:, OWN : 2 * OWN],
            left[:, shared] + right[:, shared],
            left[:, steps],
            right[:, steps],
        ],
        axis=1,
    )
    half = WIDTH // 2
    wout = out_total.reshape(8, 3, half).transpose(1, 0, 2).reshape(24, half)
    dwout = in_order(core, part(wout, core, 12, 0), swapped(part(wout, 1 - core, 12, 0)), 1)
    tile = rest_total[:, OWN_CONV:REST]
    vectors = tile[:, VECTORS : VECTORS + VECTOR_COLS] + tile[:, REMAINDERS : REMAINDERS + VECTOR_COLS]
    others = swapped(vectors)
    heads = in_order(core, vectors[7, :36].reshape(3, 12), others[7, :36].reshape(3, 12), 1)
    vectors = vectors + others
    taps = part(vectors[:5, :28], core, 14, 1)
    return (
        dwin,
        dwout,
        taps[:4],
        taps[4],
        part(vectors[5, :12], core, 6, 0),
        part(vectors[6, :24], core, 12, 0),
        heads,
    )


def mean_square_scale(values):
    return lax.rsqrt(jnp.mean(values * values, axis=1, keepdims=True) + NORM_EPS)


def layers_of(
    hidden, cotangent, segments, head_values, weights, wouts, core, send_gate, send_rest,
    interpret=False,
):
    segr = segments
    segc = segments.reshape(TOKENS, 1)
    heads_all = padded(part(head_values, core, OWN_HEADS, 2), (LAYERS, 8, 128))
    maps = vector_maps(core)
    current = hidden.astype(F32)
    saved = []
    for layer in range(LAYERS):
        sigma = mean_square_scale(current)
        xhat = lax.all_gather((current * sigma).astype(BF16), "seq", axis=0, tiled=True)
        gate, rest, y, out, square, taps, norm, gain = forward_mix(
            layer, xhat, weights, wouts[layer], segc, segr, heads_all[layer], maps,
            interpret=interpret,
        )
        square = square + swapped(square)
        rho = lax.rsqrt(square[:, :1] / INNER + NORM_EPS)
        branch = over_positions(out, core)
        own_rho = part(rho, core, HALF, 0)
        saved.append((current, sigma, xhat, gate, rest, y, rho, own_rho, branch, taps, norm, gain))
        current = current + own_rho * branch
    upstream = cotangent.astype(F32)
    sent = [None] * LAYERS
    for layer in reversed(range(LAYERS)):
        before, sigma, xhat, gate, rest, y, rho, own_rho, branch, taps, norm, gain = saved[layer]
        seed = upstream.astype(BF16)
        mean = own_rho * jnp.sum(seed.astype(F32) * branch, axis=1, keepdims=True) / INNER
        high = lax.reduce_precision(mean, 8, 7)
        means = jnp.concatenate([high, mean - high], axis=1).astype(BF16)
        seed = jnp.concatenate([seed, padded(means, (HALF, 128))], axis=1)
        seed = lax.all_gather(seed, "seq", axis=0, tiled=True)
        dgate, dy, dwin_gate, dwout, dgain = gate_back(
            seed, rho, xhat, norm, wouts[layer], gate, y, gain, interpret=interpret
        )
        early = send_gate(dwin_gate, dwout)
        dscaled, dwin_rest = backward_mix(
            layer, dgate, dy, xhat, norm, weights, rest, segc, segr, taps, heads_all[layer],
            dgain, maps, interpret=interpret,
        )
        sent[layer] = early + (send_rest(dwin_rest),)
        scaled = over_positions(dscaled, core)
        upstream = upstream + sigma * (
            scaled
            - before * (sigma * sigma) * jnp.mean(scaled * before, axis=1, keepdims=True)
        )
    return current.astype(BF16), upstream.astype(BF16), sent


def per_device(
    hidden_in,
    segments,
    projection_in,
    projection_out,
    kernel_weight,
    kernel_bias,
    norm_gain,
    gate_gain,
    head_values,
    cotangent,
):
    core = lax.axis_index("seq")
    block = packed_weights(
        projection_in, projection_out, kernel_weight, kernel_bias, norm_gain, gate_gain, core
    )
    weights = lax.all_gather(block, DP, axis=0, tiled=True)
    wouts = output_weights(weights, core)

    def send_gate(dwin, dwout):
        return reduced_input(dwin), reduced_output(dwout, core)

    hidden_out, input_gradient, totals = layers_of(
        hidden_in[0], cotangent[0], segments, head_values, weights, wouts, core, send_gate,
        reduced_input,
    )
    pieces = [unpacked_gradients(*total, core) for total in totals]
    stacked = tuple(jnp.stack([piece[slot] for piece in pieces]) for slot in range(7))
    return (hidden_out[None], input_gradient[None]) + stacked


def solution(mesh):
    torus = Mesh(mesh.devices.reshape(4, 4, 4, mesh.shape["seq"]), DP_SEQ)
    tokens = P(DP, "seq", None)
    weights = (
        P(None, DP_SEQ, None),
        P(None, DP_SEQ, None),
        P(None, None, DP_SEQ),
        P(None, DP_SEQ),
        P(None, DP_SEQ),
        P(None, DP_SEQ),
    )
    return jax.shard_map(
        per_device,
        mesh=torus,
        in_specs=(tokens, P(DP, None)) + weights + (P(), tokens),
        out_specs=(tokens, tokens) + weights + (P(),),
        check_vma=False,
    )
```

```python
import functools

import jax
import jax.numpy as jnp
from jax import lax
from jax.experimental import pallas as pl
from jax.experimental.pallas import tpu as pltpu
from jax.sharding import Mesh
from jax.sharding import PartitionSpec as P

HEADS = 24
HEAD_DIM = 64
STATE = 128
INNER = 1536
CONV_CH = 1792
WIDTH = 768
TOKENS = 512
CHIPS = 64
HALF = 256
OWN_HEADS = 12
OWN = OWN_HEADS * HEAD_DIM
OWN_CONV = OWN + 2 * STATE
REST = OWN_CONV + 128
GATE_FOLD = OWN // 2
REST_FOLD = 640
GATE_COLS = OWN + GATE_FOLD
REST_COLS = REST + REST_FOLD
WIN_COLS = GATE_COLS + REST_COLS
OUT_COLS = 3 * (WIDTH // 2)
LAYER_COLS = WIN_COLS + OUT_COLS
VECTORS = OWN_HEADS
REMAINDERS = 64
VECTOR_COLS = 40
NORM_EPS = 1e-05
NEGATIVE = -1e30
F32 = jnp.float32
BF16 = jnp.bfloat16
HIGHEST = lax.Precision.HIGHEST


def dot(a, b, dims=((1,), (0,)), precision=None):
    return lax.dot_general(a, b, (dims, ((), ())), precision=precision, preferred_element_type=F32)


def dot_nt(a, b, precision=None):
    return dot(a, b, ((1,), (1,)), precision)


def dot_tn(a, b, precision=None):
    return dot(a, b, ((0,), (0,)), precision)


def iota(shape, dim):
    return lax.broadcasted_iota(jnp.int32, shape, dim)


def padded_orders():
    column = iota((WIDTH, 512), 1)
    row = iota((WIDTH, 512), 0)
    start = 12 * (column >> 3)
    place = column & 7
    features = (
        start + place,
        jnp.where(place < 4, start + place + 8, -1),
        jnp.where(place < 4, -1, start + place + 4),
    )
    return [jnp.where(feature == row, 1.0, 0.0).astype(BF16) for feature in features]


def head_spread():
    return jnp.where(iota((128, OWN), 0) == (iota((128, OWN), 1) >> 6), 1.0, 0.0).astype(F32)


def softplus(v):
    return jnp.maximum(v, 0.0) + jnp.log1p(jnp.exp(-jnp.abs(v)))


def tap_masks(segment_column):
    position = iota((TOKENS, 1), 0)
    wide = jnp.broadcast_to(segment_column, (TOKENS, 128))
    masks = [None]
    for back in range(1, 4):
        before = pltpu.roll(wide, back, 0)[:, :1]
        same = (before == segment_column) & (position >= back)
        masks.append(jnp.where(same, 1.0, 0.0).astype(F32))
    return masks


def convolved(signal, taps, masks):
    total = taps[3:4] * signal
    for back in range(1, 4):
        total = total + taps[3 - back : 4 - back] * (pltpu.roll(signal, back, 0) * masks[back])
    return total + taps[4:5]


def steps_of(raw, heads):
    shifted = raw + heads[0:1]
    step = softplus(shifted)
    log_decay = -step * jnp.exp(heads[1:2])
    lower = jnp.where(iota((TOKENS, TOKENS), 0) >= iota((TOKENS, TOKENS), 1), 1.0, 0.0).astype(F32)
    return shifted, step, dot(lower, log_decay, precision=HIGHEST)


def lane_masks():
    low = iota((1, 128), 1) < HEAD_DIM
    return (jnp.where(low, 1.0, 0.0).astype(BF16), jnp.where(low, 0.0, 1.0).astype(BF16))


def reordered(scaled):
    return [dot(scaled, order).astype(BF16) for order in padded_orders()]


def projected(parts, full, folded, fold):
    u_full, u_low, u_high = parts
    rest = full.shape[1] - fold
    left = dot(u_full, full[:, :fold]) + dot(u_low, folded)
    right = dot(u_full, full[:, fold:]) + dot(u_high, folded[:, :rest])
    return left, right


def weight_gradient(parts, grad, fold):
    u_full, u_low, u_high = parts
    rest = grad.shape[1] - fold
    folded = dot_tn(u_low, grad[:, :fold])
    high = dot_tn(u_high, grad[:, fold:])
    if rest < fold:
        high = jnp.concatenate([high, jnp.zeros((high.shape[0], fold - rest), F32)], axis=1)
    return dot_tn(u_full, grad), folded + high


def input_gradients(grad, full, folded, fold):
    rest = grad.shape[1] - fold
    return (
        dot_nt(grad, full),
        dot_nt(grad[:, :fold], folded),
        dot_nt(grad[:, fold:], folded[:, :rest]),
    )


def column_picks(maps, kind, columns):
    chips = maps[2 * kind : 2 * kind + 1, :columns]
    places = maps[2 * kind + 1 : 2 * kind + 2, :columns]
    rows = iota((512, 1), 0) >> 3
    keep = jnp.where(rows == chips, 1.0, 0.0).astype(F32)
    pick = jnp.where(iota((128, columns), 0) == places + VECTORS, 1.0, 0.0).astype(F32)
    return keep, pick


def vectors_from(tile, maps, kind, columns):
    keep, pick = column_picks(maps, kind, columns)
    spread = dot(tile, pick.astype(BF16)) * keep
    return jnp.sum(spread.reshape(CHIPS, 8, columns), axis=0)


def vectors_into(values, maps, kind):
    columns = values.shape[1]
    keep, pick = column_picks(maps, kind, columns)
    tiled = jnp.broadcast_to(values[None], (CHIPS, 8, columns)).reshape(512, columns)
    return dot_nt(tiled * keep, pick, precision=HIGHEST)


def only_row(values, row):
    return jnp.where(iota((8, 1), 0) == row, values, 0.0)


def fetched(source, target, semaphore, layer, columns):
    start = layer * LAYER_COLS
    return pltpu.make_async_copy(source.at[:, start : start + columns], target, semaphore)


def forward_kernel(
    layer, xhat_ref, weights_ref, wout_ref, segc_ref, segr_ref, heads_ref, maps_ref,
    gate_ref, rest_ref, y_ref, out_ref, square_ref, taps_ref, norm_ref, gain_ref,
    win_ref, dtx_ref, affinity_ref, bias_ref, semaphore,
):
    copy = fetched(weights_ref, win_ref, semaphore, layer, WIN_COLS)
    copy.start()
    segc = segc_ref[...]
    masks = tap_masks(segc)
    allowed = (iota((TOKENS, TOKENS), 0) >= iota((TOKENS, TOKENS), 1)) & (segc == segr_ref[...])
    bias_ref[...] = jnp.where(allowed, 0.0, NEGATIVE).astype(F32)
    copy.wait()
    maps = maps_ref[...]
    tile = win_ref[:, GATE_COLS + OWN_CONV : GATE_COLS + REST]
    taps = vectors_from(tile, maps, 0, OWN_CONV)
    norm = vectors_from(tile, maps, 1, WIDTH)[5:6]
    gain = vectors_from(tile, maps, 2, OWN)[6:7]
    taps_ref[...] = taps
    norm_ref[...] = jnp.broadcast_to(norm, norm_ref.shape)
    gain_ref[...] = jnp.broadcast_to(gain, gain_ref.shape)
    parts = reordered((xhat_ref[...].astype(F32) * norm).astype(BF16))
    rest_ref[:, :REST_FOLD], rest_ref[:, REST_FOLD:] = projected(
        parts, win_ref[:, GATE_COLS : GATE_COLS + REST], win_ref[:, GATE_COLS + REST :], REST_FOLD
    )
    gate_ref[:, :GATE_FOLD], gate_ref[:, GATE_FOLD:] = projected(
        parts, win_ref[:, :OWN], win_ref[:, OWN:GATE_COLS], GATE_FOLD
    )
    heads = heads_ref[...]
    before = convolved(rest_ref[:, :OWN_CONV], taps, masks)
    active = before * jax.nn.sigmoid(before)
    inputs = active[:, :OWN]
    writers = active[:, OWN : OWN + STATE].astype(BF16)
    readers = active[:, OWN + STATE :].astype(BF16)
    _, step, cumul = steps_of(rest_ref[:, OWN_CONV:], heads)
    cumul_rows = cumul.T
    spread = head_spread()
    dtx_ref[...] = (dot(step, spread, precision=HIGHEST) * inputs).astype(BF16)
    y_ref[...] = dot(heads, spread, precision=HIGHEST)[2:3] * inputs
    affinity_ref[...] = dot_nt(readers, writers)
    halves = lane_masks()
    for pair in range(OWN_HEADS // 2):
        lanes = slice(128 * pair, 128 * pair + 128)
        pair_inputs = dtx_ref[:, lanes]
        for block in range(2):
            rows = slice(HALF * block, HALF * block + HALF)
            reach = HALF * (block + 1)
            total = y_ref[rows, lanes]
            for member in range(2):
                head = 2 * pair + member
                decay = jnp.exp(
                    cumul[rows, head : head + 1]
                    - cumul_rows[head : head + 1, :reach]
                    + bias_ref[rows, :reach]
                )
                mixing = (decay * affinity_ref[rows, :reach]).astype(BF16)
                total = total + dot(mixing, pair_inputs[:reach] * halves[member])
            y_ref[rows, lanes] = total
    gate = gate_ref[...]
    gated = y_ref[...] * (gate * jax.nn.sigmoid(gate))
    out_ref[...] = dot((gated * gain).astype(BF16), wout_ref[...]).astype(out_ref.dtype)
    square_ref[...] = jnp.broadcast_to(
        jnp.sum(gated * gated, axis=1, keepdims=True), square_ref.shape
    )


def cost(microseconds):
    flops, bytes_accessed = int(1.1e9 * microseconds), int(3.6e6 * microseconds)
    return pl.CostEstimate(flops=flops, bytes_accessed=bytes_accessed, transcendentals=0)


def vmem(count):
    return [pl.BlockSpec(memory_space=pltpu.VMEM)] * count


def forward_mix(layer, xhat, weights, wout, segc, segr, heads, maps, interpret=False):
    return pl.pallas_call(
        functools.partial(forward_kernel, layer),
        in_specs=vmem(1) + [pl.BlockSpec(memory_space=pl.ANY)] + vmem(5),
        out_shape=(
            jax.ShapeDtypeStruct((TOKENS, OWN), F32),
            jax.ShapeDtypeStruct((TOKENS, REST), F32),
            jax.ShapeDtypeStruct((TOKENS, OWN), F32),
            jax.ShapeDtypeStruct((TOKENS, WIDTH), BF16),
            jax.ShapeDtypeStruct((TOKENS, 128), F32),
            jax.ShapeDtypeStruct((8, OWN_CONV), F32),
            jax.ShapeDtypeStruct((8, WIDTH), F32),
            jax.ShapeDtypeStruct((8, OWN), F32),
        ),
        scratch_shapes=[
            pltpu.VMEM((512, WIN_COLS), BF16),
            pltpu.VMEM((TOKENS, OWN), BF16),
            pltpu.VMEM((TOKENS, TOKENS), F32),
            pltpu.VMEM((TOKENS, TOKENS), F32),
            pltpu.SemaphoreType.DMA,
        ],
        compiler_params=pltpu.CompilerParams(vmem_limit_bytes=58 * 2**20),
        cost_estimate=cost(15),
        interpret=interpret,
    )(xhat, weights, wout, segc, segr, heads, maps)


def gate_kernel(
    seed_ref, rho_ref, xhat_ref, norm_ref, wout_ref, gate_ref, y_ref, gain_ref, after_ref,
    dgate_ref, dy_ref, dwin_ref, dwout_ref, dgain_ref,
):
    seed = seed_ref[:, :WIDTH]
    mean = seed_ref[:, WIDTH : WIDTH + 128].astype(F32)
    mean = mean[:, 0:1] + mean[:, 1:2]
    gain = gain_ref[0:1]
    rho = rho_ref[...]
    gate = gate_ref[...]
    y = y_ref[...]
    open_gate = jax.nn.sigmoid(gate)
    passed = gate * open_gate
    scaled = y * passed * rho
    dyn = dot_nt(seed, wout_ref[...])
    dwout_ref[...] = dot_tn((scaled * gain).astype(BF16), seed).astype(BF16)
    dgain_ref[...] = jnp.broadcast_to(jnp.sum(dyn * scaled, axis=0, keepdims=True), dgain_ref.shape)
    dgated = rho * (dyn * gain - scaled * mean)
    dy_ref[...] = dgated * passed
    dgate = (dgated * y * (open_gate * (1.0 + gate * (1.0 - open_gate)))).astype(BF16)
    dgate_ref[...] = dgate
    parts = reordered((xhat_ref[...].astype(F32) * norm_ref[0:1]).astype(BF16))
    full, folded = weight_gradient(parts, dgate, GATE_FOLD)
    dwin_ref[:, :OWN] = full.astype(BF16)
    dwin_ref[:, OWN:] = folded.astype(BF16)


def gate_back(seed, rho, xhat, norm, wout, gate, y, gain, after, interpret=False):
    return pl.pallas_call(
        gate_kernel,
        out_shape=(
            jax.ShapeDtypeStruct((TOKENS, OWN), BF16),
            jax.ShapeDtypeStruct((TOKENS, OWN), F32),
            jax.ShapeDtypeStruct((512, GATE_COLS), BF16),
            jax.ShapeDtypeStruct((OWN, WIDTH), BF16),
            jax.ShapeDtypeStruct((8, OWN), F32),
        ),
        compiler_params=pltpu.CompilerParams(vmem_limit_bytes=58 * 2**20),
        cost_estimate=cost(8),
        interpret=interpret,
    )(seed, rho, xhat, norm, wout, gate, y, gain, after)


def backward_kernel(
    layer, dgate_ref, dy_ref, xhat_ref, norm_ref, weights_ref, rest_ref,
    segc_ref, segr_ref, taps_ref, heads_ref, dgain_ref, maps_ref, after_ref,
    dscaled_ref, dwin_ref,
    win_ref, dtx_ref, affinity_ref, bias_ref, daffinity_ref, drest_ref, dact_ref, rise_ref,
    direct_ref, dtaps_ref, semaphore,
):
    copy = fetched(weights_ref, win_ref, semaphore, layer, WIN_COLS)
    copy.start()
    taps = taps_ref[...]
    heads = heads_ref[...]
    segc = segc_ref[...]
    masks = tap_masks(segc)
    signal = rest_ref[:, :OWN_CONV]
    before = convolved(signal, taps, masks)
    open_act = jax.nn.sigmoid(before)
    active = before * open_act
    inputs = active[:, :OWN]
    writers = active[:, OWN : OWN + STATE].astype(BF16)
    readers = active[:, OWN + STATE :].astype(BF16)
    shifted, step, cumul = steps_of(rest_ref[:, OWN_CONV:], heads)
    cumul_rows = cumul.T
    spread = head_spread()
    step_wide = dot(step, spread, precision=HIGHEST)
    skip_wide = dot(heads, spread, precision=HIGHEST)[2:3]
    dtx_ref[...] = (step_wide * inputs).astype(BF16)
    allowed = (iota((TOKENS, TOKENS), 0) <= iota((TOKENS, TOKENS), 1)) & (segc == segr_ref[...])
    bias_ref[...] = jnp.where(allowed, 0.0, NEGATIVE).astype(F32)
    affinity_ref[...] = dot_nt(writers, readers)
    daffinity_ref[...] = jnp.zeros_like(daffinity_ref)
    rise_ref[...] = jnp.zeros_like(rise_ref)
    halves = lane_masks()
    head_lane = iota((1, 128), 1)
    fall_blocks = [jnp.zeros((HALF, 128), F32), jnp.zeros((HALF, 128), F32)]
    for pair in range(OWN_HEADS // 2):
        lanes = slice(128 * pair, 128 * pair + 128)
        pair_inputs = dtx_ref[:, lanes]
        pair_dy = dy_ref[:, lanes].astype(BF16)
        member_dy = [pair_dy * half for half in halves]
        for block in range(2):
            rows = slice(HALF * block, HALF * block + HALF)
            start = HALF * block
            dinput = jnp.zeros((HALF, 128), F32)
            for member in range(2):
                head = 2 * pair + member
                decay = jnp.exp(
                    cumul_rows[head : head + 1, start:]
                    - cumul[rows, head : head + 1]
                    + bias_ref[rows, start:]
                )
                dmixing = dot_nt(pair_inputs[rows], member_dy[member][start:]) * decay
                daffinity_ref[rows, start:] += dmixing
                affinity = affinity_ref[rows, start:]
                dinput = dinput + dot((decay * affinity).astype(BF16), member_dy[member][start:])
                dspread = dmixing * affinity
                fall = jnp.sum(dspread, axis=1, keepdims=True)
                fall_blocks[block] = fall_blocks[block] + jnp.where(head_lane == head, fall, 0.0)
                rise_ref[head : head + 1, start:] += jnp.sum(dspread, axis=0, keepdims=True)
            direct_ref[rows, lanes] = dinput
    dinputs = direct_ref[...]
    dy = dy_ref[...]
    dact_ref[:, :OWN] = step_wide * dinputs + skip_wide * dy
    daffinity = daffinity_ref[...].astype(BF16)
    dact_ref[:, OWN : OWN + STATE] = dot(daffinity, readers)
    dact_ref[:, OWN + STATE :] = dot_tn(daffinity, writers)
    dstep = dot_nt(dinputs * inputs, spread, precision=HIGHEST)
    skip_sum = jnp.broadcast_to(jnp.sum(dy * inputs, axis=0, keepdims=True), (8, OWN))
    dskip = dot_nt(skip_sum, spread, precision=HIGHEST)[0:1]
    dcumul = rise_ref[...].T - jnp.concatenate(fall_blocks, axis=0)
    upper = jnp.where(iota((TOKENS, TOKENS), 0) <= iota((TOKENS, TOKENS), 1), 1.0, 0.0).astype(F32)
    dlog = dot(upper, dcumul, precision=HIGHEST)
    rate = jnp.exp(heads[1:2])
    draw = (dstep - dlog * rate) * jax.nn.sigmoid(shifted)
    head_rows = (
        jnp.sum(draw, axis=0, keepdims=True),
        jnp.sum(-dlog * step * rate, axis=0, keepdims=True),
        dskip,
    )
    drest_ref[:, OWN_CONV:] = draw.astype(BF16)

    dconv = dact_ref[...] * (open_act * (1.0 + before * (1.0 - open_act)))
    dtaps_ref[...] = jnp.zeros_like(dtaps_ref)
    dtaps_ref[4:5] = jnp.sum(dconv, axis=0, keepdims=True)
    dtaps_ref[3:4] = jnp.sum(dconv * signal, axis=0, keepdims=True)
    dsignal = taps[3:4] * dconv
    for back in range(1, 4):
        masked = dconv * masks[back]
        dtaps_ref[3 - back : 4 - back] = jnp.sum(
            masked * pltpu.roll(signal, back, 0), axis=0, keepdims=True
        )
        dsignal = dsignal + taps[3 - back : 4 - back] * pltpu.roll(masked, TOKENS - back, 0)
    drest_ref[:, :OWN_CONV] = dsignal.astype(BF16)

    norm = norm_ref[0:1]
    xhat = xhat_ref[...].astype(F32)
    orders = padded_orders()
    u = (xhat * norm).astype(BF16)
    parts = [dot(u, order).astype(BF16) for order in orders]
    drest = drest_ref[...]
    copy.wait()
    from_rest = input_gradients(
        drest, win_ref[:, GATE_COLS : GATE_COLS + REST], win_ref[:, GATE_COLS + REST :], REST_FOLD
    )
    from_gate = input_gradients(
        dgate_ref[...], win_ref[:, :OWN], win_ref[:, OWN:GATE_COLS], GATE_FOLD
    )
    du = jnp.zeros((TOKENS, WIDTH), F32)
    for one, other, order in zip(from_rest, from_gate, orders):
        du = du + dot_nt((one + other).astype(BF16), order)
    dscaled_ref[...] = (du * norm).astype(BF16)

    full, folded = weight_gradient(parts, drest, REST_FOLD)
    dwin_ref[:, :OWN_CONV] = full[:, :OWN_CONV].astype(BF16)
    dwin_ref[:, REST:] = folded.astype(BF16)
    maps = maps_ref[...]
    dnorm = jnp.sum(du * xhat, axis=0, keepdims=True)
    vectors = (
        vectors_into(dtaps_ref[...], maps, 0)
        + vectors_into(only_row(dnorm, 5), maps, 1)
        + vectors_into(only_row(dgain_ref[...], 6), maps, 2)
    )
    last_row = jnp.zeros((8, 128), F32)
    for place, row in enumerate(head_rows):
        shift = VECTORS + OWN_HEADS * place
        last_row = last_row + pltpu.roll(jnp.broadcast_to(row, (8, 128)), shift, 1)
    vectors = vectors + jnp.where((iota((512, 1), 0) & 7) == 7, last_row[0:1], 0.0)
    high = vectors.astype(BF16).astype(F32)
    low = pltpu.roll(vectors - high, REMAINDERS - VECTORS, 1)
    dwin_ref[:, OWN_CONV:REST] = (full[:, OWN_CONV:] + high + low).astype(BF16)


def backward_mix(
    layer, dgate, dy, xhat, norm, weights, rest, segc, segr, taps, heads, dgain, maps,
    after, interpret=False,
):
    square = (TOKENS, TOKENS)
    return pl.pallas_call(
        functools.partial(backward_kernel, layer),
        in_specs=vmem(4) + [pl.BlockSpec(memory_space=pl.ANY)] + vmem(8),
        out_shape=(
            jax.ShapeDtypeStruct((TOKENS, WIDTH), BF16),
            jax.ShapeDtypeStruct((512, REST_COLS), BF16),
        ),
        scratch_shapes=[
            pltpu.VMEM((512, WIN_COLS), BF16),
            pltpu.VMEM((TOKENS, OWN), BF16),
            pltpu.VMEM(square, F32),
            pltpu.VMEM(square, F32),
            pltpu.VMEM(square, F32),
            pltpu.VMEM((TOKENS, REST), BF16),
            pltpu.VMEM((TOKENS, OWN_CONV), F32),
            pltpu.VMEM((128, TOKENS), F32),
            pltpu.VMEM((TOKENS, OWN), F32),
            pltpu.VMEM((8, OWN_CONV), F32),
            pltpu.SemaphoreType.DMA,
        ],
        compiler_params=pltpu.CompilerParams(vmem_limit_bytes=58 * 2**20),
        cost_estimate=cost(30),
        interpret=interpret,
    )(dgate, dy, xhat, norm, weights, rest, segc, segr, taps, heads, dgain, maps, after)


DP = ("dp_0", "dp_1", "dp_2")
DP_SEQ = DP + ("seq",)
LAYERS = 2


def swapped(v):
    return lax.ppermute(v, "seq", [(0, 1), (1, 0)])


def part(v, index, size, axis):
    return lax.dynamic_slice_in_dim(v, index * size, size, axis)


def in_order(core, own, other, axis):
    first = jnp.where(core == 0, own, other)
    second = jnp.where(core == 0, other, own)
    return jnp.concatenate([first, second], axis=axis)


def padded(v, sizes):
    return jnp.pad(v, [(0, size - now) for now, size in zip(v.shape, sizes)])


def folded_rows(rows, fold):
    tail = padded(rows[:, 8:], (LAYERS, 4, 2 * fold)).reshape(LAYERS, 4, 2, fold)
    return tail.transpose(0, 2, 1, 3).reshape(LAYERS, 8, fold)


def packed_weights(win, wout, kernel_weight, kernel_bias, norm_gain, gate_gain, core):
    win = in_order(core, win, swapped(win), 1)
    wout = in_order(core, wout, swapped(wout), 1)
    rows = [kernel_weight, kernel_bias[:, None]]
    rows += [padded(vector[:, None], (LAYERS, 1, 14)) for vector in (norm_gain, gate_gain)]
    vectors = padded(jnp.concatenate(rows, axis=1), (LAYERS, 8, 14))
    others = swapped(vectors)
    first = jnp.where(core == 0, vectors, others)
    second = jnp.where(core == 0, others, vectors)
    joined = []
    for start, stop, size in ((0, 5, 14), (5, 6, 6), (6, 8, 12)):
        both = [first[:, start:stop, :size], second[:, start:stop, :size]]
        both = jnp.concatenate(both, axis=2)
        joined.append(padded(both, both.shape[:2] + (128 - OWN_HEADS,)))
    vectors = jnp.concatenate(joined, axis=1)
    gate = part(win[:, :, :INNER], core, OWN, 2)
    steps = part(win[:, :, INNER + CONV_CH :], core, OWN_HEADS, 2)
    tail = padded(steps[:, 8:], (LAYERS, 4, 128))
    tile = jnp.concatenate([steps[:, :8], vectors], axis=2)
    rest = jnp.concatenate(
        [
            part(win[:, :, INNER : 2 * INNER], core, OWN, 2),
            win[:, :, 2 * INNER : INNER + CONV_CH],
            jnp.concatenate([tile, tail], axis=1),
        ],
        axis=2,
    )
    wout = part(wout, core, WIDTH // 2, 2)
    wout = wout.reshape(LAYERS, 3, 8, WIDTH // 2).transpose(0, 2, 1, 3)
    block = jnp.concatenate(
        [
            gate[:, :8],
            folded_rows(gate, GATE_FOLD),
            rest[:, :8],
            folded_rows(rest, REST_FOLD),
            wout.reshape(LAYERS, 8, OUT_COLS),
        ],
        axis=2,
    )
    return block.transpose(1, 0, 2).reshape(8, LAYERS * LAYER_COLS)


def output_weights(gathered, core):
    wout = gathered.reshape(CHIPS, 8, LAYERS, LAYER_COLS)[:, :, :, WIN_COLS:]
    wout = wout.reshape(CHIPS, 8, LAYERS, 3, WIDTH // 2).transpose(2, 0, 3, 1, 4)
    wout = wout.reshape(LAYERS, INNER, WIDTH // 2)
    return in_order(core, part(wout, core, OWN, 1), swapped(part(wout, 1 - core, OWN, 1)), 2)


def vector_maps(core):
    column = jnp.arange(OWN_CONV)
    channel = jnp.where(column < OWN, column + core * OWN, column - OWN + INNER)
    feature = column + core * OWN
    rows = [channel // 28, channel % 28, column // 12, column % 12, feature // 24, feature % 24]
    return padded(jnp.stack(rows).astype(jnp.int32), (8, OWN_CONV))


def over_positions(partial_sum, core):
    own = part(partial_sum, core, HALF, 0).astype(F32)
    return own + swapped(part(partial_sum, 1 - core, HALF, 0)).astype(F32)


def reduced(packed, earlier):
    if earlier is not None:
        packed, earlier = lax.optimization_barrier((packed, earlier))
    arrived = lax.all_to_all(packed, DP, 0, 0, tiled=True)
    total = jnp.sum(arrived.astype(F32), axis=0)
    if earlier is not None:
        total = jnp.where(jnp.isnan(earlier), earlier, total)
    return total, arrived[0, :1, :1].astype(F32)


def reduced_gate(dwin, dwout, core, earlier):
    half = WIDTH // 2
    dwout = in_order(core, part(dwout, core, half, 1), swapped(part(dwout, 1 - core, half, 1)), 0)
    dwout = dwout.reshape(CHIPS, 3, 8, half).transpose(0, 2, 1, 3)
    dwin = dwin.reshape(CHIPS, 8, GATE_COLS)
    packed = jnp.concatenate([dwin, dwout.reshape(CHIPS, 8, OUT_COLS)], axis=2)
    return reduced(packed, earlier)


def reduced_rest(dwin, earlier):
    return reduced(dwin.reshape(CHIPS, 8, REST_COLS), earlier)


def unfolded(total, columns, fold):
    tail = total[:, :, columns:].reshape(LAYERS, 2, 4, fold).transpose(0, 2, 1, 3)
    tail = tail.reshape(LAYERS, 4, 2 * fold)[:, :, :columns]
    return jnp.concatenate([total[:, :, :columns], tail], axis=1)


def unpacked_gradients(early_total, rest_total, core):
    win = jnp.concatenate(
        [
            unfolded(early_total[:, :, :GATE_COLS], OWN, GATE_FOLD),
            unfolded(rest_total, REST, REST_FOLD),
        ],
        axis=2,
    )
    own = part(win, core, 6, 1)
    got = swapped(part(win, 1 - core, 6, 1))
    left = jnp.where(core == 0, own, got)
    right = jnp.where(core == 0, got, own)
    shared = slice(2 * OWN, 2 * OWN + 2 * STATE)
    steps = slice(2 * OWN + 2 * STATE, 2 * OWN + 2 * STATE + OWN_HEADS)
    dwin = jnp.concatenate(
        [
            left[:, :, :OWN],
            right[:, :, :OWN],
            left[:, :, OWN : 2 * OWN],
            right[:, :, OWN : 2 * OWN],
            left[:, :, shared] + right[:, :, shared],
            left[:, :, steps],
            right[:, :, steps],
        ],
        axis=2,
    )
    half = WIDTH // 2
    wout = early_total[:, :, GATE_COLS:].reshape(LAYERS, 8, 3, half).transpose(0, 2, 1, 3)
    wout = wout.reshape(LAYERS, 24, half)
    dwout = in_order(core, part(wout, core, 12, 1), swapped(part(wout, 1 - core, 12, 1)), 2)
    tile = rest_total[:, :, OWN_CONV:REST]
    vectors = tile[:, :, VECTORS : VECTORS + VECTOR_COLS]
    vectors = vectors + tile[:, :, REMAINDERS : REMAINDERS + VECTOR_COLS]
    others = swapped(vectors)
    heads = in_order(
        core,
        vectors[:, 7, :36].reshape(LAYERS, 3, 12),
        others[:, 7, :36].reshape(LAYERS, 3, 12),
        2,
    )
    vectors = vectors + others
    taps = part(vectors[:, :5, :28], core, 14, 2)
    return (
        dwin,
        dwout,
        taps[:, :4],
        taps[:, 4],
        part(vectors[:, 5, :12], core, 6, 1),
        part(vectors[:, 6, :24], core, 12, 1),
        heads,
    )


def mean_square_scale(values):
    return lax.rsqrt(jnp.mean(values * values, axis=1, keepdims=True) + NORM_EPS)


def layers_of(
    hidden, cotangent, segments, head_values, weights, wouts, core, interpret=False
):
    segr = segments
    segc = segments.reshape(TOKENS, 1)
    heads_all = padded(part(head_values, core, OWN_HEADS, 2), (LAYERS, 8, 128))
    maps = vector_maps(core)
    current = hidden.astype(F32)
    saved = []
    for layer in range(LAYERS):
        sigma = mean_square_scale(current)
        xhat = lax.all_gather((current * sigma).astype(BF16), "seq", axis=0, tiled=True)
        gate, rest, y, out, square, taps, norm, gain = forward_mix(
            layer, xhat, weights, wouts[layer], segc, segr, heads_all[layer], maps,
            interpret=interpret,
        )
        square = square + swapped(square)
        rho = lax.rsqrt(square[:, :1] / INNER + NORM_EPS)
        branch = over_positions(out, core)
        own_rho = part(rho, core, HALF, 0)
        saved.append((current, sigma, xhat, gate, rest, y, rho, own_rho, branch, taps, norm, gain))
        current = current + own_rho * branch
    upstream = cotangent.astype(F32)
    sent = [None] * LAYERS
    arrived = None
    after = [jnp.zeros((1, 1), F32)] * 2
    for layer in reversed(range(LAYERS)):
        before, sigma, xhat, gate, rest, y, rho, own_rho, branch, taps, norm, gain = saved[layer]
        seed = upstream.astype(BF16)
        mean = own_rho * jnp.sum(seed.astype(F32) * branch, axis=1, keepdims=True) / INNER
        high = lax.reduce_precision(mean, 8, 7)
        means = jnp.concatenate([high, mean - high], axis=1).astype(BF16)
        seed = jnp.concatenate([seed, padded(means, (HALF, 128))], axis=1)
        seed = lax.all_gather(seed, "seq", axis=0, tiled=True)
        dgate, dy, dwin_gate, dwout, dgain = gate_back(
            seed, rho, xhat, norm, wouts[layer], gate, y, gain, after[0], interpret=interpret
        )
        early, arrived = reduced_gate(dwin_gate, dwout, core, arrived)
        after_early = arrived
        dscaled, dwin_rest = backward_mix(
            layer, dgate, dy, xhat, norm, weights, rest, segc, segr, taps, heads_all[layer],
            dgain, maps, after[1], interpret=interpret,
        )
        late, arrived = reduced_rest(dwin_rest, arrived)
        sent[layer] = (early, late)
        after = [after_early, arrived]
        dscaled, after_early = lax.optimization_barrier((dscaled, after_early))
        scaled = over_positions(dscaled, core)
        upstream = upstream + sigma * (
            scaled
            - before * (sigma * sigma) * jnp.mean(scaled * before, axis=1, keepdims=True)
        )
        upstream = jnp.where(jnp.isnan(after_early), after_early, upstream)
    return current.astype(BF16), upstream.astype(BF16), sent


def per_device(
    hidden_in,
    segments,
    projection_in,
    projection_out,
    kernel_weight,
    kernel_bias,
    norm_gain,
    gate_gain,
    head_values,
    cotangent,
):
    core = lax.axis_index("seq")
    block = packed_weights(
        projection_in, projection_out, kernel_weight, kernel_bias, norm_gain, gate_gain, core
    )
    weights = lax.all_gather(block, DP, axis=0, tiled=True)
    wouts = output_weights(weights, core)

    hidden_out, input_gradient, totals = layers_of(
        hidden_in[0], cotangent[0], segments, head_values, weights, wouts, core
    )
    totals = [jnp.stack(layers) for layers in zip(*totals)]
    return (hidden_out[None], input_gradient[None]) + unpacked_gradients(*totals, core)


def solution(mesh):
    torus = Mesh(mesh.devices.reshape(4, 4, 4, mesh.shape["seq"]), DP_SEQ)
    tokens = P(DP, "seq", None)
    weights = (
        P(None, DP_SEQ, None),
        P(None, DP_SEQ, None),
        P(None, None, DP_SEQ),
        P(None, DP_SEQ),
        P(None, DP_SEQ),
        P(None, DP_SEQ),
    )
    return jax.shard_map(
        per_device,
        mesh=torus,
        in_specs=(tokens, P(DP, None)) + weights + (P(), tokens),
        out_specs=(tokens, tokens) + weights + (P(),),
        check_vma=False,
    )
```

```python
import functools

import jax
import jax.numpy as jnp
from jax import lax
from jax.experimental import pallas as pl
from jax.experimental.pallas import tpu as pltpu
from jax.sharding import Mesh
from jax.sharding import PartitionSpec as P

HEADS = 24
HEAD_DIM = 64
STATE = 128
INNER = 1536
CONV_CH = 1792
WIDTH = 768
TOKENS = 512
CHIPS = 64
HALF = 256
OWN_HEADS = 12
OWN = OWN_HEADS * HEAD_DIM
OWN_CONV = OWN + 2 * STATE
REST = OWN_CONV + 128
GATE_FOLD = OWN // 2
REST_FOLD = 640
GATE_COLS = OWN + GATE_FOLD
REST_COLS = REST + REST_FOLD
WIN_COLS = GATE_COLS + REST_COLS
OUT_COLS = 3 * (WIDTH // 2)
LAYER_COLS = WIN_COLS + OUT_COLS
VECTORS = OWN_HEADS
REMAINDERS = 64
VECTOR_COLS = 40
NORM_EPS = 1e-05
NEGATIVE = -1e30
F32 = jnp.float32
BF16 = jnp.bfloat16
HIGHEST = lax.Precision.HIGHEST


def dot(a, b, dims=((1,), (0,)), precision=None):
    return lax.dot_general(a, b, (dims, ((), ())), precision=precision, preferred_element_type=F32)


def dot_nt(a, b, precision=None):
    return dot(a, b, ((1,), (1,)), precision)


def dot_tn(a, b, precision=None):
    return dot(a, b, ((0,), (0,)), precision)


def iota(shape, dim):
    return lax.broadcasted_iota(jnp.int32, shape, dim)


def padded_orders():
    column = iota((1, 512), 1)
    row = iota((WIDTH, 512), 0)
    start = 12 * (column >> 3)
    place = column & 7
    features = (start + place, start + 8 + (place & 3))
    return [jnp.where(feature == row, 1.0, 0.0).astype(BF16) for feature in features]


def half_places():
    low = (iota((1, 512), 1) & 7) < 4
    return jnp.where(low, 1.0, 0.0).astype(BF16), jnp.where(low, 0.0, 1.0).astype(BF16)


def head_spread():
    return jnp.where(iota((128, OWN), 0) == (iota((128, OWN), 1) >> 6), 1.0, 0.0).astype(F32)


def softplus(v):
    return jnp.maximum(v, 0.0) + jnp.log1p(jnp.exp(-jnp.abs(v)))


def tap_masks(segment_column):
    position = iota((TOKENS, 1), 0)
    wide = jnp.broadcast_to(segment_column, (TOKENS, 128))
    masks = [None]
    for back in range(1, 4):
        before = pltpu.roll(wide, back, 0)[:, :1]
        same = (before == segment_column) & (position >= back)
        masks.append(jnp.where(same, 1.0, 0.0).astype(F32))
    return masks


def convolved(signal, taps, masks):
    total = taps[3:4] * signal
    for back in range(1, 4):
        total = total + taps[3 - back : 4 - back] * (pltpu.roll(signal, back, 0) * masks[back])
    return total + taps[4:5]


def steps_of(raw, heads):
    shifted = raw + heads[0:1]
    step = softplus(shifted)
    log_decay = -step * jnp.exp(heads[1:2])
    lower = jnp.where(iota((TOKENS, TOKENS), 0) >= iota((TOKENS, TOKENS), 1), 1.0, 0.0).astype(F32)
    return shifted, step, dot(lower, log_decay, precision=HIGHEST)


def lane_masks():
    low = iota((1, 128), 1) < HEAD_DIM
    return (jnp.where(low, 1.0, 0.0).astype(BF16), jnp.where(low, 0.0, 1.0).astype(BF16))


def reordered(scaled, orders=None):
    once, twice = [dot(scaled, order).astype(BF16) for order in orders or padded_orders()]
    low, high = half_places()
    return once, twice * low, twice * high


def projected(parts, full, folded, fold):
    u_full, u_low, u_high = parts
    rest = full.shape[1] - fold
    left = dot(u_full, full[:, :fold]) + dot(u_low, folded)
    right = dot(u_full, full[:, fold:]) + dot(u_high, folded[:, :rest])
    return left, right


def weight_gradient(parts, grad, fold):
    u_full, u_low, u_high = parts
    rest = grad.shape[1] - fold
    folded = dot_tn(u_low, grad[:, :fold])
    high = dot_tn(u_high, grad[:, fold:])
    if rest < fold:
        high = jnp.concatenate([high, jnp.zeros((high.shape[0], fold - rest), F32)], axis=1)
    return dot_tn(u_full, grad), folded + high


def input_gradients(grad, full, folded, fold):
    rest = grad.shape[1] - fold
    return (
        dot_nt(grad, full),
        dot_nt(grad[:, :fold], folded),
        dot_nt(grad[:, fold:], folded[:, :rest]),
    )


def column_picks(maps, kind, columns):
    chips = maps[2 * kind : 2 * kind + 1, :columns]
    places = maps[2 * kind + 1 : 2 * kind + 2, :columns]
    rows = iota((512, 1), 0) >> 3
    keep = jnp.where(rows == chips, 1.0, 0.0).astype(F32)
    pick = jnp.where(iota((128, columns), 0) == places + VECTORS, 1.0, 0.0).astype(F32)
    return keep, pick


def vectors_from(tile, maps, kind, columns):
    keep, pick = column_picks(maps, kind, columns)
    spread = dot(tile, pick.astype(BF16)) * keep
    return jnp.sum(spread.reshape(CHIPS, 8, columns), axis=0)


def vectors_into(values, maps, kind):
    columns = values.shape[1]
    keep, pick = column_picks(maps, kind, columns)
    tiled = jnp.broadcast_to(values[None], (CHIPS, 8, columns)).reshape(512, columns)
    return dot_nt(tiled * keep, pick, precision=HIGHEST)


def only_row(values, row):
    return jnp.where(iota((8, 1), 0) == row, values, 0.0)


def fetched(source, target, semaphore, layer, columns):
    start = layer * LAYER_COLS
    return pltpu.make_async_copy(source.at[:, start : start + columns], target, semaphore)


def spread_steps(step, spread):
    spread = spread.astype(BF16)
    high = step.astype(BF16)
    low = (step - high.astype(F32)).astype(BF16)
    return dot(high, spread) + dot(low, spread)


def forward_kernel(
    layer, xhat_ref, weights_ref, wout_ref, segc_ref, segr_ref, heads_ref, maps_ref,
    gate_ref, rest_ref, y_ref, out_ref, square_ref, taps_ref, norm_ref, gain_ref,
    win_ref, dtx_ref, affinity_ref, bias_ref, semaphore,
):
    copy = fetched(weights_ref, win_ref, semaphore, layer, WIN_COLS)
    copy.start()
    segc = segc_ref[...]
    masks = tap_masks(segc)
    allowed = (iota((TOKENS, TOKENS), 0) >= iota((TOKENS, TOKENS), 1)) & (segc == segr_ref[...])
    bias_ref[...] = jnp.where(allowed, 0.0, NEGATIVE).astype(F32)
    copy.wait()
    maps = maps_ref[...]
    tile = win_ref[:, GATE_COLS + OWN_CONV : GATE_COLS + REST]
    taps = vectors_from(tile, maps, 0, OWN_CONV)
    norm = vectors_from(tile, maps, 1, WIDTH)[5:6]
    gain = vectors_from(tile, maps, 2, OWN)[6:7]
    taps_ref[...] = taps
    norm_ref[...] = jnp.broadcast_to(norm, norm_ref.shape)
    gain_ref[...] = jnp.broadcast_to(gain, gain_ref.shape)
    parts = reordered((xhat_ref[...].astype(F32) * norm).astype(BF16))
    rest_ref[:, :REST_FOLD], rest_ref[:, REST_FOLD:] = projected(
        parts, win_ref[:, GATE_COLS : GATE_COLS + REST], win_ref[:, GATE_COLS + REST :], REST_FOLD
    )
    gate_ref[:, :GATE_FOLD], gate_ref[:, GATE_FOLD:] = projected(
        parts, win_ref[:, :OWN], win_ref[:, OWN:GATE_COLS], GATE_FOLD
    )
    heads = heads_ref[...]
    before = convolved(rest_ref[:, :OWN_CONV], taps, masks)
    active = before * jax.nn.sigmoid(before)
    inputs = active[:, :OWN]
    writers = active[:, OWN : OWN + STATE].astype(BF16)
    readers = active[:, OWN + STATE :].astype(BF16)
    _, step, cumul = steps_of(rest_ref[:, OWN_CONV:], heads)
    cumul_rows = cumul.T
    spread = head_spread()
    dtx_ref[...] = (spread_steps(step, spread) * inputs).astype(BF16)
    y_ref[...] = dot(heads, spread, precision=HIGHEST)[2:3] * inputs
    affinity_ref[...] = dot_nt(readers, writers)
    halves = lane_masks()
    for pair in range(OWN_HEADS // 2):
        lanes = slice(128 * pair, 128 * pair + 128)
        pair_inputs = dtx_ref[:, lanes]
        for block in range(2):
            rows = slice(HALF * block, HALF * block + HALF)
            reach = HALF * (block + 1)
            total = y_ref[rows, lanes]
            for member in range(2):
                head = 2 * pair + member
                decay = jnp.exp(
                    cumul[rows, head : head + 1]
                    - cumul_rows[head : head + 1, :reach]
                    + bias_ref[rows, :reach]
                )
                mixing = (decay * affinity_ref[rows, :reach]).astype(BF16)
                total = total + dot(mixing, pair_inputs[:reach] * halves[member])
            y_ref[rows, lanes] = total
    gate = gate_ref[...]
    gated = y_ref[...] * (gate * jax.nn.sigmoid(gate))
    out_ref[...] = dot((gated * gain).astype(BF16), wout_ref[...]).astype(out_ref.dtype)
    square_ref[...] = jnp.broadcast_to(
        jnp.sum(gated * gated, axis=1, keepdims=True), square_ref.shape
    )


def cost(microseconds):
    flops, bytes_accessed = int(1.1e9 * microseconds), int(3.6e6 * microseconds)
    return pl.CostEstimate(flops=flops, bytes_accessed=bytes_accessed, transcendentals=0)


def vmem(count):
    return [pl.BlockSpec(memory_space=pltpu.VMEM)] * count


def forward_mix(layer, xhat, weights, wout, segc, segr, heads, maps, interpret=False):
    return pl.pallas_call(
        functools.partial(forward_kernel, layer),
        in_specs=vmem(1) + [pl.BlockSpec(memory_space=pl.ANY)] + vmem(5),
        out_shape=(
            jax.ShapeDtypeStruct((TOKENS, OWN), F32),
            jax.ShapeDtypeStruct((TOKENS, REST), F32),
            jax.ShapeDtypeStruct((TOKENS, OWN), F32),
            jax.ShapeDtypeStruct((TOKENS, WIDTH), BF16),
            jax.ShapeDtypeStruct((TOKENS, 128), F32),
            jax.ShapeDtypeStruct((8, OWN_CONV), F32),
            jax.ShapeDtypeStruct((8, WIDTH), F32),
            jax.ShapeDtypeStruct((8, OWN), F32),
        ),
        scratch_shapes=[
            pltpu.VMEM((512, WIN_COLS), BF16),
            pltpu.VMEM((TOKENS, OWN), BF16),
            pltpu.VMEM((TOKENS, TOKENS), F32),
            pltpu.VMEM((TOKENS, TOKENS), F32),
            pltpu.SemaphoreType.DMA,
        ],
        compiler_params=pltpu.CompilerParams(vmem_limit_bytes=58 * 2**20),
        cost_estimate=cost(15),
        interpret=interpret,
    )(xhat, weights, wout, segc, segr, heads, maps)


def gate_kernel(
    seed_ref, rho_ref, xhat_ref, norm_ref, wout_ref, gate_ref, y_ref, gain_ref, after_ref,
    dgate_ref, dy_ref, dwin_ref, dwout_ref, dgain_ref,
):
    seed = seed_ref[:, :WIDTH]
    mean = seed_ref[:, WIDTH : WIDTH + 128].astype(F32)
    mean = mean[:, 0:1] + mean[:, 1:2]
    gain = gain_ref[0:1]
    rho = rho_ref[...]
    gate = gate_ref[...]
    y = y_ref[...]
    open_gate = jax.nn.sigmoid(gate)
    passed = gate * open_gate
    scaled = y * passed * rho
    dyn = dot_nt(seed, wout_ref[...])
    dwout_ref[...] = dot_tn((scaled * gain).astype(BF16), seed).astype(BF16)
    dgain_ref[...] = jnp.broadcast_to(jnp.sum(dyn * scaled, axis=0, keepdims=True), dgain_ref.shape)
    dgated = rho * (dyn * gain - scaled * mean)
    dy_ref[...] = dgated * passed
    dgate = (dgated * y * (open_gate * (1.0 + gate * (1.0 - open_gate)))).astype(BF16)
    dgate_ref[...] = dgate
    parts = reordered((xhat_ref[...].astype(F32) * norm_ref[0:1]).astype(BF16))
    full, folded = weight_gradient(parts, dgate, GATE_FOLD)
    dwin_ref[:, :OWN] = full.astype(BF16)
    dwin_ref[:, OWN:] = folded.astype(BF16)


def gate_back(seed, rho, xhat, norm, wout, gate, y, gain, after, interpret=False):
    return pl.pallas_call(
        gate_kernel,
        out_shape=(
            jax.ShapeDtypeStruct((TOKENS, OWN), BF16),
            jax.ShapeDtypeStruct((TOKENS, OWN), F32),
            jax.ShapeDtypeStruct((512, GATE_COLS), BF16),
            jax.ShapeDtypeStruct((OWN, WIDTH), BF16),
            jax.ShapeDtypeStruct((8, OWN), F32),
        ),
        compiler_params=pltpu.CompilerParams(vmem_limit_bytes=58 * 2**20),
        cost_estimate=cost(8),
        interpret=interpret,
    )(seed, rho, xhat, norm, wout, gate, y, gain, after)


def backward_kernel(
    layer, dgate_ref, dy_ref, xhat_ref, norm_ref, weights_ref, rest_ref,
    segc_ref, segr_ref, taps_ref, heads_ref, dgain_ref, maps_ref, after_ref,
    dscaled_ref, dwin_ref,
    win_ref, dtx_ref, affinity_ref, bias_ref, daffinity_ref, drest_ref, dact_ref, rise_ref,
    direct_ref, dtaps_ref, semaphore,
):
    copy = fetched(weights_ref, win_ref, semaphore, layer, WIN_COLS)
    copy.start()
    taps = taps_ref[...]
    heads = heads_ref[...]
    segc = segc_ref[...]
    masks = tap_masks(segc)
    signal = rest_ref[:, :OWN_CONV]
    before = convolved(signal, taps, masks)
    open_act = jax.nn.sigmoid(before)
    active = before * open_act
    inputs = active[:, :OWN]
    writers = active[:, OWN : OWN + STATE].astype(BF16)
    readers = active[:, OWN + STATE :].astype(BF16)
    shifted, step, cumul = steps_of(rest_ref[:, OWN_CONV:], heads)
    cumul_rows = cumul.T
    spread = head_spread()
    step_wide = spread_steps(step, spread)
    skip_wide = dot(heads, spread, precision=HIGHEST)[2:3]
    dtx_ref[...] = (step_wide * inputs).astype(BF16)
    allowed = (iota((TOKENS, TOKENS), 0) <= iota((TOKENS, TOKENS), 1)) & (segc == segr_ref[...])
    bias_ref[...] = jnp.where(allowed, 0.0, NEGATIVE).astype(F32)
    affinity_ref[...] = dot_nt(writers, readers)
    daffinity_ref[...] = jnp.zeros_like(daffinity_ref)
    rise_ref[...] = jnp.zeros_like(rise_ref)
    halves = lane_masks()
    head_lane = iota((1, 128), 1)
    fall_blocks = [jnp.zeros((HALF, 128), F32), jnp.zeros((HALF, 128), F32)]
    for pair in range(OWN_HEADS // 2):
        lanes = slice(128 * pair, 128 * pair + 128)
        pair_inputs = dtx_ref[:, lanes]
        pair_dy = dy_ref[:, lanes].astype(BF16)
        member_dy = [pair_dy * half for half in halves]
        for block in range(2):
            rows = slice(HALF * block, HALF * block + HALF)
            start = HALF * block
            dinput = jnp.zeros((HALF, 128), F32)
            for member in range(2):
                head = 2 * pair + member
                decay = jnp.exp(
                    cumul_rows[head : head + 1, start:]
                    - cumul[rows, head : head + 1]
                    + bias_ref[rows, start:]
                )
                dmixing = dot_nt(pair_inputs[rows], member_dy[member][start:]) * decay
                daffinity_ref[rows, start:] += dmixing
                affinity = affinity_ref[rows, start:]
                dinput = dinput + dot((decay * affinity).astype(BF16), member_dy[member][start:])
                dspread = dmixing * affinity
                fall = jnp.sum(dspread, axis=1, keepdims=True)
                fall_blocks[block] = fall_blocks[block] + jnp.where(head_lane == head, fall, 0.0)
                rise_ref[head : head + 1, start:] += jnp.sum(dspread, axis=0, keepdims=True)
            direct_ref[rows, lanes] = dinput
    dinputs = direct_ref[...]
    dy = dy_ref[...]
    dact_ref[:, :OWN] = step_wide * dinputs + skip_wide * dy
    daffinity = daffinity_ref[...].astype(BF16)
    dact_ref[:, OWN : OWN + STATE] = dot(daffinity, readers)
    dact_ref[:, OWN + STATE :] = dot_tn(daffinity, writers)
    dstep = dot_nt(dinputs * inputs, spread, precision=HIGHEST)
    skip_sum = jnp.broadcast_to(jnp.sum(dy * inputs, axis=0, keepdims=True), (8, OWN))
    dskip = dot_nt(skip_sum, spread, precision=HIGHEST)[0:1]
    dcumul = rise_ref[...].T - jnp.concatenate(fall_blocks, axis=0)
    upper = jnp.where(iota((TOKENS, TOKENS), 0) <= iota((TOKENS, TOKENS), 1), 1.0, 0.0).astype(F32)
    dlog = dot(upper, dcumul, precision=HIGHEST)
    rate = jnp.exp(heads[1:2])
    draw = (dstep - dlog * rate) * jax.nn.sigmoid(shifted)
    head_rows = (
        jnp.sum(draw, axis=0, keepdims=True),
        jnp.sum(-dlog * step * rate, axis=0, keepdims=True),
        dskip,
    )
    drest_ref[:, OWN_CONV:] = draw.astype(BF16)

    dconv = dact_ref[...] * (open_act * (1.0 + before * (1.0 - open_act)))
    dtaps_ref[...] = jnp.zeros_like(dtaps_ref)
    dtaps_ref[4:5] = jnp.sum(dconv, axis=0, keepdims=True)
    dtaps_ref[3:4] = jnp.sum(dconv * signal, axis=0, keepdims=True)
    dsignal = taps[3:4] * dconv
    for back in range(1, 4):
        masked = dconv * masks[back]
        dtaps_ref[3 - back : 4 - back] = jnp.sum(
            masked * pltpu.roll(signal, back, 0), axis=0, keepdims=True
        )
        dsignal = dsignal + taps[3 - back : 4 - back] * pltpu.roll(masked, TOKENS - back, 0)
    drest_ref[:, :OWN_CONV] = dsignal.astype(BF16)

    norm = norm_ref[0:1]
    xhat = xhat_ref[...].astype(F32)
    orders = padded_orders()
    u = (xhat * norm).astype(BF16)
    parts = reordered(u, orders)
    drest = drest_ref[...]
    copy.wait()
    from_rest = input_gradients(
        drest, win_ref[:, GATE_COLS : GATE_COLS + REST], win_ref[:, GATE_COLS + REST :], REST_FOLD
    )
    from_gate = input_gradients(
        dgate_ref[...], win_ref[:, :OWN], win_ref[:, OWN:GATE_COLS], GATE_FOLD
    )
    once, low, high = [(one + other).astype(BF16) for one, other in zip(from_rest, from_gate)]
    low_places, high_places = half_places()
    du = dot_nt(once, orders[0]) + dot_nt(low * low_places + high * high_places, orders[1])
    dscaled_ref[...] = (du * norm).astype(BF16)

    full, folded = weight_gradient(parts, drest, REST_FOLD)
    dwin_ref[:, :OWN_CONV] = full[:, :OWN_CONV].astype(BF16)
    dwin_ref[:, REST:] = folded.astype(BF16)
    maps = maps_ref[...]
    dnorm = jnp.sum(du * xhat, axis=0, keepdims=True)
    vectors = (
        vectors_into(dtaps_ref[...], maps, 0)
        + vectors_into(only_row(dnorm, 5), maps, 1)
        + vectors_into(only_row(dgain_ref[...], 6), maps, 2)
    )
    last_row = jnp.zeros((8, 128), F32)
    for place, row in enumerate(head_rows):
        shift = VECTORS + OWN_HEADS * place
        last_row = last_row + pltpu.roll(jnp.broadcast_to(row, (8, 128)), shift, 1)
    vectors = vectors + jnp.where((iota((512, 1), 0) & 7) == 7, last_row[0:1], 0.0)
    high = vectors.astype(BF16).astype(F32)
    low = pltpu.roll(vectors - high, REMAINDERS - VECTORS, 1)
    dwin_ref[:, OWN_CONV:REST] = (full[:, OWN_CONV:] + high + low).astype(BF16)


def backward_mix(
    layer, dgate, dy, xhat, norm, weights, rest, segc, segr, taps, heads, dgain, maps,
    after, interpret=False,
):
    square = (TOKENS, TOKENS)
    return pl.pallas_call(
        functools.partial(backward_kernel, layer),
        in_specs=vmem(4) + [pl.BlockSpec(memory_space=pl.ANY)] + vmem(8),
        out_shape=(
            jax.ShapeDtypeStruct((TOKENS, WIDTH), BF16),
            jax.ShapeDtypeStruct((512, REST_COLS), BF16),
        ),
        scratch_shapes=[
            pltpu.VMEM((512, WIN_COLS), BF16),
            pltpu.VMEM((TOKENS, OWN), BF16),
            pltpu.VMEM(square, F32),
            pltpu.VMEM(square, F32),
            pltpu.VMEM(square, F32),
            pltpu.VMEM((TOKENS, REST), BF16),
            pltpu.VMEM((TOKENS, OWN_CONV), F32),
            pltpu.VMEM((128, TOKENS), F32),
            pltpu.VMEM((TOKENS, OWN), F32),
            pltpu.VMEM((8, OWN_CONV), F32),
            pltpu.SemaphoreType.DMA,
        ],
        compiler_params=pltpu.CompilerParams(vmem_limit_bytes=58 * 2**20),
        cost_estimate=cost(30),
        interpret=interpret,
    )(dgate, dy, xhat, norm, weights, rest, segc, segr, taps, heads, dgain, maps, after)


DP = ("dp_0", "dp_1", "dp_2")
DP_SEQ = DP + ("seq",)
LAYERS = 2


def swapped(v):
    return lax.ppermute(v, "seq", [(0, 1), (1, 0)])


def part(v, index, size, axis):
    return lax.dynamic_slice_in_dim(v, index * size, size, axis)


def in_order(core, own, other, axis):
    first = jnp.where(core == 0, own, other)
    second = jnp.where(core == 0, other, own)
    return jnp.concatenate([first, second], axis=axis)


def padded(v, sizes):
    return jnp.pad(v, [(0, size - now) for now, size in zip(v.shape, sizes)])


def folded_rows(rows, fold):
    tail = padded(rows[:, 8:], (LAYERS, 4, 2 * fold)).reshape(LAYERS, 4, 2, fold)
    return tail.transpose(0, 2, 1, 3).reshape(LAYERS, 8, fold)


def packed_weights(win, wout, kernel_weight, kernel_bias, norm_gain, gate_gain, core):
    win = in_order(core, win, swapped(win), 1)
    wout = in_order(core, wout, swapped(wout), 1)
    rows = [kernel_weight, kernel_bias[:, None]]
    rows += [padded(vector[:, None], (LAYERS, 1, 14)) for vector in (norm_gain, gate_gain)]
    vectors = padded(jnp.concatenate(rows, axis=1), (LAYERS, 8, 14))
    others = swapped(vectors)
    first = jnp.where(core == 0, vectors, others)
    second = jnp.where(core == 0, others, vectors)
    joined = []
    for start, stop, size in ((0, 5, 14), (5, 6, 6), (6, 8, 12)):
        both = [first[:, start:stop, :size], second[:, start:stop, :size]]
        both = jnp.concatenate(both, axis=2)
        joined.append(padded(both, both.shape[:2] + (128 - OWN_HEADS,)))
    vectors = jnp.concatenate(joined, axis=1)
    gate = part(win[:, :, :INNER], core, OWN, 2)
    steps = part(win[:, :, INNER + CONV_CH :], core, OWN_HEADS, 2)
    tail = padded(steps[:, 8:], (LAYERS, 4, 128))
    tile = jnp.concatenate([steps[:, :8], vectors], axis=2)
    rest = jnp.concatenate(
        [
            part(win[:, :, INNER : 2 * INNER], core, OWN, 2),
            win[:, :, 2 * INNER : INNER + CONV_CH],
            jnp.concatenate([tile, tail], axis=1),
        ],
        axis=2,
    )
    wout = part(wout, core, WIDTH // 2, 2)
    wout = wout.reshape(LAYERS, 3, 8, WIDTH // 2).transpose(0, 2, 1, 3)
    block = jnp.concatenate(
        [
            gate[:, :8],
            folded_rows(gate, GATE_FOLD),
            rest[:, :8],
            folded_rows(rest, REST_FOLD),
            wout.reshape(LAYERS, 8, OUT_COLS),
        ],
        axis=2,
    )
    return block.transpose(1, 0, 2).reshape(8, LAYERS * LAYER_COLS)


def output_weights(gathered, core):
    wout = gathered.reshape(CHIPS, 8, LAYERS, LAYER_COLS)[:, :, :, WIN_COLS:]
    wout = wout.reshape(CHIPS, 8, LAYERS, 3, WIDTH // 2).transpose(2, 0, 3, 1, 4)
    wout = wout.reshape(LAYERS, INNER, WIDTH // 2)
    return in_order(core, part(wout, core, OWN, 1), swapped(part(wout, 1 - core, OWN, 1)), 2)


def vector_maps(core):
    column = jnp.arange(OWN_CONV)
    channel = jnp.where(column < OWN, column + core * OWN, column - OWN + INNER)
    feature = column + core * OWN
    rows = [channel // 28, channel % 28, column // 12, column % 12, feature // 24, feature % 24]
    return padded(jnp.stack(rows).astype(jnp.int32), (8, OWN_CONV))


def over_positions(partial_sum, core):
    own = part(partial_sum, core, HALF, 0).astype(F32)
    return own + swapped(part(partial_sum, 1 - core, HALF, 0)).astype(F32)


def reduced(packed, earlier):
    if earlier is not None:
        packed, earlier = lax.optimization_barrier((packed, earlier))
    arrived = lax.all_to_all(packed, DP, 0, 0, tiled=True)
    total = jnp.sum(arrived.astype(F32), axis=0)
    if earlier is not None:
        total = jnp.where(jnp.isnan(earlier), earlier, total)
    return total, arrived[0, :1, :1].astype(F32)


def reduced_gate(dwin, dwout, core, earlier):
    half = WIDTH // 2
    dwout = in_order(core, part(dwout, core, half, 1), swapped(part(dwout, 1 - core, half, 1)), 0)
    dwout = dwout.reshape(CHIPS, 3, 8, half).transpose(0, 2, 1, 3)
    dwin = dwin.reshape(CHIPS, 8, GATE_COLS)
    packed = jnp.concatenate([dwin, dwout.reshape(CHIPS, 8, OUT_COLS)], axis=2)
    return reduced(packed, earlier)


def reduced_rest(dwin, earlier):
    return reduced(dwin.reshape(CHIPS, 8, REST_COLS), earlier)


def unfolded(total, columns, fold):
    tail = total[:, :, columns:].reshape(LAYERS, 2, 4, fold).transpose(0, 2, 1, 3)
    tail = tail.reshape(LAYERS, 4, 2 * fold)[:, :, :columns]
    return jnp.concatenate([total[:, :, :columns], tail], axis=1)


def unpacked_gradients(early_total, rest_total, core):
    win = jnp.concatenate(
        [
            unfolded(early_total[:, :, :GATE_COLS], OWN, GATE_FOLD),
            unfolded(rest_total, REST, REST_FOLD),
        ],
        axis=2,
    )
    own = part(win, core, 6, 1)
    got = swapped(part(win, 1 - core, 6, 1))
    left = jnp.where(core == 0, own, got)
    right = jnp.where(core == 0, got, own)
    shared = slice(2 * OWN, 2 * OWN + 2 * STATE)
    steps = slice(2 * OWN + 2 * STATE, 2 * OWN + 2 * STATE + OWN_HEADS)
    dwin = jnp.concatenate(
        [
            left[:, :, :OWN],
            right[:, :, :OWN],
            left[:, :, OWN : 2 * OWN],
            right[:, :, OWN : 2 * OWN],
            left[:, :, shared] + right[:, :, shared],
            left[:, :, steps],
            right[:, :, steps],
        ],
        axis=2,
    )
    half = WIDTH // 2
    wout = early_total[:, :, GATE_COLS:].reshape(LAYERS, 8, 3, half).transpose(0, 2, 1, 3)
    wout = wout.reshape(LAYERS, 24, half)
    dwout = in_order(core, part(wout, core, 12, 1), swapped(part(wout, 1 - core, 12, 1)), 2)
    tile = rest_total[:, :, OWN_CONV:REST]
    vectors = tile[:, :, VECTORS : VECTORS + VECTOR_COLS]
    vectors = vectors + tile[:, :, REMAINDERS : REMAINDERS + VECTOR_COLS]
    others = swapped(vectors)
    heads = in_order(
        core,
        vectors[:, 7, :36].reshape(LAYERS, 3, 12),
        others[:, 7, :36].reshape(LAYERS, 3, 12),
        2,
    )
    vectors = vectors + others
    taps = part(vectors[:, :5, :28], core, 14, 2)
    return (
        dwin,
        dwout,
        taps[:, :4],
        taps[:, 4],
        part(vectors[:, 5, :12], core, 6, 1),
        part(vectors[:, 6, :24], core, 12, 1),
        heads,
    )


def mean_square_scale(values):
    return lax.rsqrt(jnp.mean(values * values, axis=1, keepdims=True) + NORM_EPS)


def layers_of(
    hidden, cotangent, segments, head_values, weights, core, interpret=False
):
    segr = segments
    segc = segments.reshape(TOKENS, 1)
    heads_all = padded(part(head_values, core, OWN_HEADS, 2), (LAYERS, 8, 128))
    maps = vector_maps(core)
    current = hidden.astype(F32)
    saved = []
    for layer in range(LAYERS):
        sigma = mean_square_scale(current)
        xhat = lax.all_gather((current * sigma).astype(BF16), "seq", axis=0, tiled=True)
        if layer == 0:
            weights, xhat, segc, heads_all, maps = lax.optimization_barrier(
                (weights, xhat, segc, heads_all, maps)
            )
            wouts = output_weights(weights, core)
        gate, rest, y, out, square, taps, norm, gain = forward_mix(
            layer, xhat, weights, wouts[layer], segc, segr, heads_all[layer], maps,
            interpret=interpret,
        )
        square = square + swapped(square)
        rho = lax.rsqrt(square[:, :1] / INNER + NORM_EPS)
        branch = over_positions(out, core)
        own_rho = part(rho, core, HALF, 0)
        saved.append((current, sigma, xhat, gate, rest, y, rho, own_rho, branch, taps, norm, gain))
        current = current + own_rho * branch
    upstream = cotangent.astype(F32)
    sent = [None] * LAYERS
    arrived = None
    after = [jnp.zeros((1, 1), F32)] * 2
    for layer in reversed(range(LAYERS)):
        before, sigma, xhat, gate, rest, y, rho, own_rho, branch, taps, norm, gain = saved[layer]
        seed = upstream.astype(BF16)
        mean = own_rho * jnp.sum(seed.astype(F32) * branch, axis=1, keepdims=True) / INNER
        high = lax.reduce_precision(mean, 8, 7)
        means = jnp.concatenate([high, mean - high], axis=1).astype(BF16)
        seed = jnp.concatenate([seed, padded(means, (HALF, 128))], axis=1)
        seed = lax.all_gather(seed, "seq", axis=0, tiled=True)
        dgate, dy, dwin_gate, dwout, dgain = gate_back(
            seed, rho, xhat, norm, wouts[layer], gate, y, gain, after[0], interpret=interpret
        )
        early, arrived = reduced_gate(dwin_gate, dwout, core, arrived)
        after_early = arrived
        dscaled, dwin_rest = backward_mix(
            layer, dgate, dy, xhat, norm, weights, rest, segc, segr, taps, heads_all[layer],
            dgain, maps, after[1], interpret=interpret,
        )
        late, arrived = reduced_rest(dwin_rest, arrived)
        sent[layer] = (early, late)
        after = [after_early, arrived]
        dscaled, after_early = lax.optimization_barrier((dscaled, after_early))
        scaled = over_positions(dscaled, core)
        upstream = upstream + sigma * (
            scaled
            - before * (sigma * sigma) * jnp.mean(scaled * before, axis=1, keepdims=True)
        )
        upstream = jnp.where(jnp.isnan(after_early), after_early, upstream)
    return current.astype(BF16), upstream.astype(BF16), sent


def per_device(
    hidden_in,
    segments,
    projection_in,
    projection_out,
    kernel_weight,
    kernel_bias,
    norm_gain,
    gate_gain,
    head_values,
    cotangent,
):
    core = lax.axis_index("seq")
    block = packed_weights(
        projection_in, projection_out, kernel_weight, kernel_bias, norm_gain, gate_gain, core
    )
    weights = lax.all_gather(block, DP, axis=0, tiled=True)
    hidden_out, input_gradient, totals = layers_of(
        hidden_in[0], cotangent[0], segments, head_values, weights, core
    )
    totals = [jnp.stack(layers) for layers in zip(*totals)]
    return (hidden_out[None], input_gradient[None]) + unpacked_gradients(*totals, core)


def solution(mesh):
    torus = Mesh(mesh.devices.reshape(4, 4, 4, mesh.shape["seq"]), DP_SEQ)
    tokens = P(DP, "seq", None)
    weights = (
        P(None, DP_SEQ, None),
        P(None, DP_SEQ, None),
        P(None, None, DP_SEQ),
        P(None, DP_SEQ),
        P(None, DP_SEQ),
        P(None, DP_SEQ),
    )
    return jax.shard_map(
        per_device,
        mesh=torus,
        in_specs=(tokens, P(DP, None)) + weights + (P(), tokens),
        out_specs=(tokens, tokens) + weights + (P(),),
        check_vma=False,
    )
```

```python
import functools

import jax
import jax.numpy as jnp
from jax import lax
from jax.experimental import pallas as pl
from jax.experimental.pallas import tpu as pltpu
from jax.sharding import Mesh
from jax.sharding import PartitionSpec as P

HEADS = 24
HEAD_DIM = 64
STATE = 128
INNER = 1536
CONV_CH = 1792
WIDTH = 768
TOKENS = 512
CHIPS = 64
HALF = 256
OWN_HEADS = 12
OWN = OWN_HEADS * HEAD_DIM
OWN_CONV = OWN + 2 * STATE
REST = OWN_CONV + 128
GATE_FOLD = OWN // 2
REST_FOLD = 640
GATE_COLS = OWN + GATE_FOLD
REST_COLS = REST + REST_FOLD
WIN_COLS = GATE_COLS + REST_COLS
OUT_COLS = 3 * (WIDTH // 2)
LAYER_COLS = WIN_COLS + OUT_COLS
VECTORS = OWN_HEADS
REMAINDERS = 64
VECTOR_COLS = 40
NORM_EPS = 1e-05
NEGATIVE = -1e30
F32 = jnp.float32
BF16 = jnp.bfloat16
HIGHEST = lax.Precision.HIGHEST


def dot(a, b, dims=((1,), (0,)), precision=None):
    return lax.dot_general(a, b, (dims, ((), ())), precision=precision, preferred_element_type=F32)


def dot_nt(a, b, precision=None):
    return dot(a, b, ((1,), (1,)), precision)


def dot_tn(a, b, precision=None):
    return dot(a, b, ((0,), (0,)), precision)


def iota(shape, dim):
    return lax.broadcasted_iota(jnp.int32, shape, dim)


def padded_orders():
    column = iota((1, 512), 1)
    row = iota((WIDTH, 512), 0)
    start = 12 * (column >> 3)
    place = column & 7
    features = (start + place, start + 8 + (place & 3))
    return [jnp.where(feature == row, 1.0, 0.0).astype(BF16) for feature in features]


def half_places():
    low = (iota((1, 512), 1) & 7) < 4
    return jnp.where(low, 1.0, 0.0).astype(BF16), jnp.where(low, 0.0, 1.0).astype(BF16)


def head_spread():
    return jnp.where(iota((128, OWN), 0) == (iota((128, OWN), 1) >> 6), 1.0, 0.0).astype(F32)


def softplus(v):
    return jnp.maximum(v, 0.0) + jnp.log1p(jnp.exp(-jnp.abs(v)))


def tap_masks(segment_column):
    position = iota((TOKENS, 1), 0)
    wide = jnp.broadcast_to(segment_column, (TOKENS, 128))
    masks = [None]
    for back in range(1, 4):
        before = pltpu.roll(wide, back, 0)[:, :1]
        same = (before == segment_column) & (position >= back)
        masks.append(jnp.where(same, 1.0, 0.0).astype(F32))
    return masks


def convolved(signal, taps, masks):
    total = taps[3:4] * signal
    for back in range(1, 4):
        total = total + taps[3 - back : 4 - back] * (pltpu.roll(signal, back, 0) * masks[back])
    return total + taps[4:5]


def steps_of(raw, heads):
    shifted = raw + heads[0:1]
    step = softplus(shifted)
    log_decay = -step * jnp.exp(heads[1:2])
    lower = jnp.where(iota((TOKENS, TOKENS), 0) >= iota((TOKENS, TOKENS), 1), 1.0, 0.0).astype(F32)
    return shifted, step, dot(lower, log_decay, precision=HIGHEST)


def lane_masks():
    low = iota((1, 128), 1) < HEAD_DIM
    return (jnp.where(low, 1.0, 0.0).astype(BF16), jnp.where(low, 0.0, 1.0).astype(BF16))


def reordered(scaled, orders=None):
    once, twice = [dot(scaled, order).astype(BF16) for order in orders or padded_orders()]
    low, high = half_places()
    return once, twice * low, twice * high


def projected(parts, full, folded, fold):
    u_full, u_low, u_high = parts
    rest = full.shape[1] - fold
    left = dot(u_full, full[:, :fold]) + dot(u_low, folded)
    right = dot(u_full, full[:, fold:]) + dot(u_high, folded[:, :rest])
    return left, right


def weight_gradient(parts, grad, fold):
    u_full, u_low, u_high = parts
    rest = grad.shape[1] - fold
    folded = dot_tn(u_low, grad[:, :fold])
    high = dot_tn(u_high, grad[:, fold:])
    if rest < fold:
        high = jnp.concatenate([high, jnp.zeros((high.shape[0], fold - rest), F32)], axis=1)
    return dot_tn(u_full, grad), folded + high


def input_gradients(grad, full, folded, fold):
    rest = grad.shape[1] - fold
    return (
        dot_nt(grad, full),
        dot_nt(grad[:, :fold], folded),
        dot_nt(grad[:, fold:], folded[:, :rest]),
    )


def column_picks(maps, kind, columns):
    chips = maps[2 * kind : 2 * kind + 1, :columns]
    places = maps[2 * kind + 1 : 2 * kind + 2, :columns]
    rows = iota((512, 1), 0) >> 3
    keep = jnp.where(rows == chips, 1.0, 0.0).astype(F32)
    pick = jnp.where(iota((128, columns), 0) == places + VECTORS, 1.0, 0.0).astype(F32)
    return keep, pick


def vectors_from(tile, maps, kind, columns):
    keep, pick = column_picks(maps, kind, columns)
    spread = dot(tile, pick.astype(BF16)) * keep
    return jnp.sum(spread.reshape(CHIPS, 8, columns), axis=0)


def vectors_into(values, maps, kind):
    columns = values.shape[1]
    keep, pick = column_picks(maps, kind, columns)
    tiled = jnp.broadcast_to(values[None], (CHIPS, 8, columns)).reshape(512, columns)
    return dot_nt(tiled * keep, pick, precision=HIGHEST)


def only_row(values, row):
    return jnp.where(iota((8, 1), 0) == row, values, 0.0)


def column_halves(core_ref):
    half = WIDTH // 2
    core = core_ref[0]
    return (
        pl.ds(pl.multiple_of(core * half, 128), half),
        pl.ds(pl.multiple_of((1 - core) * half, 128), half),
    )


def fetched(source, target, semaphore, layer, columns):
    start = layer * LAYER_COLS
    return pltpu.make_async_copy(source.at[:, start : start + columns], target, semaphore)


def spread_steps(step, spread):
    spread = spread.astype(BF16)
    high = step.astype(BF16)
    low = (step - high.astype(F32)).astype(BF16)
    return dot(high, spread) + dot(low, spread)


def forward_kernel(
    layer, core_ref, xhat_ref, weights_ref, wout_ref, wother_ref, segc_ref, segr_ref, heads_ref, maps_ref,
    gate_ref, rest_ref, y_ref, out_ref, square_ref, taps_ref, norm_ref, gain_ref,
    win_ref, dtx_ref, affinity_ref, bias_ref, semaphore,
):
    copy = fetched(weights_ref, win_ref, semaphore, layer, WIN_COLS)
    copy.start()
    segc = segc_ref[...]
    masks = tap_masks(segc)
    allowed = (iota((TOKENS, TOKENS), 0) >= iota((TOKENS, TOKENS), 1)) & (segc == segr_ref[...])
    bias_ref[...] = jnp.where(allowed, 0.0, NEGATIVE).astype(F32)
    copy.wait()
    maps = maps_ref[...]
    tile = win_ref[:, GATE_COLS + OWN_CONV : GATE_COLS + REST]
    taps = vectors_from(tile, maps, 0, OWN_CONV)
    norm = vectors_from(tile, maps, 1, WIDTH)[5:6]
    gain = vectors_from(tile, maps, 2, OWN)[6:7]
    taps_ref[...] = taps
    norm_ref[...] = jnp.broadcast_to(norm, norm_ref.shape)
    gain_ref[...] = jnp.broadcast_to(gain, gain_ref.shape)
    parts = reordered((xhat_ref[...].astype(F32) * norm).astype(BF16))
    rest_ref[:, :REST_FOLD], rest_ref[:, REST_FOLD:] = projected(
        parts, win_ref[:, GATE_COLS : GATE_COLS + REST], win_ref[:, GATE_COLS + REST :], REST_FOLD
    )
    gate_ref[:, :GATE_FOLD], gate_ref[:, GATE_FOLD:] = projected(
        parts, win_ref[:, :OWN], win_ref[:, OWN:GATE_COLS], GATE_FOLD
    )
    heads = heads_ref[...]
    before = convolved(rest_ref[:, :OWN_CONV], taps, masks)
    active = before * jax.nn.sigmoid(before)
    inputs = active[:, :OWN]
    writers = active[:, OWN : OWN + STATE].astype(BF16)
    readers = active[:, OWN + STATE :].astype(BF16)
    _, step, cumul = steps_of(rest_ref[:, OWN_CONV:], heads)
    cumul_rows = cumul.T
    spread = head_spread()
    dtx_ref[...] = (spread_steps(step, spread) * inputs).astype(BF16)
    y_ref[...] = dot(heads, spread, precision=HIGHEST)[2:3] * inputs
    affinity_ref[...] = dot_nt(readers, writers)
    halves = lane_masks()
    for pair in range(OWN_HEADS // 2):
        lanes = slice(128 * pair, 128 * pair + 128)
        pair_inputs = dtx_ref[:, lanes]
        for block in range(2):
            rows = slice(HALF * block, HALF * block + HALF)
            reach = HALF * (block + 1)
            total = y_ref[rows, lanes]
            for member in range(2):
                head = 2 * pair + member
                decay = jnp.exp(
                    cumul[rows, head : head + 1]
                    - cumul_rows[head : head + 1, :reach]
                    + bias_ref[rows, :reach]
                )
                mixing = (decay * affinity_ref[rows, :reach]).astype(BF16)
                total = total + dot(mixing, pair_inputs[:reach] * halves[member])
            y_ref[rows, lanes] = total
    gate = gate_ref[...]
    gated = y_ref[...] * (gate * jax.nn.sigmoid(gate))
    outgoing = (gated * gain).astype(BF16)
    own, other = column_halves(core_ref)
    out_ref[:, own] = dot(outgoing, wout_ref[...]).astype(BF16)
    out_ref[:, other] = dot(outgoing, wother_ref[...]).astype(BF16)
    square_ref[...] = jnp.broadcast_to(
        jnp.sum(gated * gated, axis=1, keepdims=True), square_ref.shape
    )


def cost(microseconds):
    flops, bytes_accessed = int(1.1e9 * microseconds), int(3.6e6 * microseconds)
    return pl.CostEstimate(flops=flops, bytes_accessed=bytes_accessed, transcendentals=0)


SCALAR = pl.BlockSpec(memory_space=pltpu.SMEM)


def vmem(count):
    return [pl.BlockSpec(memory_space=pltpu.VMEM)] * count


def forward_mix(layer, core, xhat, weights, wout, segc, segr, heads, maps, interpret=False):
    return pl.pallas_call(
        functools.partial(forward_kernel, layer),
        in_specs=[SCALAR] + vmem(1) + [pl.BlockSpec(memory_space=pl.ANY)] + vmem(6),
        out_shape=(
            jax.ShapeDtypeStruct((TOKENS, OWN), F32),
            jax.ShapeDtypeStruct((TOKENS, REST), F32),
            jax.ShapeDtypeStruct((TOKENS, OWN), F32),
            jax.ShapeDtypeStruct((TOKENS, WIDTH), BF16),
            jax.ShapeDtypeStruct((TOKENS, 128), F32),
            jax.ShapeDtypeStruct((8, OWN_CONV), F32),
            jax.ShapeDtypeStruct((8, WIDTH), F32),
            jax.ShapeDtypeStruct((8, OWN), F32),
        ),
        scratch_shapes=[
            pltpu.VMEM((512, WIN_COLS), BF16),
            pltpu.VMEM((TOKENS, OWN), BF16),
            pltpu.VMEM((TOKENS, TOKENS), F32),
            pltpu.VMEM((TOKENS, TOKENS), F32),
            pltpu.SemaphoreType.DMA,
        ],
        compiler_params=pltpu.CompilerParams(vmem_limit_bytes=58 * 2**20),
        cost_estimate=cost(15),
        interpret=interpret,
    )(core, xhat, weights, *wout, segc, segr, heads, maps)


def gate_kernel(
    core_ref, seed_ref, rho_ref, xhat_ref, norm_ref, wout_ref, wother_ref, gate_ref, y_ref,
    gain_ref, after_ref, dgate_ref, dy_ref, dwin_ref, dwout_ref, dwother_ref, dgain_ref,
):
    own, other = column_halves(core_ref)
    seed_own = seed_ref[:, own]
    seed_other = seed_ref[:, other]
    mean = seed_ref[:, WIDTH : WIDTH + 128].astype(F32)
    mean = mean[:, 0:1] + mean[:, 1:2]
    gain = gain_ref[0:1]
    rho = rho_ref[...]
    gate = gate_ref[...]
    y = y_ref[...]
    open_gate = jax.nn.sigmoid(gate)
    passed = gate * open_gate
    scaled = y * passed * rho
    dyn = dot_nt(seed_own, wout_ref[...]) + dot_nt(seed_other, wother_ref[...])
    outgoing = (scaled * gain).astype(BF16)
    dwout_ref[...] = dot_tn(outgoing, seed_own).astype(BF16)
    dwother_ref[...] = dot_tn(outgoing, seed_other).astype(BF16)
    dgain_ref[...] = jnp.broadcast_to(jnp.sum(dyn * scaled, axis=0, keepdims=True), dgain_ref.shape)
    dgated = rho * (dyn * gain - scaled * mean)
    dy_ref[...] = dgated * passed
    dgate = (dgated * y * (open_gate * (1.0 + gate * (1.0 - open_gate)))).astype(BF16)
    dgate_ref[...] = dgate
    parts = reordered((xhat_ref[...].astype(F32) * norm_ref[0:1]).astype(BF16))
    full, folded = weight_gradient(parts, dgate, GATE_FOLD)
    dwin_ref[:, :OWN] = full.astype(BF16)
    dwin_ref[:, OWN:] = folded.astype(BF16)


def gate_back(core, seed, rho, xhat, norm, wout, gate, y, gain, after, interpret=False):
    return pl.pallas_call(
        gate_kernel,
        in_specs=[SCALAR] + vmem(10),
        out_shape=(
            jax.ShapeDtypeStruct((TOKENS, OWN), BF16),
            jax.ShapeDtypeStruct((TOKENS, OWN), F32),
            jax.ShapeDtypeStruct((512, GATE_COLS), BF16),
            jax.ShapeDtypeStruct((OWN, WIDTH // 2), BF16),
            jax.ShapeDtypeStruct((OWN, WIDTH // 2), BF16),
            jax.ShapeDtypeStruct((8, OWN), F32),
        ),
        compiler_params=pltpu.CompilerParams(vmem_limit_bytes=58 * 2**20),
        cost_estimate=cost(8),
        interpret=interpret,
    )(core, seed, rho, xhat, norm, *wout, gate, y, gain, after)


def backward_kernel(
    layer, dgate_ref, dy_ref, xhat_ref, norm_ref, weights_ref, rest_ref,
    segc_ref, segr_ref, taps_ref, heads_ref, dgain_ref, maps_ref, after_ref,
    dscaled_ref, dwin_ref,
    win_ref, dtx_ref, affinity_ref, bias_ref, daffinity_ref, drest_ref, dact_ref, rise_ref,
    direct_ref, dtaps_ref, semaphore,
):
    copy = fetched(weights_ref, win_ref, semaphore, layer, WIN_COLS)
    copy.start()
    taps = taps_ref[...]
    heads = heads_ref[...]
    segc = segc_ref[...]
    masks = tap_masks(segc)
    signal = rest_ref[:, :OWN_CONV]
    before = convolved(signal, taps, masks)
    open_act = jax.nn.sigmoid(before)
    active = before * open_act
    inputs = active[:, :OWN]
    writers = active[:, OWN : OWN + STATE].astype(BF16)
    readers = active[:, OWN + STATE :].astype(BF16)
    shifted, step, cumul = steps_of(rest_ref[:, OWN_CONV:], heads)
    cumul_rows = cumul.T
    spread = head_spread()
    step_wide = spread_steps(step, spread)
    skip_wide = dot(heads, spread, precision=HIGHEST)[2:3]
    dtx_ref[...] = (step_wide * inputs).astype(BF16)
    allowed = (iota((TOKENS, TOKENS), 0) <= iota((TOKENS, TOKENS), 1)) & (segc == segr_ref[...])
    bias_ref[...] = jnp.where(allowed, 0.0, NEGATIVE).astype(F32)
    affinity_ref[...] = dot_nt(writers, readers)
    daffinity_ref[...] = jnp.zeros_like(daffinity_ref)
    rise_ref[...] = jnp.zeros_like(rise_ref)
    halves = lane_masks()
    head_lane = iota((1, 128), 1)
    fall_blocks = [jnp.zeros((HALF, 128), F32), jnp.zeros((HALF, 128), F32)]
    for pair in range(OWN_HEADS // 2):
        lanes = slice(128 * pair, 128 * pair + 128)
        pair_inputs = dtx_ref[:, lanes]
        pair_dy = dy_ref[:, lanes].astype(BF16)
        member_dy = [pair_dy * half for half in halves]
        for block in range(2):
            rows = slice(HALF * block, HALF * block + HALF)
            start = HALF * block
            dinput = jnp.zeros((HALF, 128), F32)
            for member in range(2):
                head = 2 * pair + member
                decay = jnp.exp(
                    cumul_rows[head : head + 1, start:]
                    - cumul[rows, head : head + 1]
                    + bias_ref[rows, start:]
                )
                dmixing = dot_nt(pair_inputs[rows], member_dy[member][start:]) * decay
                daffinity_ref[rows, start:] += dmixing
                affinity = affinity_ref[rows, start:]
                dinput = dinput + dot((decay * affinity).astype(BF16), member_dy[member][start:])
                dspread = dmixing * affinity
                fall = jnp.sum(dspread, axis=1, keepdims=True)
                fall_blocks[block] = fall_blocks[block] + jnp.where(head_lane == head, fall, 0.0)
                rise_ref[head : head + 1, start:] += jnp.sum(dspread, axis=0, keepdims=True)
            direct_ref[rows, lanes] = dinput
    dinputs = direct_ref[...]
    dy = dy_ref[...]
    dact_ref[:, :OWN] = step_wide * dinputs + skip_wide * dy
    daffinity = daffinity_ref[...].astype(BF16)
    dact_ref[:, OWN : OWN + STATE] = dot(daffinity, readers)
    dact_ref[:, OWN + STATE :] = dot_tn(daffinity, writers)
    dstep = dot_nt(dinputs * inputs, spread, precision=HIGHEST)
    skip_sum = jnp.broadcast_to(jnp.sum(dy * inputs, axis=0, keepdims=True), (8, OWN))
    dskip = dot_nt(skip_sum, spread, precision=HIGHEST)[0:1]
    dcumul = rise_ref[...].T - jnp.concatenate(fall_blocks, axis=0)
    upper = jnp.where(iota((TOKENS, TOKENS), 0) <= iota((TOKENS, TOKENS), 1), 1.0, 0.0).astype(F32)
    dlog = dot(upper, dcumul, precision=HIGHEST)
    rate = jnp.exp(heads[1:2])
    draw = (dstep - dlog * rate) * jax.nn.sigmoid(shifted)
    head_rows = (
        jnp.sum(draw, axis=0, keepdims=True),
        jnp.sum(-dlog * step * rate, axis=0, keepdims=True),
        dskip,
    )
    drest_ref[:, OWN_CONV:] = draw.astype(BF16)

    dconv = dact_ref[...] * (open_act * (1.0 + before * (1.0 - open_act)))
    dtaps_ref[...] = jnp.zeros_like(dtaps_ref)
    dtaps_ref[4:5] = jnp.sum(dconv, axis=0, keepdims=True)
    dtaps_ref[3:4] = jnp.sum(dconv * signal, axis=0, keepdims=True)
    dsignal = taps[3:4] * dconv
    for back in range(1, 4):
        masked = dconv * masks[back]
        dtaps_ref[3 - back : 4 - back] = jnp.sum(
            masked * pltpu.roll(signal, back, 0), axis=0, keepdims=True
        )
        dsignal = dsignal + taps[3 - back : 4 - back] * pltpu.roll(masked, TOKENS - back, 0)
    drest_ref[:, :OWN_CONV] = dsignal.astype(BF16)

    norm = norm_ref[0:1]
    xhat = xhat_ref[...].astype(F32)
    orders = padded_orders()
    u = (xhat * norm).astype(BF16)
    parts = reordered(u, orders)
    drest = drest_ref[...]
    copy.wait()
    from_rest = input_gradients(
        drest, win_ref[:, GATE_COLS : GATE_COLS + REST], win_ref[:, GATE_COLS + REST :], REST_FOLD
    )
    from_gate = input_gradients(
        dgate_ref[...], win_ref[:, :OWN], win_ref[:, OWN:GATE_COLS], GATE_FOLD
    )
    once, low, high = [(one + other).astype(BF16) for one, other in zip(from_rest, from_gate)]
    low_places, high_places = half_places()
    du = dot_nt(once, orders[0]) + dot_nt(low * low_places + high * high_places, orders[1])
    dscaled_ref[...] = (du * norm).astype(BF16)

    full, folded = weight_gradient(parts, drest, REST_FOLD)
    dwin_ref[:, :OWN_CONV] = full[:, :OWN_CONV].astype(BF16)
    dwin_ref[:, REST:] = folded.astype(BF16)
    maps = maps_ref[...]
    dnorm = jnp.sum(du * xhat, axis=0, keepdims=True)
    vectors = (
        vectors_into(dtaps_ref[...], maps, 0)
        + vectors_into(only_row(dnorm, 5), maps, 1)
        + vectors_into(only_row(dgain_ref[...], 6), maps, 2)
    )
    last_row = jnp.zeros((8, 128), F32)
    for place, row in enumerate(head_rows):
        shift = VECTORS + OWN_HEADS * place
        last_row = last_row + pltpu.roll(jnp.broadcast_to(row, (8, 128)), shift, 1)
    vectors = vectors + jnp.where((iota((512, 1), 0) & 7) == 7, last_row[0:1], 0.0)
    high = vectors.astype(BF16).astype(F32)
    low = pltpu.roll(vectors - high, REMAINDERS - VECTORS, 1)
    dwin_ref[:, OWN_CONV:REST] = (full[:, OWN_CONV:] + high + low).astype(BF16)


def backward_mix(
    layer, dgate, dy, xhat, norm, weights, rest, segc, segr, taps, heads, dgain, maps,
    after, interpret=False,
):
    square = (TOKENS, TOKENS)
    return pl.pallas_call(
        functools.partial(backward_kernel, layer),
        in_specs=vmem(4) + [pl.BlockSpec(memory_space=pl.ANY)] + vmem(8),
        out_shape=(
            jax.ShapeDtypeStruct((TOKENS, WIDTH), BF16),
            jax.ShapeDtypeStruct((512, REST_COLS), BF16),
        ),
        scratch_shapes=[
            pltpu.VMEM((512, WIN_COLS), BF16),
            pltpu.VMEM((TOKENS, OWN), BF16),
            pltpu.VMEM(square, F32),
            pltpu.VMEM(square, F32),
            pltpu.VMEM(square, F32),
            pltpu.VMEM((TOKENS, REST), BF16),
            pltpu.VMEM((TOKENS, OWN_CONV), F32),
            pltpu.VMEM((128, TOKENS), F32),
            pltpu.VMEM((TOKENS, OWN), F32),
            pltpu.VMEM((8, OWN_CONV), F32),
            pltpu.SemaphoreType.DMA,
        ],
        compiler_params=pltpu.CompilerParams(vmem_limit_bytes=58 * 2**20),
        cost_estimate=cost(30),
        interpret=interpret,
    )(dgate, dy, xhat, norm, weights, rest, segc, segr, taps, heads, dgain, maps, after)


DP = ("dp_0", "dp_1", "dp_2")
DP_SEQ = DP + ("seq",)
LAYERS = 2


def swapped(v):
    return lax.ppermute(v, "seq", [(0, 1), (1, 0)])


def part(v, index, size, axis):
    return lax.dynamic_slice_in_dim(v, index * size, size, axis)


def in_order(core, own, other, axis):
    first = jnp.where(core == 0, own, other)
    second = jnp.where(core == 0, other, own)
    return jnp.concatenate([first, second], axis=axis)


def padded(v, sizes):
    return jnp.pad(v, [(0, size - now) for now, size in zip(v.shape, sizes)])


def folded_rows(rows, fold):
    tail = padded(rows[:, 8:], (LAYERS, 4, 2 * fold)).reshape(LAYERS, 4, 2, fold)
    return tail.transpose(0, 2, 1, 3).reshape(LAYERS, 8, fold)


def packed_weights(win, wout, kernel_weight, kernel_bias, norm_gain, gate_gain, core):
    win = in_order(core, win, swapped(win), 1)
    wout = in_order(core, wout, swapped(wout), 1)
    rows = [kernel_weight, kernel_bias[:, None]]
    rows += [padded(vector[:, None], (LAYERS, 1, 14)) for vector in (norm_gain, gate_gain)]
    vectors = padded(jnp.concatenate(rows, axis=1), (LAYERS, 8, 14))
    others = swapped(vectors)
    first = jnp.where(core == 0, vectors, others)
    second = jnp.where(core == 0, others, vectors)
    joined = []
    for start, stop, size in ((0, 5, 14), (5, 6, 6), (6, 8, 12)):
        both = [first[:, start:stop, :size], second[:, start:stop, :size]]
        both = jnp.concatenate(both, axis=2)
        joined.append(padded(both, both.shape[:2] + (128 - OWN_HEADS,)))
    vectors = jnp.concatenate(joined, axis=1)
    gate = part(win[:, :, :INNER], core, OWN, 2)
    steps = part(win[:, :, INNER + CONV_CH :], core, OWN_HEADS, 2)
    tail = padded(steps[:, 8:], (LAYERS, 4, 128))
    tile = jnp.concatenate([steps[:, :8], vectors], axis=2)
    rest = jnp.concatenate(
        [
            part(win[:, :, INNER : 2 * INNER], core, OWN, 2),
            win[:, :, 2 * INNER : INNER + CONV_CH],
            jnp.concatenate([tile, tail], axis=1),
        ],
        axis=2,
    )
    wout = part(wout, core, WIDTH // 2, 2)
    wout = wout.reshape(LAYERS, 3, 8, WIDTH // 2).transpose(0, 2, 1, 3)
    block = jnp.concatenate(
        [
            gate[:, :8],
            folded_rows(gate, GATE_FOLD),
            rest[:, :8],
            folded_rows(rest, REST_FOLD),
            wout.reshape(LAYERS, 8, OUT_COLS),
        ],
        axis=2,
    )
    return block.transpose(1, 0, 2).reshape(8, LAYERS * LAYER_COLS)


def output_weights(gathered, core):
    wout = gathered.reshape(CHIPS, 8, LAYERS, LAYER_COLS)[:, :, :, WIN_COLS:]
    wout = wout.reshape(CHIPS, 8, LAYERS, 3, WIDTH // 2).transpose(2, 0, 3, 1, 4)
    wout = wout.reshape(LAYERS, INNER, WIDTH // 2)
    own, other = part(wout, core, OWN, 1), swapped(part(wout, 1 - core, OWN, 1))
    return [(own[layer], other[layer]) for layer in range(LAYERS)]


def vector_maps(core):
    column = jnp.arange(OWN_CONV)
    channel = jnp.where(column < OWN, column + core * OWN, column - OWN + INNER)
    feature = column + core * OWN
    rows = [channel // 28, channel % 28, column // 12, column % 12, feature // 24, feature % 24]
    return padded(jnp.stack(rows).astype(jnp.int32), (8, OWN_CONV))


def over_positions(partial_sum, core):
    own = part(partial_sum, core, HALF, 0).astype(F32)
    return own + swapped(part(partial_sum, 1 - core, HALF, 0)).astype(F32)


def reduced(packed, earlier):
    if earlier is not None:
        packed, earlier = lax.optimization_barrier((packed, earlier))
    arrived = lax.all_to_all(packed, DP, 0, 0, tiled=True)
    total = jnp.sum(arrived.astype(F32), axis=0)
    if earlier is not None:
        total = jnp.where(jnp.isnan(earlier), earlier, total)
    return total, arrived[0, :1, :1].astype(F32)


def reduced_gate(dwin, dwout, dwother, core, earlier):
    half = WIDTH // 2
    dwout = in_order(core, dwout, swapped(dwother), 0).reshape(CHIPS, 3, 8, half).transpose(0, 2, 1, 3)
    dwin = dwin.reshape(CHIPS, 8, GATE_COLS)
    packed = jnp.concatenate([dwin, dwout.reshape(CHIPS, 8, OUT_COLS)], axis=2)
    return reduced(packed, earlier)


def reduced_rest(dwin, earlier):
    return reduced(dwin.reshape(CHIPS, 8, REST_COLS), earlier)


def unfolded(total, columns, fold):
    tail = total[:, :, columns:].reshape(LAYERS, 2, 4, fold).transpose(0, 2, 1, 3)
    tail = tail.reshape(LAYERS, 4, 2 * fold)[:, :, :columns]
    return jnp.concatenate([total[:, :, :columns], tail], axis=1)


def unpacked_gradients(early_total, rest_total, core):
    win = jnp.concatenate(
        [
            unfolded(early_total[:, :, :GATE_COLS], OWN, GATE_FOLD),
            unfolded(rest_total, REST, REST_FOLD),
        ],
        axis=2,
    )
    own = part(win, core, 6, 1)
    got = swapped(part(win, 1 - core, 6, 1))
    left = jnp.where(core == 0, own, got)
    right = jnp.where(core == 0, got, own)
    shared = slice(2 * OWN, 2 * OWN + 2 * STATE)
    steps = slice(2 * OWN + 2 * STATE, 2 * OWN + 2 * STATE + OWN_HEADS)
    dwin = jnp.concatenate(
        [
            left[:, :, :OWN],
            right[:, :, :OWN],
            left[:, :, OWN : 2 * OWN],
            right[:, :, OWN : 2 * OWN],
            left[:, :, shared] + right[:, :, shared],
            left[:, :, steps],
            right[:, :, steps],
        ],
        axis=2,
    )
    half = WIDTH // 2
    wout = early_total[:, :, GATE_COLS:].reshape(LAYERS, 8, 3, half).transpose(0, 2, 1, 3)
    wout = wout.reshape(LAYERS, 24, half)
    dwout = in_order(core, part(wout, core, 12, 1), swapped(part(wout, 1 - core, 12, 1)), 2)
    tile = rest_total[:, :, OWN_CONV:REST]
    vectors = tile[:, :, VECTORS : VECTORS + VECTOR_COLS]
    vectors = vectors + tile[:, :, REMAINDERS : REMAINDERS + VECTOR_COLS]
    others = swapped(vectors)
    heads = in_order(
        core,
        vectors[:, 7, :36].reshape(LAYERS, 3, 12),
        others[:, 7, :36].reshape(LAYERS, 3, 12),
        2,
    )
    vectors = vectors + others
    taps = part(vectors[:, :5, :28], core, 14, 2)
    return (
        dwin,
        dwout,
        taps[:, :4],
        taps[:, 4],
        part(vectors[:, 5, :12], core, 6, 1),
        part(vectors[:, 6, :24], core, 12, 1),
        heads,
    )


def mean_square_scale(values):
    return lax.rsqrt(jnp.mean(values * values, axis=1, keepdims=True) + NORM_EPS)


def layers_of(
    hidden, cotangent, segments, head_values, weights, core, interpret=False
):
    segr = segments
    segc = segments.reshape(TOKENS, 1)
    heads_all = padded(part(head_values, core, OWN_HEADS, 2), (LAYERS, 8, 128))
    maps = vector_maps(core)
    place = core.astype(jnp.int32).reshape(1)
    current = hidden.astype(F32)
    saved = []
    for layer in range(LAYERS):
        sigma = mean_square_scale(current)
        xhat = lax.all_gather((current * sigma).astype(BF16), "seq", axis=0, tiled=True)
        if layer == 0:
            weights, xhat, segc, heads_all, maps = lax.optimization_barrier(
                (weights, xhat, segc, heads_all, maps)
            )
            wouts = output_weights(weights, core)
        gate, rest, y, out, square, taps, norm, gain = forward_mix(
            layer, place, xhat, weights, wouts[layer], segc, segr, heads_all[layer], maps,
            interpret=interpret,
        )
        square = square + swapped(square)
        rho = lax.rsqrt(square[:, :1] / INNER + NORM_EPS)
        branch = over_positions(out, core)
        own_rho = part(rho, core, HALF, 0)
        saved.append((current, sigma, xhat, gate, rest, y, rho, own_rho, branch, taps, norm, gain))
        current = current + own_rho * branch
    upstream = cotangent.astype(F32)
    sent = [None] * LAYERS
    arrived = None
    after = [jnp.zeros((1, 1), F32)] * 2
    for layer in reversed(range(LAYERS)):
        before, sigma, xhat, gate, rest, y, rho, own_rho, branch, taps, norm, gain = saved[layer]
        seed = upstream.astype(BF16)
        mean = own_rho * jnp.sum(seed.astype(F32) * branch, axis=1, keepdims=True) / INNER
        high = lax.reduce_precision(mean, 8, 7)
        means = jnp.concatenate([high, mean - high], axis=1).astype(BF16)
        seed = jnp.concatenate([seed, padded(means, (HALF, 128))], axis=1)
        seed = lax.all_gather(seed, "seq", axis=0, tiled=True)
        dgate, dy, dwin_gate, dwout, dwother, dgain = gate_back(
            place, seed, rho, xhat, norm, wouts[layer], gate, y, gain, after[0], interpret=interpret
        )
        early, arrived = reduced_gate(dwin_gate, dwout, dwother, core, arrived)
        after_early = arrived
        dscaled, dwin_rest = backward_mix(
            layer, dgate, dy, xhat, norm, weights, rest, segc, segr, taps, heads_all[layer],
            dgain, maps, after[1], interpret=interpret,
        )
        late, arrived = reduced_rest(dwin_rest, arrived)
        sent[layer] = (early, late)
        after = [after_early, arrived]
        dscaled, after_early = lax.optimization_barrier((dscaled, after_early))
        scaled = over_positions(dscaled, core)
        upstream = upstream + sigma * (
            scaled
            - before * (sigma * sigma) * jnp.mean(scaled * before, axis=1, keepdims=True)
        )
        upstream = jnp.where(jnp.isnan(after_early), after_early, upstream)
    return current.astype(BF16), upstream.astype(BF16), sent


def per_device(
    hidden_in,
    segments,
    projection_in,
    projection_out,
    kernel_weight,
    kernel_bias,
    norm_gain,
    gate_gain,
    head_values,
    cotangent,
):
    core = lax.axis_index("seq")
    block = packed_weights(
        projection_in, projection_out, kernel_weight, kernel_bias, norm_gain, gate_gain, core
    )
    weights = lax.all_gather(block, DP, axis=0, tiled=True)
    hidden_out, input_gradient, totals = layers_of(
        hidden_in[0], cotangent[0], segments, head_values, weights, core
    )
    totals = [jnp.stack(layers) for layers in zip(*totals)]
    return (hidden_out[None], input_gradient[None]) + unpacked_gradients(*totals, core)


def solution(mesh):
    torus = Mesh(mesh.devices.reshape(4, 4, 4, mesh.shape["seq"]), DP_SEQ)
    tokens = P(DP, "seq", None)
    weights = (
        P(None, DP_SEQ, None),
        P(None, DP_SEQ, None),
        P(None, None, DP_SEQ),
        P(None, DP_SEQ),
        P(None, DP_SEQ),
        P(None, DP_SEQ),
    )
    return jax.shard_map(
        per_device,
        mesh=torus,
        in_specs=(tokens, P(DP, None)) + weights + (P(), tokens),
        out_specs=(tokens, tokens) + weights + (P(),),
        check_vma=False,
    )
```
